32 devices in a mesh: dp: 8 (over z, y), mp: 4 (over x, core).
Axes of the slice: x: 2, y: 2, z: 4, core: 2. Of those that a mesh axis runs over, the one named last changes fastest.
Arguments:
- images: bfloat16 [256, 196, 768], P(('dp', 'mp')), may hold values from -6 to 6
- kept_mask: int32 [256, 196], P(('dp', 'mp')), may hold values from 0 to 1, as said below
- pooled_grad: float32 [256, 768], P(('dp', 'mp')), may hold values from -600 to 600
- token_weights: float32 [2, 196, 384], P(None, None, 'dp'), may hold values from -0.4375 to 0.4375
- norm_gain: float32 [2, 768], replicated, may hold values from 0.5 to 1.5
- norm_bias: float32 [2, 768], replicated, may hold values from -1.8 to 1.8
- mixing_bias: float32 [384], replicated, may hold values from -1.8 to 1.8
- patch_bias: float32 [196], replicated, may hold values from -1.8 to 1.8
- widening: float32 [768, 3072], P('dp', 'mp'), may hold values from -0.21875 to 0.21875
- narrowing: float32 [3072, 768], P('mp', 'dp'), may hold values from -0.109375 to 0.109375
- hidden_bias: float32 [3072], replicated, may hold values from -1.8 to 1.8
- output_bias: float32 [768], replicated, may hold values from -1.8 to 1.8
- width_maps: bfloat16 [2, 768, 64], replicated, may hold values from -0.21875 to 0.21875
- hidden_maps: bfloat16 [2, 3072, 64], P(None, 'mp'), may hold values from -0.109375 to 0.109375
- queries: bfloat16 [256, 162176], P(None, 'dp'), may hold values from -0.015625 to 0.015625
Outputs:
- pooled: float32 [256, 768], P(('dp', 'mp'))
- image_grad: float32 [256, 196, 768], P(('dp', 'mp'))
- token_grad: float32 [2, 196, 384], P(None, None, 'dp')
- gain_grad: float32 [2, 768], replicated
- shift_grad: float32 [2, 768], replicated
- mixing_grad: float32 [384], replicated
- patch_grad: float32 [196], replicated
- widening_grad: float32 [768, 3072], P('dp', 'mp')
- narrowing_grad: float32 [3072, 768], P('mp', 'dp')
- hidden_grad: float32 [3072], replicated
- output_grad: float32 [768], replicated
- influence: float32 [256, 256], P(('dp', 'mp'))
The draws below stay inside these ranges and needn't reach their ends.
Inputs may be any that keep to these rules, and one draw needn't show every extreme that they name: `kept_mask`: every image keeps at least 49 of its patches.
All inputs are finite; a program needn't handle non-finite values.
Results may differ from the reference program's by a relative error of at most 0.012.
Values may be sent and summed in bfloat16 or wider, within the bound.
No kernel may reach another device: no remote copies, remote signals or barrier semaphores. Data moves between devices by JAX's collectives and lax.ppermute only.
A program may use at most 320 MiB of HBM per device.

```python
import jax
import jax.numpy as jnp
from jax import lax

P_SIZE = 196
C = 768
TH = 384
F = 3072
R = 64
Q = 256
B = 256
K = 162176


def draw_kept_mask(key, part):
    key = jax.random.fold_in(key, 7)
    count_key, order_key = jax.random.split(key)
    kept_counts = jax.random.randint(count_key, (B,), P_SIZE // 4, P_SIZE + 1)
    order_keys = jax.random.split(order_key, B)
    orders = jax.vmap(lambda single_key: jax.random.permutation(single_key, P_SIZE))(order_keys)
    return (orders < kept_counts[:, None]).astype(jnp.int32)


def block_scale(key, shape, cuts, smallest, largest):
    gain = 1.0
    for axis_at, blocks in cuts:
        draws = jax.random.uniform(jax.random.fold_in(jax.random.fold_in(key, 6), axis_at), (blocks,), jnp.float32, smallest / len(cuts), largest / len(cuts))
        gain = gain * jnp.repeat(jnp.exp(draws), shape[axis_at] // blocks).reshape((-1,) + (1,) * (len(shape) - 1 - axis_at))
    return gain


def scatter_about(own_key, extent, scale, reach, cuts=(), held_as=jnp.bfloat16):
    factor_of = block_scale(own_key, extent, cuts, -0.22, 0.18) if cuts else 1.0
    drawn = jax.random.normal(own_key, extent, jnp.float32) * scale * factor_of
    return jnp.minimum(jnp.maximum(drawn, -reach), reach).astype(held_as)


def setup_inputs(seed: int = 0) -> dict:
    streams_of = jax.random.split(jax.random.key(seed), 16)
    images = scatter_about(streams_of[0], (B, P_SIZE, C), 1.0, 6.0, ((0, 32),))
    kept_mask = draw_kept_mask(jax.random.fold_in(streams_of[15], 71), 0)
    pooled_grad = scatter_about(streams_of[2], (B, C), 100.0, 600.0, ((0, 32),), jnp.float32)
    token_weights = scatter_about(streams_of[3], (2, P_SIZE, TH), P_SIZE ** -0.5, 0.4375, ((2, 8),), jnp.float32)
    norm_gain = jnp.clip(1.0 + 0.1 * jax.random.normal(streams_of[4], (2, C), jnp.float32), 0.5, 1.5)
    norm_bias = scatter_about(streams_of[5], (2, C), 0.3, 1.8, (), jnp.float32)
    mixing_bias = scatter_about(streams_of[6], (TH,), 0.3, 1.8, (), jnp.float32)
    patch_bias = scatter_about(streams_of[7], (P_SIZE,), 0.3, 1.8, (), jnp.float32)
    widening = scatter_about(streams_of[8], (C, F), C ** -0.5, 0.21875, ((0, 8), (1, 4)), jnp.float32)
    narrowing = scatter_about(streams_of[9], (F, C), F ** -0.5, 0.109375, ((0, 4), (1, 8)), jnp.float32)
    hidden_bias = scatter_about(streams_of[10], (F,), 0.3, 1.8, (), jnp.float32)
    output_bias = scatter_about(streams_of[11], (C,), 0.3, 1.8, (), jnp.float32)
    width_maps = scatter_about(streams_of[12], (2, C, R), C ** -0.5, 0.21875)
    hidden_maps = scatter_about(streams_of[13], (2, F, R), F ** -0.5, 0.109375, ((1, 4),))
    queries = scatter_about(streams_of[14], (Q, K), K ** -0.5, 0.015625, ((1, 8),))
    return dict(images=images, kept_mask=kept_mask, pooled_grad=pooled_grad, token_weights=token_weights, norm_gain=norm_gain, norm_bias=norm_bias, mixing_bias=mixing_bias, patch_bias=patch_bias, widening=widening, narrowing=narrowing, hidden_bias=hidden_bias, output_bias=output_bias, width_maps=width_maps, hidden_maps=hidden_maps, queries=queries)


@jax.custom_vjp
def low(v):
    return lax.optimization_barrier(v.astype(jnp.bfloat16)).astype(jnp.float32)

@jax.custom_vjp
def low_back(v):
    return v

def low_keep(v):
    return (low(v), None)

def low_pass(kept, grad):
    return (grad,)

def back_keep(v):
    return (v, None)

def back_low(kept, grad):
    return (low(grad),)
low.defvjp(low_keep, low_pass)
low_back.defvjp(back_keep, back_low)
highest = lax.Precision.HIGHEST

def layer_norm(values, scale_vec, shift_vec):
    average = lax.optimization_barrier(jnp.mean(values, axis=-1, keepdims=True))
    centered = values - average
    spread = lax.optimization_barrier(jnp.mean(centered * centered, axis=-1, keepdims=True))
    return centered * lax.rsqrt(spread + 1e-06) * scale_vec + shift_vec

def block_forward(inputs_f, keep_f, token_rep, mixing_rep, gain_rep, shift_rep, adapters, patch_bias, widen_low, narrow_low, hidden_bias, output_bias, width_maps, hidden_maps):
    first_norm = layer_norm(inputs_f, gain_rep[:, 0][:, None, :], shift_rep[:, 0][:, None, :])
    masked = low(first_norm * keep_f)
    mixed_in = jnp.einsum('gpc,gpj->gcj', masked, token_rep[:, 0], precision=highest) + mixing_rep[:, None, :]
    mixed_in = low_back(mixed_in)
    token_hidden = low(jax.nn.gelu(mixed_in, approximate=False))
    mixed_out = jnp.einsum('gcj,gpj->gpc', token_hidden, token_rep[:, 1], precision=highest) + patch_bias[None, :, None]
    mixed_out = low_back(mixed_out)
    residual = inputs_f + mixed_out
    second = low(layer_norm(residual, gain_rep[:, 1][:, None, :], shift_rep[:, 1][:, None, :]))
    adapt_in = jnp.einsum('gpc,cr->gpr', second, width_maps[0], precision=highest)
    adapt_in = jnp.einsum('gpr,grs->gps', adapt_in, adapters[:, 0], precision=highest)
    pre_hidden = jnp.einsum('gpc,cf->gpf', second, widen_low, precision=highest) + hidden_bias
    pre_hidden = low_back(pre_hidden + jnp.einsum('gps,fs->gpf', adapt_in, hidden_maps[0], precision=highest))
    chan_hidden = low(jax.nn.gelu(pre_hidden, approximate=False))
    adapt_out = jnp.einsum('gpf,fr->gpr', chan_hidden, hidden_maps[1], precision=highest)
    adapt_out = jnp.einsum('gpr,grs->gps', adapt_out, adapters[:, 1], precision=highest)
    chan_out = jnp.einsum('gpf,fc->gpc', chan_hidden, narrow_low, precision=highest) + output_bias
    chan_out = low_back(chan_out + jnp.einsum('gps,cs->gpc', adapt_out, width_maps[1], precision=highest))
    return residual + chan_out

def reference(images, kept_mask, pooled_grad, token_weights, norm_gain, norm_bias, mixing_bias, patch_bias, widening, narrowing, hidden_bias, output_bias, width_maps, hidden_maps, queries):
    group_size = 16
    image_total, patches, features = images.shape
    steps_count = image_total // group_size
    token_low = low(token_weights)
    widen_low = low(widening)
    narrow_low = low(narrowing)
    width_f = width_maps.astype(jnp.float32)
    hidden_f = hidden_maps.astype(jnp.float32)
    queries_f = queries.astype(jnp.float32)
    adapter_rank = width_maps.shape[2]

    def one_group(running, pieces):
        image_blk, keep_blk, grad_blk = pieces
        inputs_f = image_blk.astype(jnp.float32)
        keep_f = keep_blk.astype(jnp.float32)[:, :, None]
        kept_count = lax.optimization_barrier(jnp.sum(keep_f, axis=1))
        token_rep = jnp.broadcast_to(token_low[None], (group_size,) + token_low.shape)
        mixing_rep = jnp.broadcast_to(mixing_bias[None], (group_size,) + mixing_bias.shape)
        gain_rep = jnp.broadcast_to(norm_gain[None], (group_size,) + norm_gain.shape)
        shift_rep = jnp.broadcast_to(norm_bias[None], (group_size,) + norm_bias.shape)
        adapters = jnp.zeros((group_size, 2, adapter_rank, adapter_rank), jnp.float32)

        def forward_fn(inputs_v, token_v, mixing_v, gain_v, shift_v, adapter_v, patch_v, widen_v, narrow_v, hidden_v, output_v):
            return block_forward(inputs_v, keep_f, token_v, mixing_v, gain_v, shift_v, adapter_v, patch_v, widen_v, narrow_v, hidden_v, output_v, width_f, hidden_f)
        block_out, pullback = jax.vjp(forward_fn, inputs_f, token_rep, mixing_rep, gain_rep, shift_rep, adapters, patch_bias, widen_low, narrow_low, hidden_bias, output_bias)
        pooled = lax.optimization_barrier(jnp.sum(block_out * keep_f, axis=1)) / kept_count
        cotangent = keep_f * (grad_blk / kept_count)[:, None, :]
        gradients = pullback(cotangent)
        image_grad = gradients[0]
        token_each, mixing_each, gain_each, shift_each, adapter_each = gradients[1:6]
        vector = jnp.concatenate([token_each.reshape(group_size, -1), mixing_each, gain_each.reshape(group_size, -1), shift_each.reshape(group_size, -1), adapter_each.reshape(group_size, -1)], axis=1)
        vector_low = low(vector)

        def one_query(query_row):
            return lax.optimization_barrier(jnp.sum(vector_low * query_row[None, :], axis=1))
        scores = lax.map(one_query, queries_f).T
        group_sums = (lax.optimization_barrier(jnp.sum(token_each, axis=0)), lax.optimization_barrier(jnp.sum(gain_each, axis=0)), lax.optimization_barrier(jnp.sum(shift_each, axis=0)), lax.optimization_barrier(jnp.sum(mixing_each, axis=0)), gradients[6], gradients[7], gradients[8], gradients[9], gradients[10])
        running = jax.tree.map(jnp.add, running, group_sums)
        return (running, (pooled, image_grad, scores))
    start = (jnp.zeros(token_weights.shape, jnp.float32), jnp.zeros(norm_gain.shape, jnp.float32), jnp.zeros(norm_bias.shape, jnp.float32), jnp.zeros(mixing_bias.shape, jnp.float32), jnp.zeros(patch_bias.shape, jnp.float32), jnp.zeros(widening.shape, jnp.float32), jnp.zeros(narrowing.shape, jnp.float32), jnp.zeros(hidden_bias.shape, jnp.float32), jnp.zeros(output_bias.shape, jnp.float32))
    blocks = (images.reshape(steps_count, group_size, patches, features), kept_mask.reshape(steps_count, group_size, patches), pooled_grad.reshape(steps_count, group_size, features))
    totals, stacked = lax.scan(one_group, start, blocks)
    pooled = stacked[0].reshape(image_total, features)
    image_grad = stacked[1].reshape(image_total, patches, features)
    influence = stacked[2].reshape(image_total, -1)
    return (pooled, image_grad, totals[0], totals[1], totals[2], totals[3], totals[4], totals[5], totals[6], totals[7], totals[8], influence)
```

```python
import functools

import jax
import jax.numpy as jnp
from jax import lax
from jax.experimental import pallas as pl
from jax.experimental.pallas import tpu as pltpu
from jax.sharding import PartitionSpec as P

norm_eps = 1e-06
bf16 = jnp.bfloat16
f32 = jnp.float32
vmem_cap = 56 * 1024 * 1024


def dot(left, right):
    return jnp.dot(left, right, preferred_element_type=f32)


def dot_nt(left, right):
    return lax.dot_general(left, right, (((1,), (1,)), ((), ())), preferred_element_type=f32)


def dot_tn(left, right):
    return lax.dot_general(left, right, (((0,), (0,)), ((), ())), preferred_element_type=f32)


def gelu_pair(values):
    reach = jnp.abs(values)
    ratio = 1.0 / (1.0 + 0.23164188 * reach)
    bell = jnp.exp2(values * values * -0.7213475204444817)
    series = 0.5307027145
    series = series * ratio - 0.7265760135
    series = series * ratio + 0.7107068705
    series = series * ratio - 0.142248368
    series = series * ratio + 0.127414796
    tail = series * ratio * bell
    cumulative = jnp.where(values >= 0.0, 1.0 - tail, tail)
    return (values * cumulative, cumulative + values * bell * 0.3989422804014327)


def normalize(values):
    average = jnp.mean(values, axis=-1, keepdims=True)
    centered = values - average
    spread = jnp.mean(centered * centered, axis=-1, keepdims=True)
    inverse = lax.rsqrt(spread + norm_eps)
    return (centered * inverse, inverse)


def norm_back(grad_norm, normed, inverse):
    first_mean = jnp.mean(grad_norm, axis=-1, keepdims=True)
    second_mean = jnp.mean(grad_norm * normed, axis=-1, keepdims=True)
    return inverse * (grad_norm - first_mean - normed * second_mean)


def token_forward_kernel(
    image_ref, keep_ref, inward_t_ref, outward_ref, gain_ref, shift_ref, mixing_ref, patch_ref, width_ref,
    hidden_ref, slope_ref, second_ref, normed_ref, inverse_ref, pooled_ref, left_ref,
):
    inputs = image_ref[0].astype(f32)
    keep = keep_ref[0]
    normed_one, _ = normalize(inputs)
    masked = ((normed_one * gain_ref[0:1] + shift_ref[0:1]) * keep).astype(bf16)
    mixed = dot(inward_t_ref[...], masked) + mixing_ref[...]
    hidden, slope = gelu_pair(mixed)
    hidden = hidden.astype(bf16)
    hidden_ref[0] = hidden
    slope_ref[0] = slope.astype(bf16)
    residual = inputs + dot(outward_ref[...], hidden) + patch_ref[...]
    pooled_ref[0] = jnp.sum(residual * keep, axis=0, keepdims=True)
    normed_two, inverse_two = normalize(residual)
    second = (normed_two * gain_ref[1:2] + shift_ref[1:2]).astype(bf16)
    second_ref[0] = second
    normed_ref[0] = normed_two.astype(bf16)
    inverse_ref[0] = inverse_two
    left_ref[0] = dot(second, width_ref[...])


def whole(shape):
    return pl.BlockSpec(shape, lambda i: (0,) * len(shape))


def each(shape):
    return pl.BlockSpec((1,) + shape, lambda i: (i,) + (0,) * len(shape))


def token_forward(images, keep, inward_t, outward, norm_gain, norm_bias, mixing_col, patch_col, width_map):
    count, patches, features = images.shape
    mixers = inward_t.shape[0]
    rank = width_map.shape[1]
    return pl.pallas_call(
        token_forward_kernel,
        grid=(count,),
        in_specs=[
            each((patches, features)), each((patches, 1)), whole((mixers, patches)), whole((patches, mixers)),
            whole((2, features)), whole((2, features)), whole((mixers, 1)), whole((patches, 1)), whole((features, rank)),
        ],
        out_specs=[
            each((mixers, features)), each((mixers, features)), each((patches, features)), each((patches, features)),
            each((patches, 1)), each((1, features)), each((patches, rank)),
        ],
        out_shape=[
            jax.ShapeDtypeStruct((count, mixers, features), bf16),
            jax.ShapeDtypeStruct((count, mixers, features), bf16),
            jax.ShapeDtypeStruct((count, patches, features), bf16),
            jax.ShapeDtypeStruct((count, patches, features), bf16),
            jax.ShapeDtypeStruct((count, patches, 1), f32),
            jax.ShapeDtypeStruct((count, 1, features), f32),
            jax.ShapeDtypeStruct((count, patches, rank), f32),
        ],
        compiler_params=pltpu.CompilerParams(vmem_limit_bytes=vmem_cap),
        name="token_forward",
    )(images, keep, inward_t, outward, norm_gain, norm_bias, mixing_col, patch_col, width_map)


def channel_kernel(
    blocks, second_ref, keep_ref, back_ref, left_ref, widen_ref, bias_ref, hidden_map_ref,
    grad_ref, pooled_ref, sum_ref, adapter_ref, share_ref, total_ref,
):
    step = pl.program_id(0)
    second = second_ref[0]
    keep = keep_ref[0]
    hidden_size = widen_ref.shape[1]
    width = hidden_size // blocks

    @pl.when(step == 0)
    def _():
        total_ref[...] = jnp.zeros_like(total_ref)
        sum_ref[...] = jnp.zeros_like(sum_ref)

    grad = None
    right = None
    for block in range(blocks):
        cols = slice(block * width, (block + 1) * width)
        widen = widen_ref[:, cols]
        pre = dot(second, widen) + bias_ref[:, cols]
        hidden, slope = gelu_pair(pre)
        hidden = hidden.astype(bf16).astype(f32)
        pooled_ref[0, :, cols] = jnp.sum(hidden * keep, axis=0, keepdims=True)
        pre_grad = (slope * back_ref[0, :, cols] * keep).astype(bf16)
        sum_ref[:, cols] += jnp.sum(pre_grad.astype(f32), axis=0, keepdims=True)
        part = dot_nt(pre_grad, widen)
        grad = part if grad is None else grad + part
        part = dot_nt(pre_grad, hidden_map_ref[:, cols])
        right = part if right is None else right + part
        total_ref[:, cols] += dot_tn(second, pre_grad)
    grad_ref[0] = grad
    adapter_ref[0] = lax.dot_general(
        left_ref[0], right, (((0,), (0,)), ((), ())), precision=lax.Precision.HIGHEST, preferred_element_type=f32
    )

    @pl.when(step == pl.num_programs(0) - 1)
    def _():
        share_ref[...] = total_ref[...].astype(bf16)


def channel(second, keep, back_rows, left, widen, bias_row, hidden_map_t):
    count, patches, features = second.shape
    hidden_size = widen.shape[1]
    rank = left.shape[2]
    once = pl.Buffered(1)
    return pl.pallas_call(
        functools.partial(channel_kernel, 4),
        grid=(count,),
        in_specs=[
            each((patches, features)), each((patches, 1)), each((1, hidden_size)), each((patches, rank)),
            pl.BlockSpec((features, hidden_size), lambda i: (0, 0), pipeline_mode=once),
            whole((1, hidden_size)), whole((rank, hidden_size)),
        ],
        out_specs=[
            each((patches, features)), each((1, hidden_size)), whole((1, hidden_size)), each((rank, rank)),
            pl.BlockSpec((features, hidden_size), lambda i: (0, 0), pipeline_mode=once),
        ],
        out_shape=[
            jax.ShapeDtypeStruct((count, patches, features), f32),
            jax.ShapeDtypeStruct((count, 1, hidden_size), f32),
            jax.ShapeDtypeStruct((1, hidden_size), f32),
            jax.ShapeDtypeStruct((count, rank, rank), f32),
            jax.ShapeDtypeStruct((features, hidden_size), bf16),
        ],
        scratch_shapes=[pltpu.VMEM((features, hidden_size), f32)],
        compiler_params=pltpu.CompilerParams(vmem_limit_bytes=vmem_cap),
        name="channel",
    )(second, keep, back_rows, left, widen, bias_row, hidden_map_t)


def token_backward_kernel(
    image_ref, keep_ref, row_ref, grad_ref, normed_ref, inverse_ref, hidden_ref, slope_ref,
    inward_ref, outward_t_ref, gain_ref, shift_ref,
    image_grad_ref, vector_ref, sums_ref, patch_ref, total_ref,
):
    step = pl.program_id(0)
    patches, features = image_ref.shape[1:]
    mixers = hidden_ref.shape[1]
    keep = keep_ref[0]
    grad = grad_ref[0]
    normed_two = normed_ref[0].astype(f32)
    half = features // 2
    residual_grad = keep * row_ref[0] + norm_back(grad * gain_ref[1:2], normed_two, inverse_ref[0])
    gain_two = jnp.sum(grad * normed_two, axis=0, keepdims=True)
    shift_two = jnp.sum(grad, axis=0, keepdims=True)
    low = residual_grad.astype(bf16)
    outward_grad = dot_nt(low, hidden_ref[0])
    mixed_grad = (dot(outward_t_ref[...], low) * slope_ref[0].astype(f32)).astype(bf16)
    mixing = dot_nt(jnp.ones((8, features), bf16), mixed_grad)[0:1]
    normed_one, inverse_one = normalize(image_ref[0].astype(f32))
    masked = ((normed_one * gain_ref[0:1] + shift_ref[0:1]) * keep).astype(bf16)
    inward_grad = dot_nt(masked, mixed_grad)
    first_grad = dot(inward_ref[...], mixed_grad) * keep
    gain_one = jnp.sum(first_grad * normed_one, axis=0, keepdims=True)
    shift_one = jnp.sum(first_grad, axis=0, keepdims=True)
    image_grad_ref[0] = residual_grad + norm_back(first_grad * gain_ref[0:1], normed_one, inverse_one)
    vector_ref[0, 0:patches] = inward_grad.astype(bf16)
    vector_ref[0, patches : 2 * patches] = outward_grad.astype(bf16)
    rows = [mixing]
    for row in (gain_one, gain_two, shift_one, shift_two):
        for at in range(0, features, mixers):
            rows.append(row[:, at : at + mixers])
    small = jnp.concatenate(rows, axis=0)
    vector_ref[0, 2 * patches : 2 * patches + len(rows)] = small.astype(bf16)

    @pl.when(step == 0)
    def _():
        total_ref[...] = jnp.zeros_like(total_ref)
        sums_ref[...] = jnp.zeros_like(sums_ref)
        patch_ref[...] = jnp.zeros_like(patch_ref)

    total_ref[0] += inward_grad
    total_ref[1] += outward_grad
    sums_ref[...] += small
    patch_ref[...] += jnp.sum(low.astype(f32), axis=1, keepdims=True)


def token_backward(images, keep, rows, grad, normed, inverse, hidden, slope, inward, outward_t, norm_gain, norm_bias):
    count, patches, features = images.shape
    mixers = hidden.shape[1]
    small = 1 + 4 * (features // mixers)
    return pl.pallas_call(
        token_backward_kernel,
        grid=(count,),
        in_specs=[
            each((patches, features)), each((patches, 1)), each((1, features)), each((patches, features)),
            each((patches, features)), each((patches, 1)), each((mixers, features)), each((mixers, features)),
            whole((patches, mixers)), whole((mixers, patches)), whole((2, features)), whole((2, features)),
        ],
        out_specs=[
            each((patches, features)), each((2 * patches + small, mixers)), whole((small, mixers)), whole((patches, 1)),
            whole((2, patches, mixers)),
        ],
        out_shape=[
            jax.ShapeDtypeStruct((count, patches, features), f32),
            jax.ShapeDtypeStruct((count, 2 * patches + small, mixers), bf16),
            jax.ShapeDtypeStruct((small, mixers), f32),
            jax.ShapeDtypeStruct((patches, 1), f32),
            jax.ShapeDtypeStruct((2, patches, mixers), f32),
        ],
        compiler_params=pltpu.CompilerParams(vmem_limit_bytes=vmem_cap),
        name="token_backward",
    )(images, keep, rows, grad, normed, inverse, hidden, slope, inward, outward_t, norm_gain, norm_bias)


def score_kernel(received_ref, query_ref, score_ref):
    step = pl.program_id(0)
    rows = received_ref.shape[0]
    width = received_ref.shape[2]

    @pl.when(step == 0)
    def _():
        score_ref[...] = jnp.zeros_like(score_ref)

    total = None
    for row in range(rows):
        part = dot_nt(received_ref[row], query_ref[:, row * width : (row + 1) * width])
        total = part if total is None else total + part
    score_ref[...] += total


def scores(received, queries, step_rows):
    rows, count, width = received.shape
    asked = queries.shape[0]
    return pl.pallas_call(
        score_kernel,
        grid=(rows // step_rows,),
        in_specs=[
            pl.BlockSpec((step_rows, count, width), lambda i: (i, 0, 0)),
            pl.BlockSpec((asked, step_rows * width), lambda i: (0, i)),
        ],
        out_specs=whole((count, asked)),
        out_shape=jax.ShapeDtypeStruct((count, asked), f32),
        compiler_params=pltpu.CompilerParams(vmem_limit_bytes=vmem_cap),
        name="scores",
    )(received, queries)


def body(
    images,
    kept_mask,
    pooled_grad,
    token_weights,
    norm_gain,
    norm_bias,
    mixing_bias,
    patch_bias,
    widening,
    narrowing,
    hidden_bias,
    output_bias,
    width_maps,
    hidden_maps,
    queries,
):
    count, patches, features = images.shape
    mixers = mixing_bias.shape[0]
    rank = width_maps.shape[2]
    hidden_size = hidden_bias.shape[0]
    groups = lax.axis_size("dp")
    group = lax.axis_index("dp")
    share = queries.shape[1]
    asked = queries.shape[0]

    token_low = lax.all_gather(
        jnp.swapaxes(token_weights, 1, 2).astype(bf16), "dp", axis=1, tiled=True
    )
    widen_own = lax.all_gather(widening.astype(bf16), "dp", axis=0, tiled=True)
    widen = lax.all_gather(widen_own, "mp", axis=1, tiled=True)
    narrow_own = lax.all_gather(narrowing.astype(bf16), "dp", axis=1, tiled=True)
    hidden_map_t = lax.all_gather(hidden_maps[0].T, "mp", axis=1, tiled=True)

    keep_f = kept_mask.astype(f32)
    kept_count = jnp.sum(keep_f, axis=1, keepdims=True)
    keep = keep_f[:, :, None]
    grad_rows = pooled_grad / kept_count
    grad_low = grad_rows.astype(bf16)
    grad_group = lax.all_gather(grad_low, "mp", axis=0, tiled=True)
    back_part = dot_nt(grad_group, narrow_own)
    back_rows = lax.all_to_all(back_part.astype(bf16), "mp", split_axis=0, concat_axis=1, tiled=True).astype(f32)

    inward_t, outward_t = (token_low[0], token_low[1])
    hidden, slope, second, normed, inverse, pooled_in, left = token_forward(
        images, keep, inward_t, outward_t.T, norm_gain, norm_bias, mixing_bias[:, None], patch_bias[:, None], width_maps[0]
    )
    second_grad, chan_pooled, hidden_sum, adapter_in, widen_share = channel(
        second, keep, back_rows[:, None, :], left, widen, hidden_bias[None, :], hidden_map_t
    )
    image_grad, vector, small_sums, patch_sum, token_sum = token_backward(
        images, keep, grad_rows[:, None, :], second_grad, normed, inverse, hidden, slope,
        inward_t.T, outward_t, norm_gain, norm_bias,
    )

    chan_group = lax.all_to_all(
        chan_pooled[:, 0].astype(bf16), "mp", split_axis=1, concat_axis=0, tiled=True
    )
    pooled_part = dot(chan_group, jnp.concatenate([narrow_own, hidden_maps[1]], axis=1))
    pooled_back = lax.psum_scatter(pooled_part, "mp", scatter_dimension=0, tiled=True)
    pooled = (pooled_in[:, 0] + pooled_back[:, :features]) / kept_count + output_bias
    adapter_out = pooled_back[:, features:, None] * dot(grad_low, width_maps[1])[:, None, :]

    chan_all = lax.all_gather(chan_group, "dp", axis=0, tiled=True)
    grad_all = lax.all_to_all(grad_group, "dp", split_axis=1, concat_axis=0, tiled=True)
    narrowing_grad = dot_tn(chan_all, grad_all)

    widen_mine = lax.psum_scatter(widen_share, "mp", scatter_dimension=1, tiled=True)
    widening_grad = lax.psum_scatter(widen_mine, "dp", scatter_dimension=0, tiled=True).astype(f32)

    token_mine = lax.psum_scatter(token_sum.astype(bf16), "dp", scatter_dimension=2, tiled=True)
    token_grad = lax.psum(token_mine.astype(f32), "mp")

    row_ends = [-(-share * (place + 1) // mixers) for place in range(groups)]
    row_starts = [share * place // mixers for place in range(groups)]
    part_rows = max(end - start for start, end in zip(row_starts, row_ends))
    adapter_rows = jnp.concatenate(
        [adapter_in.reshape(count, rank * rank), adapter_out.reshape(count, rank * rank)], axis=1
    ).astype(bf16)
    whole_rows = row_starts[-1] + part_rows
    fill = (whole_rows - vector.shape[1]) * mixers - adapter_rows.shape[1]
    adapter_rows = jnp.pad(adapter_rows, ((0, 0), (0, fill))).reshape(count, -1, mixers)
    rows_first = jnp.swapaxes(jnp.concatenate([vector, adapter_rows], axis=1), 0, 1)
    parts = jnp.stack([rows_first[start : start + part_rows] for start in row_starts], axis=0)
    received = lax.all_to_all(parts, "dp", split_axis=0, concat_axis=2, tiled=True)[0]
    offset = group * share - mixers * (group * share // mixers)
    shifted = lax.dynamic_update_slice(
        jnp.zeros((asked, part_rows * mixers), bf16), queries, (jnp.int32(0), offset.astype(jnp.int32))
    )
    step_rows = max(step for step in range(1, 10) if part_rows % step == 0)
    partial_scores = scores(received, shifted, step_rows)
    influence = lax.psum_scatter(partial_scores, "dp", scatter_dimension=0, tiled=True)

    small, patch_grad, hidden_grad, output_grad = lax.psum(
        (
            small_sums,
            patch_sum[:, 0],
            hidden_sum[0],
            jnp.sum(grad_low.astype(f32) * kept_count, axis=0),
        ),
        ("dp", "mp"),
    )
    lines = features // mixers
    mixing_grad = small[0]
    gain_grad = small[1 : 1 + 2 * lines].reshape(2, features)
    shift_grad = small[1 + 2 * lines :].reshape(2, features)
    return (
        pooled,
        image_grad,
        token_grad,
        gain_grad,
        shift_grad,
        mixing_grad,
        patch_grad,
        widening_grad,
        narrowing_grad,
        hidden_grad,
        output_grad,
        influence,
    )


def solution(mesh):
    placed = (
        P(("dp", "mp"), None, None),
        P(("dp", "mp"), None),
        P(("dp", "mp"), None),
        P(None, None, "dp"),
        P(),
        P(),
        P(),
        P(),
        P("dp", "mp"),
        P("mp", "dp"),
        P(),
        P(),
        P(),
        P(None, "mp", None),
        P(None, "dp"),
    )
    return jax.shard_map(
        body,
        mesh=mesh,
        in_specs=placed,
        out_specs=(
            P(("dp", "mp"), None),
            P(("dp", "mp"), None, None),
            P(None, None, "dp"),
            P(),
            P(),
            P(),
            P(),
            P("dp", "mp"),
            P("mp", "dp"),
            P(),
            P(),
            P(("dp", "mp"), None),
        ),
        check_vma=False,
    )
```

```python
import functools

import jax
import jax.numpy as jnp
from jax import lax
from jax.experimental import pallas as pl
from jax.experimental.pallas import tpu as pltpu
from jax.sharding import Mesh
from jax.sharding import PartitionSpec as P

norm_eps = 1e-06
bf16 = jnp.bfloat16
f32 = jnp.float32
vmem_cap = 58 * 1024 * 1024
dp_axes = ("line", "side")


def dot(left, right):
    return jnp.dot(left, right, preferred_element_type=f32)


def dot_nt(left, right):
    return lax.dot_general(left, right, (((1,), (1,)), ((), ())), preferred_element_type=f32)


def dot_tn(left, right):
    return lax.dot_general(left, right, (((0,), (0,)), ((), ())), preferred_element_type=f32)


def exact_tn(left, right):
    return lax.dot_general(
        left, right, (((0,), (0,)), ((), ())), precision=lax.Precision.HIGHEST, preferred_element_type=f32
    )


def gelu_pair(values):
    cumulative = 0.5 + 0.5 * lax.erf(values * 0.7071067811865476)
    density = jnp.exp2(values * values * -0.7213475204444817) * 0.3989422804014327
    return (values * cumulative, cumulative + values * density)


def normalize(values):
    average = jnp.mean(values, axis=-1, keepdims=True)
    centered = values - average
    spread = jnp.mean(centered * centered, axis=-1, keepdims=True)
    inverse = lax.rsqrt(spread + norm_eps)
    return (centered * inverse, inverse)


def norm_back(grad_norm, normed, inverse):
    first_mean = jnp.mean(grad_norm, axis=-1, keepdims=True)
    second_mean = jnp.mean(grad_norm * normed, axis=-1, keepdims=True)
    return inverse * (grad_norm - first_mean - normed * second_mean)


def whole(shape):
    return pl.BlockSpec(shape, lambda i: (0,) * len(shape))


def each(shape, first=0):
    return pl.BlockSpec((1,) + shape, lambda i: (i + first,) + (0,) * len(shape))


def struct(shape, dtype=f32):
    return jax.ShapeDtypeStruct(shape, dtype)


def place_of():
    return lax.axis_index("line") * lax.axis_size("side") + lax.axis_index("side")


def assemble_tokens(piece_refs, codes, token_ref):
    place = place_of()
    for piece_ref, own_codes in zip(piece_refs, codes):
        own = piece_ref.shape[2]
        for at, code in enumerate(own_codes):
            start = 0 if code is None else pl.multiple_of((place ^ code) * own, own)
            for which in range(2):
                token_ref[which, pl.ds(start, own)] = piece_ref[at, which]


def token_forward_kernel(
    codes, image_ref, keep_ref, gain_ref, shift_ref, column_ref, width_ref, *refs,
):
    piece_refs, refs = (refs[: len(codes)], refs[len(codes) :])
    hidden_ref, slope_ref, second_ref, normed_ref, inverse_ref, pooled_ref, left_ref, token_ref, padded_ref = refs
    mixers = token_ref.shape[1]
    patches = image_ref.shape[1]

    @pl.when(pl.program_id(0) == 0)
    def _():
        assemble_tokens(piece_refs, codes, token_ref)
        padded_ref[patches:] = jnp.zeros((padded_ref.shape[0] - patches, padded_ref.shape[1]), f32)

    padded_ref[:patches] = image_ref[0].astype(f32)
    inputs = padded_ref[...]
    keep = keep_ref[0]
    normed_one, _ = normalize(inputs)
    masked = ((normed_one * gain_ref[0:1] + shift_ref[0:1]) * keep).astype(bf16)
    mixed = dot(token_ref[0], masked) + column_ref[:mixers]
    hidden, slope = gelu_pair(mixed)
    hidden = hidden.astype(bf16)
    hidden_ref[0] = hidden
    slope_ref[0] = slope.astype(bf16)
    residual = inputs + dot_tn(token_ref[1], hidden) + column_ref[mixers:]
    pooled_ref[0] = jnp.sum(residual * keep, axis=0, keepdims=True)
    normed_two, inverse_two = normalize(residual)
    second = (normed_two * gain_ref[1:2] + shift_ref[1:2]).astype(bf16)
    second_ref[0] = second
    normed_ref[0] = normed_two.astype(bf16)
    inverse_ref[0] = inverse_two
    left_ref[0] = dot_nt(second, width_ref[0])


def token_forward(images, keep, tokens, codes, norm_gain, norm_bias, column, width_maps, first, last):
    count = last - first
    _, patches, features = images.shape
    rows = keep.shape[1]
    mixers = column.shape[0] - rows
    rank = width_maps.shape[1]
    return pl.pallas_call(
        functools.partial(token_forward_kernel, codes),
        grid=(count,),
        in_specs=[
            each((patches, features), first), each((rows, 1), first),
            whole((2, features)), whole((2, features)), whole((mixers + rows, 1)), whole((2, rank, features)),
        ]
        + [whole(piece.shape) for piece in tokens],
        out_specs=[
            each((mixers, features)), each((mixers, features)), each((rows, features)), each((rows, features)),
            each((rows, 1)), each((1, features)), each((rows, rank)),
        ],
        out_shape=[
            struct((count, mixers, features), bf16), struct((count, mixers, features), bf16),
            struct((count, rows, features), bf16), struct((count, rows, features), bf16),
            struct((count, rows, 1)), struct((count, 1, features)), struct((count, rows, rank)),
        ],
        scratch_shapes=[pltpu.VMEM((2, mixers, rows), bf16), pltpu.VMEM((rows, features), f32)],
        compiler_params=pltpu.CompilerParams(vmem_limit_bytes=vmem_cap),
        name="token_forward",
    )(images, keep, norm_gain, norm_bias, column, width_maps, *tokens)


def piece_copies(piece_refs, widen_ref, maps_ref, sems, spans, layout):
    depth, wide_rows, map_at, map_rows = layout
    copies = []
    place = place_of()
    for at, (piece_ref, (codes, column)) in enumerate(zip(piece_refs, spans)):
        cols = pl.ds(column, piece_ref.shape[1])
        for part, code in enumerate(codes):
            for which, (target, first, rows) in enumerate(((widen_ref, 0, wide_rows), (maps_ref, map_at, map_rows))):
                start = 0 if code is None else pl.multiple_of((place ^ code) * rows, rows)
                copy = pltpu.make_async_copy(
                    piece_ref.at[pl.ds(part * depth + first, rows)],
                    target.at[pl.ds(start, rows), cols],
                    sems.at[at, part, which],
                )
                copies.append((column, copy))
    return copies


def channel_kernel(
    spans, layout, codes, first, resumed, final,
    second_ref, keep_ref, left_ref, back_ref, bias_ref, rows_ref, width_ref, *refs,
):
    piece_refs, refs = (refs[: len(spans)], refs[len(spans) :])
    if resumed:
        sum_before_ref, before_ref, *refs = refs
    grad_ref, pooled_ref, sum_ref, adapter_ref, *refs = refs
    share_refs, refs = (refs[: 2 if final else 1], refs[2 if final else 1 :])
    widen_ref, maps_ref, total_ref, right_ref, out_ref, pair_ref, sems = refs
    step = pl.program_id(0)
    steps = pl.num_programs(0)
    count = pooled_ref.shape[0]
    total_rows, features = second_ref.shape
    rows = total_rows // count
    rank = left_ref.shape[1]
    own = bias_ref.shape[1] // 4
    model = lax.axis_index("far") * lax.axis_size("core") + lax.axis_index("core")
    second = second_ref[...]
    keep = keep_ref[...].reshape(total_rows, 1)
    copies = piece_copies(piece_refs, widen_ref, maps_ref, sems, spans, layout)

    @pl.when(step == 0)
    def _():
        for _, copy in copies:
            copy.start()
        for column, copy in copies:
            if column < 2 * own:
                copy.wait()
        if resumed:
            sum_ref[...] = sum_before_ref[...]
        else:
            sum_ref[...] = jnp.zeros_like(sum_ref)
        right_ref[...] = jnp.zeros_like(right_ref)
        out_ref[...] = jnp.zeros_like(out_ref)
        grad_ref[...] = jnp.zeros_like(grad_ref)

    @pl.when(step > 0)
    def _():
        for column, copy in copies:
            if column >= 2 * own:
                copy.wait()

    for half in range(2):
        cols = slice(half * own, (half + 1) * own)
        wide = pl.ds(pl.multiple_of((2 * step + half) * own, own), own)
        widen = widen_ref[:, wide]
        bias_at = pl.multiple_of((model ^ (2 * step + half)) * own, own)
        pre = dot(second, widen) + bias_ref[:, pl.ds(bias_at, own)]
        hidden, slope = gelu_pair(pre)
        hidden = (hidden.astype(bf16).astype(f32) * keep).reshape(count, rows, own)
        pooled_hidden = jnp.sum(hidden, axis=1)
        pooled_ref[:, cols] = pooled_hidden
        back = back_ref[first : first + count, cols].astype(f32)[:, None, :]
        pre_grad = (slope * keep).reshape(count, rows, own) * back
        pre_grad = pre_grad.reshape(total_rows, own).astype(bf16)
        sum_ref[:, pl.ds(bias_at, own)] += jnp.sum(pre_grad.astype(f32), axis=0, keepdims=True)
        grad_ref[...] += dot_nt(pre_grad, widen)
        right_ref[...] += dot_nt(pre_grad, maps_ref[:rank, wide])
        out_ref[...] += dot_nt(pooled_hidden.astype(bf16), maps_ref[rank:, wide])
        share = dot_tn(second, pre_grad)
        if resumed:
            share = share + before_ref[:, cols].astype(f32)
        if not final:
            share_refs[0][:, cols] = share.astype(bf16)
            continue
        total_ref[...] = share
        place = place_of()
        part_rows = share_refs[half].shape[-2]
        for index, code in codes:
            start = 0 if code is None else pl.multiple_of((place ^ code) * part_rows, part_rows)
            share_refs[half][(0, *index)] = total_ref[pl.ds(start, part_rows)].astype(bf16)

    @pl.when(step == steps - 1)
    def _():
        outer = dot_nt(rows_ref[first : first + count], width_ref[1])
        lines = adapter_ref.shape[2] // rank
        pair_ref[2 * rank :] = jnp.zeros((pair_ref.shape[0] - 2 * rank, rank), f32)
        for image in range(count):
            span = slice(image * rows, (image + 1) * rows)
            pair_ref[:rank] = exact_tn(left_ref[span], right_ref[span])
            pair_ref[rank : 2 * rank] = exact_tn(out_ref[image : image + 1], outer[image : image + 1])
            adapter_ref[image] = jnp.concatenate(
                [pair_ref[pl.ds(line, adapter_ref.shape[1], stride=lines)] for line in range(lines)], axis=1
            ).astype(bf16)


def channel(
    second, keep, left, back_rows, bias_row, grad_low, width_maps, pieces, spans, layout, codes, share_shape, before,
    mixers, chunk, first, last, final,
):
    count = last - first
    total_rows, features = second.shape
    hidden_size = bias_row.shape[1]
    rank = left.shape[1]
    held = back_rows.shape[0]
    lines = mixers // rank
    adapter_rows = -(-2 * rank // lines)
    once = pl.Buffered(1)
    resumed = before is not None
    anywhere = pl.BlockSpec(memory_space=pl.ANY)
    wide = hidden_size // 2

    def columns(rows):
        return pl.BlockSpec((rows, wide), lambda i: (0, i))

    if final:
        share_specs = [
            pl.BlockSpec((1, *share_shape), lambda i: (i,) + (0,) * len(share_shape)) for _ in range(2)
        ]
        share_out = [struct((2, *share_shape), bf16) for _ in range(2)]
    else:
        share_specs = [columns(features)]
        share_out = [struct((features, hidden_size), bf16)]
    return pl.pallas_call(
        functools.partial(channel_kernel, spans, layout, codes, first, resumed, final),
        grid=(2,),
        in_specs=[
            whole((total_rows, features)), pl.BlockSpec((count, total_rows // count, 1), lambda i: (chunk, 0, 0)),
            whole((total_rows, rank)), columns(held),
            whole((1, hidden_size)), whole((held, features)), whole((2, rank, features)),
        ]
        + [anywhere] * len(pieces)
        + ([whole((1, hidden_size)), columns(features)] if resumed else []),
        out_specs=[
            whole((total_rows, features)), columns(count), whole((1, hidden_size)), whole((count, adapter_rows, mixers)),
        ]
        + share_specs,
        out_shape=[
            struct((total_rows, features)), struct((count, hidden_size)), struct((1, hidden_size)),
            struct((count, adapter_rows, mixers), bf16),
        ]
        + share_out,
        scratch_shapes=[
            pltpu.VMEM((features, hidden_size), bf16),
            pltpu.VMEM((2 * rank, hidden_size), bf16),
            pltpu.VMEM((features, hidden_size // 4), f32),
            pltpu.VMEM((total_rows, rank), f32),
            pltpu.VMEM((count, rank), f32),
            pltpu.VMEM((adapter_rows * lines, rank), f32),
            pltpu.SemaphoreType.DMA((len(spans), max(len(span[0]) for span in spans), 2)),
        ],
        compiler_params=pltpu.CompilerParams(vmem_limit_bytes=vmem_cap),
        name="channel",
    )(
        second, keep, left, back_rows, bias_row, grad_low, width_maps, *pieces, *(before if resumed else [])
    )


def token_backward_kernel(
    codes, resumed, patches, row_starts,
    image_ref, keep_ref, row_ref, grad_ref, normed_ref, inverse_ref, hidden_ref, slope_ref,
    gain_ref, shift_ref, adapter_ref, hidden_sum_ref, output_sum_ref, *refs,
):
    piece_refs, refs = (refs[: len(codes)], refs[len(codes) :])
    if resumed:
        total_before_ref, sums_before_ref, _, *refs = refs
    image_grad_ref, parts_ref, sums_ref, total_ref, share_ref, vector_ref, token_ref, padded_ref = refs
    step = pl.program_id(0)
    steps = pl.num_programs(0)
    rows, features = padded_ref.shape
    mixers = hidden_ref.shape[1]
    keep = keep_ref[0]
    grad = grad_ref[0]

    @pl.when(step == 0)
    def _():
        if resumed:
            total_ref[...] = total_before_ref[...]
            sums_ref[...] = sums_before_ref[...]
        else:
            total_ref[...] = jnp.zeros_like(total_ref)
            sums_ref[...] = jnp.zeros_like(sums_ref)
        vector_ref[...] = jnp.zeros_like(vector_ref)
        padded_ref[patches:] = jnp.zeros((rows - patches, features), f32)
        assemble_tokens(piece_refs, codes, token_ref)

    normed_two = normed_ref[0].astype(f32)
    residual_grad = keep * row_ref[0] + norm_back(grad * gain_ref[1:2], normed_two, inverse_ref[0])
    gain_two = jnp.sum(grad * normed_two, axis=0, keepdims=True)
    shift_two = jnp.sum(grad, axis=0, keepdims=True)
    low = residual_grad.astype(bf16)
    outward_grad = dot_nt(low, hidden_ref[0])
    mixed_grad = (dot(token_ref[1], low) * slope_ref[0].astype(f32)).astype(bf16)
    ones = jnp.ones((8, features), bf16)
    mixing = dot_nt(ones, mixed_grad)[0:1]
    patch_sum = dot_nt(ones, low)[0:1]
    padded_ref[:patches] = image_ref[0].astype(f32)
    normed_one, inverse_one = normalize(padded_ref[...])
    masked = ((normed_one * gain_ref[0:1] + shift_ref[0:1]) * keep).astype(bf16)
    inward_grad = dot_nt(masked, mixed_grad)
    first_grad = dot_tn(token_ref[0], mixed_grad) * keep
    gain_one = jnp.sum(first_grad * normed_one, axis=0, keepdims=True)
    shift_one = jnp.sum(first_grad, axis=0, keepdims=True)
    image_grad = residual_grad + norm_back(first_grad * gain_ref[0:1], normed_one, inverse_one)
    image_grad_ref[...] = image_grad[:patches]
    lines = [mixing]
    for row in (gain_one, gain_two, shift_one, shift_two):
        for at in range(0, features, mixers):
            lines.append(row[:, at : at + mixers])
    small = jnp.concatenate(lines, axis=0)
    adapter_at = 2 * patches + len(lines)
    vector_ref[0:patches] = inward_grad[:patches]
    vector_ref[patches : 2 * patches] = outward_grad[:patches]
    vector_ref[2 * patches : adapter_at] = small
    vector_ref[adapter_at : adapter_at + adapter_ref.shape[1]] = adapter_ref[0].astype(f32)
    part_rows = parts_ref.shape[2]
    for place, start in enumerate(row_starts):
        parts_ref[place, 0] = vector_ref[start : start + part_rows].astype(bf16)
    total_ref[0] += inward_grad
    total_ref[1] += outward_grad
    sums_ref[0 : len(lines)] += small
    sums_ref[len(lines) : len(lines) + 1, 0:rows] += patch_sum

    @pl.when(step == steps - 1)
    def _():
        sides, columns, own, wide = share_ref.shape
        half = wide // 3
        line, side = (lax.axis_index("line"), lax.axis_index("side"))
        turned = [total_ref[which].T.astype(bf16) for which in range(2)]
        sums = [sums_ref[row : row + 1, at : at + 128] for row in range(sums_ref.shape[0]) for at in range(0, mixers, 128)]
        for ref in (hidden_sum_ref, output_sum_ref):
            sums += [ref[:, at : at + 128] for at in range(0, ref.shape[1], 128)]
        per_row = half // 128
        depth = len(sums) // per_row
        sums = [jnp.concatenate(sums[at::per_row], axis=0) for at in range(per_row)]
        sums = jnp.concatenate(sums, axis=1).astype(bf16)
        for place in range(sides * columns):
            at = ((place % sides) ^ side, (place // sides) ^ line)
            for which in range(2):
                part = turned[which][place * own : (place + 1) * own]
                share_ref[at[0], at[1], :, which * half : which * half + rows] = part
            if depth <= own:
                share_ref[at[0], at[1], 0:depth, 2 * half :] = sums


def token_backward(
    images, keep, grad_rows, grad, normed, inverse, hidden, slope, tokens, codes, norm_gain, norm_bias, adapters, hidden_sum,
    output_sum, before, row_starts, part_rows, columns, first, last,
):
    count = last - first
    _, patches, features = images.shape
    rows = keep.shape[1]
    mixers = hidden.shape[1]
    adapter_rows = adapters.shape[1]
    groups = len(row_starts)
    resumed = before is not None
    small = 2 + 4 * (features // mixers)
    held = -(-(row_starts[-1] + part_rows) // 8) * 8
    held = max(held, -(-(2 * patches + small + adapter_rows) // 8) * 8)
    wide = 3 * (-(-rows // 128) * 128)
    share_shape = (groups // columns, columns, mixers // groups, wide)
    return pl.pallas_call(
        functools.partial(token_backward_kernel, codes, resumed, patches, row_starts),
        grid=(count,),
        in_specs=[
            each((patches, features), first), each((rows, 1), first), each((1, features), first), each((rows, features)),
            each((rows, features)), each((rows, 1)), each((mixers, features)), each((mixers, features)),
            whole((2, features)), whole((2, features)), each((adapter_rows, mixers)), whole(hidden_sum.shape), whole(output_sum.shape),
        ]
        + [whole(piece.shape) for piece in tokens]
        + ([whole((2, rows, mixers)), whole((small, mixers)), pl.BlockSpec(memory_space=pl.ANY)] if resumed else []),
        out_specs=[
            pl.BlockSpec((patches, features), lambda i: (0, i + first)), pl.BlockSpec((groups, 1, part_rows, mixers), lambda i: (0, i, 0, 0)),
            whole((small, mixers)), whole((2, rows, mixers)), whole(share_shape),
        ],
        out_shape=[
            struct((patches, images.shape[0] * features)), struct((groups, count, part_rows, mixers), bf16),
            struct((small, mixers)), struct((2, rows, mixers)), struct(share_shape, bf16),
        ],
        scratch_shapes=[
            pltpu.VMEM((held, mixers), f32), pltpu.VMEM((2, mixers, rows), bf16), pltpu.VMEM((rows, features), f32),
        ],
        compiler_params=pltpu.CompilerParams(vmem_limit_bytes=vmem_cap),
        input_output_aliases={len(tokens) + 15: 0} if resumed else {},
        name="token_backward",
    )(
        images, keep, grad_rows, grad, normed, inverse, hidden, slope, norm_gain, norm_bias, adapters, hidden_sum, output_sum,
        *tokens, *(before if resumed else []),
    )


def back_kernel(columns, sides, grad_ref, narrow_ref, back_ref, turned_ref):
    turned_ref[...] = grad_ref[...].astype(f32).T
    own = narrow_ref.shape[0] // columns
    line, side = (lax.axis_index("line"), lax.axis_index("side"))
    total = None
    for code in range(columns):
        start = pl.multiple_of(((line ^ code) * sides + side) * own, own)
        part = dot_tn(turned_ref[pl.ds(start, own)].astype(bf16), narrow_ref[code * own : (code + 1) * own])
        total = part if total is None else total + part
    back_ref[...] = total.astype(bf16)


def back_sent(grads, narrow_line, columns, sides):
    return pl.pallas_call(
        functools.partial(back_kernel, columns, sides),
        out_shape=struct((grads.shape[0], narrow_line.shape[1]), bf16),
        scratch_shapes=[pltpu.VMEM((grads.shape[1], grads.shape[0]), f32)],
        compiler_params=pltpu.CompilerParams(vmem_limit_bytes=vmem_cap),
        name="back_sent",
    )(grads, narrow_line)


def narrow_kernel(count, first, chan_ref, *refs):
    piece_refs, (grad_ref, held_ref, grads_ref, product_ref, sems) = (refs[:-5], refs[-5:])
    blocks, columns, sides, held_rows = held_ref.shape[:4]
    depth = piece_refs[0].shape[0] // columns
    copies = []

    def fetch(piece, part, block, line, side):
        copies.append(
            pltpu.make_async_copy(
                piece_refs[piece].at[pl.ds(part * depth + first, held_rows)],
                held_ref.at[block, line, side],
                sems.at[block, line, side],
            )
        )

    cut = columns // 2
    for core in range(2):
        for line in range(columns):
            fetch(5 * core, line, core, line, 0)
            fetch(5 * core + 1, line, core, line, 1)
            fetch(5 * core + 2, line, 2 + core, line, 0)
            fetch(5 * core + 3 + line // cut, line % cut, 2 + core, line, 1)
    for copy in copies:
        copy.start()
    for copy in copies:
        copy.wait()
    at = 0
    for line in range(columns):
        for side in range(sides):
            for block in range(blocks):
                grads_ref[at : at + count] = held_ref[block, line, side, :count].astype(f32)
                at += count
    product_ref[...] = dot_tn(grads_ref[...].astype(bf16), chan_ref[...])
    own = grad_ref.shape[0]
    grad_ref[...] = product_ref[pl.ds(pl.multiple_of(place_of() * own, own), own)]


def narrow_sums(chan_all, pieces, own_width, count, layout):
    total, hidden = chan_all.shape
    depth, wide_rows, map_at, _ = layout
    columns = pieces[0].shape[0] // depth
    sides = total // (4 * columns * count)
    return pl.pallas_call(
        functools.partial(narrow_kernel, count, wide_rows),
        in_specs=[pl.BlockSpec(memory_space=pltpu.VMEM)] + [pl.BlockSpec(memory_space=pl.ANY)] * len(pieces),
        out_specs=pl.BlockSpec(memory_space=pltpu.VMEM),
        out_shape=struct((own_width, hidden)),
        scratch_shapes=[
            pltpu.VMEM((4, columns, sides, map_at - wide_rows, pieces[0].shape[1]), bf16),
            pltpu.VMEM((total, pieces[0].shape[1]), f32),
            pltpu.VMEM((own_width * columns * sides, hidden), f32),
            pltpu.SemaphoreType.DMA((4, columns, sides)),
        ],
        compiler_params=pltpu.CompilerParams(vmem_limit_bytes=vmem_cap),
        name="narrow_sums",
    )(chan_all, *pieces)


def unpack_kernel(patches, own_ref, other_ref, token_ref, mixing_ref, gain_ref, shift_ref, patch_ref, hidden_ref, output_ref):
    half = own_ref.shape[1] // 3
    total = own_ref[...].astype(f32) + other_ref[...].astype(f32)
    for which in range(2):
        token_ref[which] = total[:, which * half : which * half + patches]
    pieces = []
    for row in range(own_ref.shape[0]):
        for at in range(2 * half, 3 * half, 128):
            pieces.append(total[row : row + 1, at : at + 128])
    mixers, features = (mixing_ref.shape[1], gain_ref.shape[1])
    at = 0

    def fill(ref, row, width, held):
        nonlocal at
        for first in range(0, held, 128):
            size = min(128, width - first)
            if size > 0:
                ref[row : row + 1, first : first + size] = pieces[at][:, :size]
            at += 1

    fill(mixing_ref, 0, mixers, mixers)
    for ref in (gain_ref, shift_ref):
        for row in range(2):
            fill(ref, row, features, features)
    fill(patch_ref, 0, patches, mixers)
    fill(hidden_ref, 0, hidden_ref.shape[1], hidden_ref.shape[1])
    fill(output_ref, 0, features, features)


def unpack(own, other, patches, mixers, features, hidden_size):
    return pl.pallas_call(
        functools.partial(unpack_kernel, patches),
        out_shape=[
            struct((2, own.shape[0], patches)), struct((1, mixers)), struct((2, features)), struct((2, features)),
            struct((1, patches)), struct((1, hidden_size)), struct((1, features)),
        ],
        name="unpack",
    )(own, other)


def score_kernel(parts, shifted, received_ref, query_hbm, score_ref, query_ref, sems):
    rows, _, width = received_ref.shape
    length = query_hbm.shape[0] // parts
    offset = 0
    if shifted:
        place = place_of()
        offset = pl.multiple_of(lax.rem(place * query_hbm.shape[0], width), 16)
        query_ref[0:width] = jnp.zeros((width, query_ref.shape[1]), bf16)
        last = rows * width - 2 * width
        query_ref[last:] = jnp.zeros((2 * width, query_ref.shape[1]), bf16)
    copies = [
        pltpu.make_async_copy(
            query_hbm.at[pl.ds(part * length, length)],
            query_ref.at[pl.ds(offset + part * length, length)],
            sems.at[part],
        )
        for part in range(parts)
    ]
    for copy in copies:
        copy.start()
    waited = 0
    total = None
    for row in range(rows):
        while waited < parts and waited * length < (row + 1) * width:
            copies[waited].wait()
            waited += 1
        part = dot(received_ref[row], query_ref[row * width : (row + 1) * width])
        total = part if total is None else total + part
    score_ref[...] = total


def scores(received, queries_t):
    rows, count, width = received.shape
    share, asked = queries_t.shape
    shifted = share != rows * width
    parts = 7 if share % 112 == 0 else 1
    return pl.pallas_call(
        functools.partial(score_kernel, parts, shifted),
        in_specs=[pl.BlockSpec(memory_space=pltpu.VMEM), pl.BlockSpec(memory_space=pl.ANY)],
        out_specs=pl.BlockSpec(memory_space=pltpu.VMEM),
        out_shape=struct((count, asked)),
        scratch_shapes=[pltpu.VMEM((rows * width, asked), bf16), pltpu.SemaphoreType.DMA((parts,))],
        compiler_params=pltpu.CompilerParams(vmem_limit_bytes=vmem_cap),
        name="scores",
    )(received, queries_t)


def swap(array, axis, code=1):
    devices = lax.axis_size(axis)
    return lax.ppermute(array, axis, [(place, place ^ code) for place in range(devices)])


def swap_both(array, line_code, side_code):
    columns, sides = (lax.axis_size("line"), lax.axis_size("side"))
    pairs = [
        (line * sides + side, (line ^ line_code) * sides + (side ^ side_code))
        for line in range(columns)
        for side in range(sides)
    ]
    return lax.ppermute(array, dp_axes, pairs)


def by_code(parts, place):
    step = 1
    while step < parts.shape[0]:
        pairs = parts.reshape(-1, 2, step, *parts.shape[1:])
        turned = jnp.concatenate([pairs[:, 1:], pairs[:, :1]], axis=1)
        parts = jnp.where((place & step) > 0, turned, pairs).reshape(parts.shape)
        step *= 2
    return parts


def together(*arrays):
    return lax.optimization_barrier(arrays)


def added(left, right):
    return (left.astype(f32) + right.astype(f32)).astype(bf16)


def body(
    images,
    kept_mask,
    pooled_grad,
    token_weights,
    norm_gain,
    norm_bias,
    mixing_bias,
    patch_bias,
    widening,
    narrowing,
    hidden_bias,
    output_bias,
    width_maps,
    hidden_maps,
    queries,
):
    count, patches, features = images.shape
    mixers = mixing_bias.shape[0]
    rank = width_maps.shape[2]
    hidden_size = hidden_bias.shape[0]
    columns = lax.axis_size("line")
    sides = lax.axis_size("side")
    groups = columns * sides
    group = lax.axis_index(dp_axes)
    share, asked = (queries.shape[1], queries.shape[0])
    own_hidden = widening.shape[1]
    own_width = narrowing.shape[1]
    by_hand = groups <= 8 and widening.shape[0] % 16 == 0
    chunks = [(0, count // 2), (count // 2, count)]
    rows = -(-patches // 8) * 8
    extra = rows - patches
    cut = columns // 2

    widen_part = widening.astype(bf16)
    token_part = jnp.pad(jnp.swapaxes(token_weights, 1, 2).astype(bf16), ((0, 0), (0, 0), (0, extra)))
    narrow_part = jnp.swapaxes(narrowing, 0, 1).astype(bf16)
    keep_f = kept_mask.astype(f32)
    kept_count = jnp.sum(keep_f, axis=1, keepdims=True)
    grad_rows = pooled_grad / kept_count
    grad_low = grad_rows.astype(bf16)
    maps_own = jnp.swapaxes(hidden_maps, 1, 2).reshape(2 * rank, own_hidden)
    width_maps = jnp.swapaxes(width_maps, 1, 2)
    keep = jnp.pad(keep_f, ((0, 0), (0, extra)))[:, :, None]
    column = jnp.concatenate([mixing_bias, jnp.pad(patch_bias, (0, extra))])[:, None]
    bias_row = hidden_bias[None, :]
    output_sum = jnp.sum(grad_low.astype(f32) * kept_count, axis=0, keepdims=True)
    if by_hand:
        map_rows = 2 * rank // groups
        maps_part = lax.dynamic_slice_in_dim(maps_own, group * map_rows, map_rows)
        grad_part = jnp.pad(grad_low, ((0, 16 - count), (0, 0)))
        piece = jnp.concatenate([widen_part, grad_part, maps_part])
        depth = piece.shape[0]
        layout = (depth, widen_part.shape[0], depth - map_rows, map_rows)
        token_line = jnp.stack([token_part] + [swap(token_part, "line", code) for code in range(1, columns)])
        piece, token_line = together(piece, token_line)
        tokens = [token_line, swap(token_line, "side")]
        widen_z = [piece] + [swap(piece, "line", code) for code in range(1, columns)]
        grad_pair = jnp.concatenate([grad_low, swap(grad_low, "core")])
        grad_group = jnp.concatenate([grad_pair, swap(grad_pair, "far")])
        grad_near = jnp.concatenate([grad_group, swap(grad_group, "side")])
        line_codes = tuple(sides * code for code in range(columns))
        side_codes = tuple(code ^ 1 for code in line_codes)
        token_codes = (line_codes, side_codes)
        codes = tuple(((side, at), sides * at ^ side) for side in range(sides) for at in range(columns))
        share_shape = (sides, columns, *widening.shape)
    else:
        tokens = [lax.all_gather(token_part, dp_axes, axis=1, tiled=True)[None]]
        token_codes = ((None,),)
        piece = jnp.concatenate([lax.all_gather(widen_part, dp_axes, axis=0, tiled=True), maps_own])
        layout = (piece.shape[0], features, features, 2 * rank)
        piece_x = swap(piece, "far")
        pieces = [piece, swap(piece, "core"), piece_x, swap(piece_x, "core")]
        spans = tuple(((None,), block * own_hidden) for block in range(4))
        codes = (((slice(None),), None),)
        share_shape = (features, own_hidden)

    def forward(chunk):
        out = token_forward(
            images, keep, tokens, token_codes, norm_gain, norm_bias, column, width_maps, *chunks[chunk]
        )
        return list(out)

    forwards = [forward(0)]
    if by_hand:
        forwards[0][:] = together(*forwards[0], *widen_z, grad_near, narrow_part, *tokens)
        widen_z, (grad_near, narrow_part), tokens = (forwards[0][7:-4], forwards[0][-4:-2], forwards[0][-2:])
        forwards[0] = forwards[0][:7]
        widen_line = jnp.concatenate(widen_z)
        widen_y, widen_x = (swap(widen_line, "side"), swap(widen_line, "far"))
        narrow_z = [narrow_part] + [swap(narrow_part, "line", code) for code in range(1, columns)]
        forwards.append(forward(1))
        forwards[1][:] = together(*forwards[1], widen_y, widen_x, *narrow_z)
        widen_y, widen_x, *narrow_z = forwards[1][7:]
        forwards[1] = forwards[1][:7]
        half = widen_line.shape[0] // 2
        corner_x, corner_y = (widen_y[:half], widen_x[half:])
        narrow_line = jnp.concatenate(narrow_z)
        back_pair = back_sent(grad_near, narrow_line, columns, sides)
        back_part = added(back_pair[: 4 * count], swap(back_pair[4 * count :], "side"))
        back_part, corner_x, corner_y = together(back_part, corner_x, corner_y)
        widen_xy, widen_yx = (swap(corner_x, "far"), swap(corner_y, "side"))
        pieces = [widen_line, widen_y, widen_x, widen_xy, widen_yx]
        pieces = pieces + [swap(piece, "core") for piece in pieces]
        near = [(line_codes, 0), (side_codes, 0), (line_codes, 2), (side_codes[:cut], 2), (side_codes[cut:], 2)]
        spans = tuple((codes, block * own_hidden) for codes, block in near) + tuple(
            (codes, (block + 1) * own_hidden) for codes, block in near
        )
    else:
        grad_pair = jnp.concatenate([grad_low, swap(grad_low, "core")])
        grad_group = jnp.concatenate([grad_pair, swap(grad_pair, "far")])
        narrow_t = lax.all_gather(narrow_part, dp_axes, axis=0, tiled=True)
        grad_all = lax.all_gather(grad_group, dp_axes, axis=0, tiled=True)
        grad_all = lax.dynamic_slice_in_dim(grad_all, group * own_width, own_width, 1)
        back_part = dot(grad_group, narrow_t).astype(bf16)
        forwards.append(forward(1))
    back_part = back_part.reshape(4, count, own_hidden)
    back_x = swap(back_part[2:], "far")
    back_core = swap(jnp.stack([back_part[1], back_x[1]]), "core")
    back_rows = jnp.concatenate([back_part[0], back_core[0], back_x[0], back_core[1]], axis=1)

    row_ends = [-(-share * (place + 1) // mixers) for place in range(groups)]
    row_starts = tuple(share * place // mixers for place in range(groups))
    part_rows = max(end - start for start, end in zip(row_starts, row_ends))
    queries_t = jnp.swapaxes(queries, 0, 1)
    if share % 16 != 0:
        offset = lax.rem(group * share, mixers)
        queries_t = lax.dynamic_update_slice(
            jnp.zeros((part_rows * mixers, asked), bf16), queries_t, (offset, jnp.int32(0))
        )

    def channel_chunk(chunk, second, left, before):
        first, last = chunks[chunk]
        number = last - first
        return channel(
            second.reshape(number * rows, features), keep, left.reshape(number * rows, rank),
            back_rows, bias_row, grad_low, width_maps, pieces, spans, layout, codes, share_shape, before, mixers,
            chunk, first, last, last == count,
        )

    def backward(chunk, grad, saved, adapters, hidden_sum, before):
        first, last = chunks[chunk]
        hidden, slope, _, normed, inverse = saved[:5]
        image_grad, *parts, sums, token_total, token_share = token_backward(
            images, keep, grad_rows[:, None, :], grad.reshape(last - first, rows, features), normed, inverse, hidden,
            slope, tokens, token_codes, norm_gain, norm_bias, adapters,
            hidden_sum, output_sum, before, row_starts, part_rows, columns,
            first, last,
        )
        return image_grad, parts, sums, token_total, token_share

    second_grad, chan_first, hidden_sum, adapters, shares_first = channel_chunk(
        0, forwards[0][2], forwards[0][6], None
    )
    if by_hand:
        narrow_y = swap(narrow_line, "side")
        second_grad, chan_first, hidden_sum, adapters, shares_first, narrow_y = together(
            second_grad, chan_first, hidden_sum, adapters, shares_first, narrow_y
        )
    image_grad_first, parts, sums, token_total, _ = backward(
        0, second_grad, forwards[0], adapters, hidden_sum, None
    )
    second, shares_first, *parts = together(forwards[1][2], shares_first, *parts)
    received_first = lax.all_to_all(parts[0], dp_axes, split_axis=0, concat_axis=0, tiled=True)

    second_grad, chan_second, hidden_sum, adapters, *shares = channel_chunk(
        1, second, forwards[1][6], (hidden_sum, shares_first)
    )
    second_grad, chan_second, hidden_sum, adapters, *shares, received_first = together(
        second_grad, chan_second, hidden_sum, adapters, *shares, received_first
    )
    share_core = swap(shares[1], "core")
    chan_pooled = jnp.concatenate([chan_first, chan_second]).astype(bf16).reshape(count, 4, own_hidden)
    chan_x = swap(chan_pooled[:, 2:], "far")
    image_grad, parts, sums, _, token_share = backward(
        1, second_grad, forwards[1], adapters, hidden_sum, (token_total, sums, image_grad_first)
    )
    image_grad, parts[0], sums, token_share, chan_x, share_core = together(
        image_grad, parts[0], sums, token_share, chan_x, share_core
    )
    received_second = lax.all_to_all(parts[0], dp_axes, split_axis=0, concat_axis=0, tiled=True)
    chan_core = swap(jnp.stack([chan_pooled[:, 1], chan_x[:, 1]]), "core")
    chan_group = jnp.concatenate([chan_pooled[:, 0], chan_core[0], chan_x[:, 0], chan_core[1]])

    own, far = (added(shares[0][0], share_core[0]), added(shares[0][1], share_core[1]))
    own_mixers, wide = token_share.shape[2:]
    lines = features // mixers
    if by_hand:
        far_x, line_x = (swap(far[1], "far"), swap(far[0], "far"))
        message = swap(jnp.concatenate([token_share[1].reshape(-1, wide), chan_group]), "side")
        image_grad = image_grad.reshape(patches, count, features)
        far_x, image_grad = together(far_x, image_grad)
        own_y = swap(added(own[1], far_x), "side")
        line = added(token_share[0], message[: -chan_group.shape[0]].reshape(token_share.shape[1:]))
        chan_pair = jnp.concatenate([chan_group, message[-chan_group.shape[0] :]])
        messages = [jnp.concatenate([line[code], chan_pair]) for code in range(1, columns)]
        received_second, *messages = together(received_second, *messages)
        messages = [swap(message, "line", code) for code, message in enumerate(messages, 1)]
        arrived = jnp.concatenate([received_first, received_second], axis=1)
        arrived = jnp.moveaxis(arrived, 2, 0).reshape(part_rows, groups * count, mixers)
        partial_scores = scores(arrived, queries_t)
        partial_scores, own_y, line_x, *messages = together(partial_scores, own_y, line_x, *messages)
        widen_line = (own[0].astype(f32) + line_x.astype(f32) + own_y.astype(f32)).astype(bf16)
        widen_sums = [swap(widen_line[code], "line", code) for code in range(1, columns)]
        image_grad = jnp.swapaxes(image_grad, 0, 1)
        total = line[0].astype(f32)
        for message in messages:
            total = total + message[:own_mixers].astype(f32)
        chan_all = jnp.concatenate([chan_pair] + [message[own_mixers:] for message in messages])
        total = total.astype(bf16)
        total = added(total, swap(total, "far"))
        token_grad, mixing_grad, gain_grad, shift_grad, patch_grad, hidden_grad, output_grad = unpack(
            total, swap(total, "core"), patches, mixers, features, hidden_size
        )
        mixing_grad, patch_grad, hidden_grad, output_grad = (
            row[0] for row in (mixing_grad, patch_grad, hidden_grad, output_grad)
        )
        narrowing_grad = narrow_sums(chan_all, pieces, own_width, count, layout).T
        widening_grad = widen_line[0].astype(f32)
        for widen_sum in widen_sums:
            widening_grad = widening_grad + widen_sum.astype(f32)
        narrow_pair = jnp.stack([narrow_line, narrow_y]).reshape(sides, columns, own_width, own_hidden)
        narrow_t = jnp.swapaxes(narrow_pair, 0, 1).reshape(features, own_hidden)
    else:
        narrowing_grad = None
        image_grad = jnp.swapaxes(image_grad.reshape(patches, count, features), 0, 1)
        arrived = jnp.concatenate([received_first, received_second], axis=1)
        arrived = jnp.moveaxis(arrived, 2, 0).reshape(part_rows, groups * count, mixers)
        partial_scores = scores(arrived, queries_t)
        own = added(own, jnp.concatenate([swap(far[:1], "far"), swap(far[1:], "far")]))
        widening_grad = lax.psum_scatter(own, dp_axes, scatter_dimension=0, tiled=True).astype(f32)
        chan_all = lax.all_gather(chan_group, dp_axes, axis=0, tiled=True)
        summed = jnp.swapaxes(token_share, 0, 1).reshape(groups, own_mixers, wide)
        summed = by_code(summed, group).astype(f32)
        total = lax.psum(lax.psum_scatter(summed, dp_axes, scatter_dimension=0, tiled=True)[0], ("far", "core"))
        half = wide // 3
        sums, more = lax.psum((sums, jnp.concatenate([hidden_sum, output_sum], axis=1)[0]), dp_axes + ("far", "core"))
        token_grad = jnp.stack([total[:, :patches], total[:, half : half + patches]])
        mixing_grad = sums[0]
        gain_grad = sums[1 : 1 + 2 * lines].reshape(2, features)
        shift_grad = sums[1 + 2 * lines : 1 + 4 * lines].reshape(2, features)
        patch_grad = sums[1 + 4 * lines, :patches]
        hidden_grad, output_grad = (more[:hidden_size], more[hidden_size : hidden_size + features])
    token_grad = jnp.swapaxes(token_grad, 1, 2)
    if narrowing_grad is None:
        narrowing_grad = dot_tn(grad_all, chan_all).T

    out_part = dot_nt(chan_group, narrow_t).reshape(4, count, features)
    out_pair = out_part[:2] + swap(out_part[2:], "far")
    chan_out = out_pair[0] + swap(out_pair[1], "core")
    if by_hand:
        chan_out = by_code(jnp.moveaxis(chan_out.reshape(count, groups, own_width), 1, 0), group)
        chan_out = jnp.moveaxis(chan_out, 0, 1).reshape(count, features)
    pooled_in = jnp.concatenate([forwards[0][5][:, 0], forwards[1][5][:, 0]])
    pooled = (pooled_in + chan_out) / kept_count + output_bias

    partial_scores = partial_scores.reshape(groups, count, asked)
    influence = jnp.sum(
        lax.all_to_all(partial_scores, dp_axes, split_axis=0, concat_axis=0, tiled=True), axis=0
    )
    return (
        pooled,
        image_grad,
        token_grad,
        gain_grad,
        shift_grad,
        mixing_grad,
        patch_grad,
        widening_grad,
        narrowing_grad,
        hidden_grad,
        output_grad,
        influence,
    )


def solution(mesh):
    groups = mesh.shape["dp"]
    models = mesh.shape["mp"]
    mesh = Mesh(mesh.devices.reshape(groups // 2, 2, models // 2, 2), ("line", "side", "far", "core"))
    dp = ("line", "side")
    mp = ("far", "core")
    every = dp + mp
    placed = (
        P(every, None, None),
        P(every, None),
        P(every, None),
        P(None, None, dp),
        P(),
        P(),
        P(),
        P(),
        P(dp, mp),
        P(mp, dp),
        P(),
        P(),
        P(),
        P(None, mp, None),
        P(None, dp),
    )
    return jax.shard_map(
        body,
        mesh=mesh,
        in_specs=placed,
        out_specs=(
            P(every, None),
            P(every, None, None),
            P(None, None, dp),
            P(),
            P(),
            P(),
            P(),
            P(dp, mp),
            P(mp, dp),
            P(),
            P(),
            P(every, None),
        ),
        check_vma=False,
    )
```

```python
import functools

import jax
import jax.numpy as jnp
from jax import lax
from jax.experimental import pallas as pl
from jax.experimental.pallas import tpu as pltpu
from jax.sharding import Mesh
from jax.sharding import PartitionSpec as P

norm_eps = 1e-06
bf16 = jnp.bfloat16
f32 = jnp.float32
vmem_cap = 58 * 1024 * 1024
dp_axes = ("line", "side")


def dot(left, right):
    return jnp.dot(left, right, preferred_element_type=f32)


def dot_nt(left, right):
    return lax.dot_general(left, right, (((1,), (1,)), ((), ())), preferred_element_type=f32)


def dot_tn(left, right):
    return lax.dot_general(left, right, (((0,), (0,)), ((), ())), preferred_element_type=f32)


def exact_tn(left, right):
    return lax.dot_general(
        left, right, (((0,), (0,)), ((), ())), precision=lax.Precision.HIGHEST, preferred_element_type=f32
    )


def gelu_pair(values):
    cumulative = 0.5 + 0.5 * lax.erf(values * 0.7071067811865476)
    density = jnp.exp2(values * values * -0.7213475204444817) * 0.3989422804014327
    return (values * cumulative, cumulative + values * density)


def normalize(values):
    average = jnp.mean(values, axis=-1, keepdims=True)
    centered = values - average
    spread = jnp.mean(centered * centered, axis=-1, keepdims=True)
    inverse = lax.rsqrt(spread + norm_eps)
    return (centered * inverse, inverse)


def norm_back(grad_norm, normed, inverse):
    first_mean = jnp.mean(grad_norm, axis=-1, keepdims=True)
    second_mean = jnp.mean(grad_norm * normed, axis=-1, keepdims=True)
    return inverse * (grad_norm - first_mean - normed * second_mean)


def whole(shape):
    return pl.BlockSpec(shape, lambda i: (0,) * len(shape))


def each(shape, first=0):
    return pl.BlockSpec((1,) + shape, lambda i: (i + first,) + (0,) * len(shape))


def struct(shape, dtype=f32):
    return jax.ShapeDtypeStruct(shape, dtype)


def place_of():
    return lax.axis_index("line") * lax.axis_size("side") + lax.axis_index("side")


def assemble_tokens(piece_refs, codes, token_ref):
    place = place_of()
    for piece_ref, own_codes in zip(piece_refs, codes):
        own = piece_ref.shape[2]
        for at, code in enumerate(own_codes):
            start = 0 if code is None else pl.multiple_of((place ^ code) * own, own)
            for which in range(2):
                token_ref[which, pl.ds(start, own)] = piece_ref[at, which]


def token_forward_kernel(
    codes, image_ref, keep_ref, gain_ref, shift_ref, column_ref, width_ref, *refs,
):
    piece_refs, refs = (refs[: len(codes)], refs[len(codes) :])
    hidden_ref, slope_ref, second_ref, normed_ref, inverse_ref, pooled_ref, left_ref, token_ref, padded_ref = refs
    mixers = token_ref.shape[1]
    patches = image_ref.shape[1]

    @pl.when(pl.program_id(0) == 0)
    def _():
        assemble_tokens(piece_refs, codes, token_ref)
        padded_ref[patches:] = jnp.zeros((padded_ref.shape[0] - patches, padded_ref.shape[1]), f32)

    padded_ref[:patches] = image_ref[0].astype(f32)
    inputs = padded_ref[...]
    keep = keep_ref[0]
    normed_one, _ = normalize(inputs)
    masked = ((normed_one * gain_ref[0:1] + shift_ref[0:1]) * keep).astype(bf16)
    mixed = dot(token_ref[0], masked) + column_ref[:mixers]
    hidden, slope = gelu_pair(mixed)
    hidden = hidden.astype(bf16)
    hidden_ref[0] = hidden
    slope_ref[0] = slope.astype(bf16)
    residual = inputs + dot_tn(token_ref[1], hidden) + column_ref[mixers:]
    pooled_ref[0] = jnp.sum(residual * keep, axis=0, keepdims=True)
    normed_two, inverse_two = normalize(residual)
    second = (normed_two * gain_ref[1:2] + shift_ref[1:2]).astype(bf16)
    second_ref[0] = second
    normed_ref[0] = normed_two.astype(bf16)
    inverse_ref[0] = inverse_two
    left_ref[0] = dot_nt(second, width_ref[0])


def token_forward(images, keep, tokens, codes, norm_gain, norm_bias, column, width_maps, first, last):
    count = last - first
    _, patches, features = images.shape
    rows = keep.shape[1]
    mixers = column.shape[0] - rows
    rank = width_maps.shape[1]
    return pl.pallas_call(
        functools.partial(token_forward_kernel, codes),
        grid=(count,),
        in_specs=[
            each((patches, features), first), each((rows, 1), first),
            whole((2, features)), whole((2, features)), whole((mixers + rows, 1)), whole((2, rank, features)),
        ]
        + [whole(piece.shape) for piece in tokens],
        out_specs=[
            each((mixers, features)), each((mixers, features)), each((rows, features)), each((rows, features)),
            each((rows, 1)), each((1, features)), each((rows, rank)),
        ],
        out_shape=[
            struct((count, mixers, features), bf16), struct((count, mixers, features), bf16),
            struct((count, rows, features), bf16), struct((count, rows, features), bf16),
            struct((count, rows, 1)), struct((count, 1, features)), struct((count, rows, rank)),
        ],
        scratch_shapes=[pltpu.VMEM((2, mixers, rows), bf16), pltpu.VMEM((rows, features), f32)],
        compiler_params=pltpu.CompilerParams(vmem_limit_bytes=vmem_cap),
        name="token_forward",
    )(images, keep, norm_gain, norm_bias, column, width_maps, *tokens)


def piece_copies(piece_refs, widen_ref, maps_ref, sems, spans, layout):
    depth, wide_rows, map_at, map_rows = layout
    copies = []
    place = place_of()
    for at, (piece_ref, (codes, column)) in enumerate(zip(piece_refs, spans)):
        cols = pl.ds(column, piece_ref.shape[1])
        for part, code in enumerate(codes):
            for which, (target, first, rows) in enumerate(((widen_ref, 0, wide_rows), (maps_ref, map_at, map_rows))):
                start = 0 if code is None else pl.multiple_of((place ^ code) * rows, rows)
                copy = pltpu.make_async_copy(
                    piece_ref.at[pl.ds(part * depth + first, rows)],
                    target.at[pl.ds(start, rows), cols],
                    sems.at[at, part, which],
                )
                copies.append((column, copy))
    return copies


def channel_kernel(
    spans, layout, codes, first, resumed, final,
    second_ref, keep_ref, left_ref, back_ref, bias_ref, rows_ref, width_ref, *refs,
):
    piece_refs, refs = (refs[: len(spans)], refs[len(spans) :])
    if resumed:
        sum_before_ref, before_ref, *refs = refs
    grad_ref, pooled_ref, sum_ref, adapter_ref, *refs = refs
    share_refs, refs = (refs[: 2 if final else 1], refs[2 if final else 1 :])
    widen_ref, maps_ref, total_ref, right_ref, out_ref, pair_ref, sems = refs
    step = pl.program_id(0)
    steps = pl.num_programs(0)
    count = pooled_ref.shape[0]
    total_rows, features = second_ref.shape
    rows = total_rows // count
    rank = left_ref.shape[1]
    own = bias_ref.shape[1] // 4
    model = lax.axis_index("far") * lax.axis_size("core") + lax.axis_index("core")
    second = second_ref[...]
    keep = keep_ref[...].reshape(total_rows, 1)
    copies = piece_copies(piece_refs, widen_ref, maps_ref, sems, spans, layout)

    @pl.when(step == 0)
    def _():
        for _, copy in copies:
            copy.start()
        for column, copy in copies:
            if column < 2 * own:
                copy.wait()
        if resumed:
            sum_ref[...] = sum_before_ref[...]
        else:
            sum_ref[...] = jnp.zeros_like(sum_ref)
        right_ref[...] = jnp.zeros_like(right_ref)
        out_ref[...] = jnp.zeros_like(out_ref)
        grad_ref[...] = jnp.zeros_like(grad_ref)

    @pl.when(step > 0)
    def _():
        for column, copy in copies:
            if column >= 2 * own:
                copy.wait()

    for half in range(2):
        cols = slice(half * own, (half + 1) * own)
        wide = pl.ds(pl.multiple_of((2 * step + half) * own, own), own)
        widen = widen_ref[:, wide]
        bias_at = pl.multiple_of((model ^ (2 * step + half)) * own, own)
        pre = dot(second, widen) + bias_ref[:, pl.ds(bias_at, own)]
        hidden, slope = gelu_pair(pre)
        hidden = (hidden.astype(bf16).astype(f32) * keep).reshape(count, rows, own)
        pooled_hidden = jnp.sum(hidden, axis=1)
        pooled_ref[:, cols] = pooled_hidden
        back = back_ref[first : first + count, cols].astype(f32)[:, None, :]
        pre_grad = (slope * keep).reshape(count, rows, own) * back
        pre_grad = pre_grad.reshape(total_rows, own).astype(bf16)
        sum_ref[:, pl.ds(bias_at, own)] += jnp.sum(pre_grad.astype(f32), axis=0, keepdims=True)
        grad_ref[...] += dot_nt(pre_grad, widen)
        right_ref[...] += dot_nt(pre_grad, maps_ref[:rank, wide])
        out_ref[...] += dot_nt(pooled_hidden.astype(bf16), maps_ref[rank:, wide])
        share = dot_tn(second, pre_grad)
        if resumed:
            share = share + before_ref[:, cols].astype(f32)
        if not final:
            share_refs[0][:, cols] = share.astype(bf16)
            continue
        total_ref[...] = share
        place = place_of()
        part_rows = share_refs[half].shape[-2]
        for index, code in codes:
            start = 0 if code is None else pl.multiple_of((place ^ code) * part_rows, part_rows)
            share_refs[half][(0, *index)] = total_ref[pl.ds(start, part_rows)].astype(bf16)

    @pl.when(step == steps - 1)
    def _():
        outer = dot_nt(rows_ref[first : first + count], width_ref[1])
        lines = adapter_ref.shape[2] // rank
        pair_ref[2 * rank :] = jnp.zeros((pair_ref.shape[0] - 2 * rank, rank), f32)
        for image in range(count):
            span = slice(image * rows, (image + 1) * rows)
            pair_ref[:rank] = exact_tn(left_ref[span], right_ref[span])
            pair_ref[rank : 2 * rank] = exact_tn(out_ref[image : image + 1], outer[image : image + 1])
            adapter_ref[image] = jnp.concatenate(
                [pair_ref[pl.ds(line, adapter_ref.shape[1], stride=lines)] for line in range(lines)], axis=1
            ).astype(bf16)


def channel(
    second, keep, left, back_rows, bias_row, grad_low, width_maps, pieces, spans, layout, codes, share_shape, before,
    mixers, chunk, first, last, final,
):
    count = last - first
    total_rows, features = second.shape
    hidden_size = bias_row.shape[1]
    rank = left.shape[1]
    held = back_rows.shape[0]
    lines = mixers // rank
    adapter_rows = -(-2 * rank // lines)
    once = pl.Buffered(1)
    resumed = before is not None
    anywhere = pl.BlockSpec(memory_space=pl.ANY)
    wide = hidden_size // 2

    def columns(rows):
        return pl.BlockSpec((rows, wide), lambda i: (0, i))

    if final:
        share_specs = [
            pl.BlockSpec((1, *share_shape), lambda i: (i,) + (0,) * len(share_shape)) for _ in range(2)
        ]
        share_out = [struct((2, *share_shape), bf16) for _ in range(2)]
    else:
        share_specs = [columns(features)]
        share_out = [struct((features, hidden_size), bf16)]
    return pl.pallas_call(
        functools.partial(channel_kernel, spans, layout, codes, first, resumed, final),
        grid=(2,),
        in_specs=[
            whole((total_rows, features)), pl.BlockSpec((count, total_rows // count, 1), lambda i: (chunk, 0, 0)),
            whole((total_rows, rank)), columns(held),
            whole((1, hidden_size)), whole((held, features)), whole((2, rank, features)),
        ]
        + [anywhere] * len(pieces)
        + ([whole((1, hidden_size)), columns(features)] if resumed else []),
        out_specs=[
            whole((total_rows, features)), columns(count), whole((1, hidden_size)), whole((count, adapter_rows, mixers)),
        ]
        + share_specs,
        out_shape=[
            struct((total_rows, features)), struct((count, hidden_size)), struct((1, hidden_size)),
            struct((count, adapter_rows, mixers), bf16),
        ]
        + share_out,
        scratch_shapes=[
            pltpu.VMEM((features, hidden_size), bf16),
            pltpu.VMEM((2 * rank, hidden_size), bf16),
            pltpu.VMEM((features, hidden_size // 4), f32),
            pltpu.VMEM((total_rows, rank), f32),
            pltpu.VMEM((count, rank), f32),
            pltpu.VMEM((adapter_rows * lines, rank), f32),
            pltpu.SemaphoreType.DMA((len(spans), max(len(span[0]) for span in spans), 2)),
        ],
        compiler_params=pltpu.CompilerParams(vmem_limit_bytes=vmem_cap),
        name="channel",
    )(
        second, keep, left, back_rows, bias_row, grad_low, width_maps, *pieces, *(before if resumed else [])
    )


def token_backward_kernel(
    codes, resumed, patches, row_starts,
    image_ref, keep_ref, row_ref, grad_ref, normed_ref, inverse_ref, hidden_ref, slope_ref,
    gain_ref, shift_ref, adapter_ref, hidden_sum_ref, output_sum_ref, *refs,
):
    piece_refs, refs = (refs[: len(codes)], refs[len(codes) :])
    if resumed:
        total_before_ref, sums_before_ref, _, *refs = refs
    image_grad_ref, parts_ref, sums_ref, total_ref, share_ref, vector_ref, token_ref, padded_ref = refs
    step = pl.program_id(0)
    steps = pl.num_programs(0)
    rows, features = padded_ref.shape
    mixers = hidden_ref.shape[1]
    keep = keep_ref[0]
    grad = grad_ref[0]

    @pl.when(step == 0)
    def _():
        if resumed:
            total_ref[...] = total_before_ref[...]
            sums_ref[...] = sums_before_ref[...]
        else:
            total_ref[...] = jnp.zeros_like(total_ref)
            sums_ref[...] = jnp.zeros_like(sums_ref)
        vector_ref[...] = jnp.zeros_like(vector_ref)
        padded_ref[patches:] = jnp.zeros((rows - patches, features), f32)
        assemble_tokens(piece_refs, codes, token_ref)

    normed_two = normed_ref[0].astype(f32)
    residual_grad = keep * row_ref[0] + norm_back(grad * gain_ref[1:2], normed_two, inverse_ref[0])
    gain_two = jnp.sum(grad * normed_two, axis=0, keepdims=True)
    shift_two = jnp.sum(grad, axis=0, keepdims=True)
    low = residual_grad.astype(bf16)
    outward_grad = dot_nt(low, hidden_ref[0])
    mixed_grad = (dot(token_ref[1], low) * slope_ref[0].astype(f32)).astype(bf16)
    ones = jnp.ones((8, features), bf16)
    mixing = dot_nt(ones, mixed_grad)[0:1]
    patch_sum = dot_nt(ones, low)[0:1]
    padded_ref[:patches] = image_ref[0].astype(f32)
    normed_one, inverse_one = normalize(padded_ref[...])
    masked = ((normed_one * gain_ref[0:1] + shift_ref[0:1]) * keep).astype(bf16)
    inward_grad = dot_nt(masked, mixed_grad)
    first_grad = dot_tn(token_ref[0], mixed_grad) * keep
    gain_one = jnp.sum(first_grad * normed_one, axis=0, keepdims=True)
    shift_one = jnp.sum(first_grad, axis=0, keepdims=True)
    image_grad = residual_grad + norm_back(first_grad * gain_ref[0:1], normed_one, inverse_one)
    image_grad_ref[...] = image_grad[:patches]
    lines = [mixing]
    for row in (gain_one, gain_two, shift_one, shift_two):
        for at in range(0, features, mixers):
            lines.append(row[:, at : at + mixers])
    small = jnp.concatenate(lines, axis=0)
    adapter_at = 2 * patches + len(lines)
    vector_ref[0:patches] = inward_grad[:patches]
    vector_ref[patches : 2 * patches] = outward_grad[:patches]
    vector_ref[2 * patches : adapter_at] = small
    vector_ref[adapter_at : adapter_at + adapter_ref.shape[1]] = adapter_ref[0].astype(f32)
    part_rows = parts_ref.shape[2]
    for place, start in enumerate(row_starts):
        parts_ref[place, 0] = vector_ref[start : start + part_rows].astype(bf16)
    total_ref[0] += inward_grad
    total_ref[1] += outward_grad
    sums_ref[0 : len(lines)] += small
    sums_ref[len(lines) : len(lines) + 1, 0:rows] += patch_sum

    @pl.when(step == steps - 1)
    def _():
        sides, columns, own, wide = share_ref.shape
        half = wide // 3
        line, side = (lax.axis_index("line"), lax.axis_index("side"))
        turned = [total_ref[which].T.astype(bf16) for which in range(2)]
        sums = [sums_ref[row : row + 1, at : at + 128] for row in range(sums_ref.shape[0]) for at in range(0, mixers, 128)]
        for ref in (hidden_sum_ref, output_sum_ref):
            sums += [ref[:, at : at + 128] for at in range(0, ref.shape[1], 128)]
        per_row = half // 128
        depth = len(sums) // per_row
        sums = [jnp.concatenate(sums[at::per_row], axis=0) for at in range(per_row)]
        sums = jnp.concatenate(sums, axis=1).astype(bf16)
        for place in range(sides * columns):
            at = ((place % sides) ^ side, (place // sides) ^ line)
            for which in range(2):
                part = turned[which][place * own : (place + 1) * own]
                share_ref[at[0], at[1], :, which * half : which * half + rows] = part
            if depth <= own:
                share_ref[at[0], at[1], 0:depth, 2 * half :] = sums


def token_backward(
    images, keep, grad_rows, grad, normed, inverse, hidden, slope, tokens, codes, norm_gain, norm_bias, adapters, hidden_sum,
    output_sum, before, row_starts, part_rows, columns, first, last,
):
    count = last - first
    _, patches, features = images.shape
    rows = keep.shape[1]
    mixers = hidden.shape[1]
    adapter_rows = adapters.shape[1]
    groups = len(row_starts)
    resumed = before is not None
    small = 2 + 4 * (features // mixers)
    held = -(-(row_starts[-1] + part_rows) // 8) * 8
    held = max(held, -(-(2 * patches + small + adapter_rows) // 8) * 8)
    wide = 3 * (-(-rows // 128) * 128)
    share_shape = (groups // columns, columns, mixers // groups, wide)
    return pl.pallas_call(
        functools.partial(token_backward_kernel, codes, resumed, patches, row_starts),
        grid=(count,),
        in_specs=[
            each((patches, features), first), each((rows, 1), first), each((1, features), first), each((rows, features)),
            each((rows, features)), each((rows, 1)), each((mixers, features)), each((mixers, features)),
            whole((2, features)), whole((2, features)), each((adapter_rows, mixers)), whole(hidden_sum.shape), whole(output_sum.shape),
        ]
        + [whole(piece.shape) for piece in tokens]
        + ([whole((2, rows, mixers)), whole((small, mixers)), pl.BlockSpec(memory_space=pl.ANY)] if resumed else []),
        out_specs=[
            pl.BlockSpec((patches, features), lambda i: (0, i + first)), pl.BlockSpec((groups, 1, part_rows, mixers), lambda i: (0, i, 0, 0)),
            whole((small, mixers)), whole((2, rows, mixers)), whole(share_shape),
        ],
        out_shape=[
            struct((patches, images.shape[0] * features)), struct((groups, count, part_rows, mixers), bf16),
            struct((small, mixers)), struct((2, rows, mixers)), struct(share_shape, bf16),
        ],
        scratch_shapes=[
            pltpu.VMEM((held, mixers), f32), pltpu.VMEM((2, mixers, rows), bf16), pltpu.VMEM((rows, features), f32),
        ],
        compiler_params=pltpu.CompilerParams(vmem_limit_bytes=vmem_cap),
        input_output_aliases={len(tokens) + 15: 0} if resumed else {},
        name="token_backward",
    )(
        images, keep, grad_rows, grad, normed, inverse, hidden, slope, norm_gain, norm_bias, adapters, hidden_sum, output_sum,
        *tokens, *(before if resumed else []),
    )


def back_kernel(columns, sides, grad_ref, narrow_ref, back_ref, turned_ref):
    turned_ref[...] = grad_ref[...].astype(f32).T
    own = narrow_ref.shape[0] // columns
    line, side = (lax.axis_index("line"), lax.axis_index("side"))
    total = None
    for code in range(columns):
        start = pl.multiple_of(((line ^ code) * sides + side) * own, own)
        part = dot_tn(turned_ref[pl.ds(start, own)].astype(bf16), narrow_ref[code * own : (code + 1) * own])
        total = part if total is None else total + part
    back_ref[...] = total.astype(bf16)


def back_sent(grads, narrow_line, columns, sides):
    return pl.pallas_call(
        functools.partial(back_kernel, columns, sides),
        out_shape=struct((grads.shape[0], narrow_line.shape[1]), bf16),
        scratch_shapes=[pltpu.VMEM((grads.shape[1], grads.shape[0]), f32)],
        compiler_params=pltpu.CompilerParams(vmem_limit_bytes=vmem_cap),
        name="back_sent",
    )(grads, narrow_line)


def narrow_kernel(count, first, chan_ref, *refs):
    piece_refs, (grad_ref, held_ref, grads_ref, product_ref, sems) = (refs[:-5], refs[-5:])
    blocks, columns, sides, held_rows = held_ref.shape[:4]
    depth = piece_refs[0].shape[0] // columns
    copies = []

    def fetch(piece, part, block, line, side):
        copies.append(
            pltpu.make_async_copy(
                piece_refs[piece].at[pl.ds(part * depth + first, held_rows)],
                held_ref.at[block, line, side],
                sems.at[block, line, side],
            )
        )

    cut = columns // 2
    for core in range(2):
        for line in range(columns):
            fetch(5 * core, line, core, line, 0)
            fetch(5 * core + 1, line, core, line, 1)
            fetch(5 * core + 2, line, 2 + core, line, 0)
            fetch(5 * core + 3 + line // cut, line % cut, 2 + core, line, 1)
    for copy in copies:
        copy.start()
    for copy in copies:
        copy.wait()
    at = 0
    for line in range(columns):
        for side in range(sides):
            for block in range(blocks):
                grads_ref[at : at + count] = held_ref[block, line, side, :count].astype(f32)
                at += count
    product_ref[...] = dot_tn(grads_ref[...].astype(bf16), chan_ref[...])
    own = grad_ref.shape[0]
    grad_ref[...] = product_ref[pl.ds(pl.multiple_of(place_of() * own, own), own)]


def narrow_sums(chan_all, pieces, own_width, count, layout):
    total, hidden = chan_all.shape
    depth, wide_rows, map_at, _ = layout
    columns = pieces[0].shape[0] // depth
    sides = total // (4 * columns * count)
    return pl.pallas_call(
        functools.partial(narrow_kernel, count, wide_rows),
        in_specs=[pl.BlockSpec(memory_space=pltpu.VMEM)] + [pl.BlockSpec(memory_space=pl.ANY)] * len(pieces),
        out_specs=pl.BlockSpec(memory_space=pltpu.VMEM),
        out_shape=struct((own_width, hidden)),
        scratch_shapes=[
            pltpu.VMEM((4, columns, sides, map_at - wide_rows, pieces[0].shape[1]), bf16),
            pltpu.VMEM((total, pieces[0].shape[1]), f32),
            pltpu.VMEM((own_width * columns * sides, hidden), f32),
            pltpu.SemaphoreType.DMA((4, columns, sides)),
        ],
        compiler_params=pltpu.CompilerParams(vmem_limit_bytes=vmem_cap),
        name="narrow_sums",
    )(chan_all, *pieces)


def join_kernel(even_ref, other_ref, *part_refs):
    step = pl.program_id(0)
    total = (even_ref[0, 0].astype(f32) + other_ref[0, 0].astype(f32)).astype(bf16)
    for at, part_ref in enumerate(part_refs):

        @pl.when(step == at)
        def _(part_ref=part_ref):
            part_ref[...] = total


def join(even, other):
    blocks, sides, *rest = even.shape
    spec = pl.BlockSpec((1, 1, *rest), lambda i: (i // sides, i % sides, 0, 0, 0))
    return pl.pallas_call(
        join_kernel,
        grid=(blocks * sides,),
        in_specs=[spec, spec],
        out_specs=[whole(tuple(rest)) for _ in range(blocks * sides)],
        out_shape=[struct(tuple(rest), bf16) for _ in range(blocks * sides)],
        compiler_params=pltpu.CompilerParams(vmem_limit_bytes=vmem_cap),
        name="join",
    )(even, other)


def lines_kernel(share_ref, message_ref, chan_ref, own_ref, *message_refs):
    own = share_ref.shape[1]
    held = chan_ref.shape[0]
    for line in range(share_ref.shape[0]):
        total = share_ref[line].astype(f32) + message_ref[line * own : (line + 1) * own].astype(f32)
        if line == 0:
            own_ref[...] = total
            continue
        message_refs[line - 1][:own] = total.astype(bf16)
        message_refs[line - 1][own : own + held] = chan_ref[...]
        message_refs[line - 1][own + held :] = message_ref[-held:]


def lines_out(share, message, chan_group):
    lines, own, wide = share.shape
    depth = own + 2 * chan_group.shape[0]
    return pl.pallas_call(
        lines_kernel,
        out_shape=[struct((own, wide))] + [struct((depth, wide), bf16) for _ in range(lines - 1)],
        compiler_params=pltpu.CompilerParams(vmem_limit_bytes=vmem_cap),
        name="lines_out",
    )(share, message, chan_group)


def spread_kernel(own_ref, line_ref, side_ref, mine_ref, *part_refs):
    for line in range(own_ref.shape[0]):
        total = own_ref[line].astype(f32) + line_ref[line].astype(f32) + side_ref[line].astype(f32)
        if line == 0:
            mine_ref[...] = total
        else:
            part_refs[line - 1][...] = total.astype(bf16)


def spread(own, line_x, own_y):
    lines, *rest = own.shape
    return pl.pallas_call(
        spread_kernel,
        out_shape=[struct(tuple(rest))] + [struct(tuple(rest), bf16) for _ in range(lines - 1)],
        compiler_params=pltpu.CompilerParams(vmem_limit_bytes=vmem_cap),
        name="spread",
    )(own, line_x, own_y)


def images_kernel(side_by_side_ref, image_ref):
    features = image_ref.shape[2]
    for image in range(image_ref.shape[1]):
        image_ref[:, image] = side_by_side_ref[:, image * features : (image + 1) * features]


def images_apart(side_by_side, count):
    patches, wide = side_by_side.shape
    step = 56
    return pl.pallas_call(
        images_kernel,
        grid=(-(-patches // step),),
        in_specs=[pl.BlockSpec((step, wide), lambda i: (i, 0))],
        out_specs=pl.BlockSpec((step, count, wide // count), lambda i: (i, 0, 0)),
        out_shape=struct((patches, count, wide // count)),
        compiler_params=pltpu.CompilerParams(vmem_limit_bytes=vmem_cap),
        name="images_apart",
    )(side_by_side)


def unpack_kernel(patches, own_ref, other_ref, token_ref, mixing_ref, gain_ref, shift_ref, patch_ref, hidden_ref, output_ref):
    half = own_ref.shape[1] // 3
    total = own_ref[...].astype(f32) + other_ref[...].astype(f32)
    for which in range(2):
        token_ref[which] = total[:, which * half : which * half + patches]
    pieces = []
    for row in range(own_ref.shape[0]):
        for at in range(2 * half, 3 * half, 128):
            pieces.append(total[row : row + 1, at : at + 128])
    mixers, features = (mixing_ref.shape[1], gain_ref.shape[1])
    at = 0

    def fill(ref, row, width, held):
        nonlocal at
        for first in range(0, held, 128):
            size = min(128, width - first)
            if size > 0:
                ref[row : row + 1, first : first + size] = pieces[at][:, :size]
            at += 1

    fill(mixing_ref, 0, mixers, mixers)
    for ref in (gain_ref, shift_ref):
        for row in range(2):
            fill(ref, row, features, features)
    fill(patch_ref, 0, patches, mixers)
    fill(hidden_ref, 0, hidden_ref.shape[1], hidden_ref.shape[1])
    fill(output_ref, 0, features, features)


def unpack(own, other, patches, mixers, features, hidden_size):
    return pl.pallas_call(
        functools.partial(unpack_kernel, patches),
        out_shape=[
            struct((2, own.shape[0], patches)), struct((1, mixers)), struct((2, features)), struct((2, features)),
            struct((1, patches)), struct((1, hidden_size)), struct((1, features)),
        ],
        name="unpack",
    )(own, other)


def score_kernel(parts, shifted, received_ref, query_hbm, score_ref, query_ref, sems):
    rows, _, width = received_ref.shape
    length = query_hbm.shape[0] // parts
    offset = 0
    if shifted:
        place = place_of()
        offset = pl.multiple_of(lax.rem(place * query_hbm.shape[0], width), 16)
        query_ref[0:width] = jnp.zeros((width, query_ref.shape[1]), bf16)
        last = rows * width - 2 * width
        query_ref[last:] = jnp.zeros((2 * width, query_ref.shape[1]), bf16)
    copies = [
        pltpu.make_async_copy(
            query_hbm.at[pl.ds(part * length, length)],
            query_ref.at[pl.ds(offset + part * length, length)],
            sems.at[part],
        )
        for part in range(parts)
    ]
    for copy in copies:
        copy.start()
    waited = 0
    total = None
    for row in range(rows):
        while waited < parts and waited * length < (row + 1) * width:
            copies[waited].wait()
            waited += 1
        part = dot(received_ref[row], query_ref[row * width : (row + 1) * width])
        total = part if total is None else total + part
    score_ref[...] = total


def scores(received, queries_t):
    rows, count, width = received.shape
    share, asked = queries_t.shape
    shifted = share != rows * width
    parts = 7 if share % 112 == 0 else 1
    return pl.pallas_call(
        functools.partial(score_kernel, parts, shifted),
        in_specs=[pl.BlockSpec(memory_space=pltpu.VMEM), pl.BlockSpec(memory_space=pl.ANY)],
        out_specs=pl.BlockSpec(memory_space=pltpu.VMEM),
        out_shape=struct((count, asked)),
        scratch_shapes=[pltpu.VMEM((rows * width, asked), bf16), pltpu.SemaphoreType.DMA((parts,))],
        compiler_params=pltpu.CompilerParams(vmem_limit_bytes=vmem_cap),
        name="scores",
    )(received, queries_t)


def swap(array, axis, code=1):
    devices = lax.axis_size(axis)
    return lax.ppermute(array, axis, [(place, place ^ code) for place in range(devices)])


def swap_both(array, line_code, side_code):
    columns, sides = (lax.axis_size("line"), lax.axis_size("side"))
    pairs = [
        (line * sides + side, (line ^ line_code) * sides + (side ^ side_code))
        for line in range(columns)
        for side in range(sides)
    ]
    return lax.ppermute(array, dp_axes, pairs)


def by_code(parts, place):
    step = 1
    while step < parts.shape[0]:
        pairs = parts.reshape(-1, 2, step, *parts.shape[1:])
        turned = jnp.concatenate([pairs[:, 1:], pairs[:, :1]], axis=1)
        parts = jnp.where((place & step) > 0, turned, pairs).reshape(parts.shape)
        step *= 2
    return parts


def together(*arrays):
    return lax.optimization_barrier(arrays)


def added(left, right):
    return (left.astype(f32) + right.astype(f32)).astype(bf16)


def body(
    images,
    kept_mask,
    pooled_grad,
    token_weights,
    norm_gain,
    norm_bias,
    mixing_bias,
    patch_bias,
    widening,
    narrowing,
    hidden_bias,
    output_bias,
    width_maps,
    hidden_maps,
    queries,
):
    count, patches, features = images.shape
    mixers = mixing_bias.shape[0]
    rank = width_maps.shape[2]
    hidden_size = hidden_bias.shape[0]
    columns = lax.axis_size("line")
    sides = lax.axis_size("side")
    groups = columns * sides
    group = lax.axis_index(dp_axes)
    share, asked = (queries.shape[1], queries.shape[0])
    own_hidden = widening.shape[1]
    own_width = narrowing.shape[1]
    by_hand = groups <= 8 and widening.shape[0] % 16 == 0
    chunks = [(0, count // 2), (count // 2, count)]
    rows = -(-patches // 8) * 8
    extra = rows - patches
    cut = columns // 2

    widen_part = widening.astype(bf16)
    token_part = jnp.pad(jnp.swapaxes(token_weights, 1, 2).astype(bf16), ((0, 0), (0, 0), (0, extra)))
    narrow_part = jnp.swapaxes(narrowing, 0, 1).astype(bf16)
    keep_f = kept_mask.astype(f32)
    kept_count = jnp.sum(keep_f, axis=1, keepdims=True)
    grad_rows = pooled_grad / kept_count
    grad_low = grad_rows.astype(bf16)
    maps_own = jnp.swapaxes(hidden_maps, 1, 2).reshape(2 * rank, own_hidden)
    width_maps = jnp.swapaxes(width_maps, 1, 2)
    keep = jnp.pad(keep_f, ((0, 0), (0, extra)))[:, :, None]
    column = jnp.concatenate([mixing_bias, jnp.pad(patch_bias, (0, extra))])[:, None]
    bias_row = hidden_bias[None, :]
    output_sum = jnp.sum(grad_low.astype(f32) * kept_count, axis=0, keepdims=True)
    if by_hand:
        map_rows = 2 * rank // groups
        maps_part = lax.dynamic_slice_in_dim(maps_own, group * map_rows, map_rows)
        grad_part = jnp.pad(grad_low, ((0, 16 - count), (0, 0)))
        piece = jnp.concatenate([widen_part, grad_part, maps_part])
        depth = piece.shape[0]
        layout = (depth, widen_part.shape[0], depth - map_rows, map_rows)
        token_line = jnp.stack([token_part] + [swap(token_part, "line", code) for code in range(1, columns)])
        tokens = [token_line, swap(token_line, "side")]
        widen_z = [piece] + [swap(piece, "line", code) for code in range(1, columns)]
        grad_pair = jnp.concatenate([grad_low, swap(grad_low, "core")])
        grad_group = jnp.concatenate([grad_pair, swap(grad_pair, "far")])
        grad_near = jnp.concatenate([grad_group, swap(grad_group, "side")])
        line_codes = tuple(sides * code for code in range(columns))
        side_codes = tuple(code ^ 1 for code in line_codes)
        token_codes = (line_codes, side_codes)
        codes = tuple(((side, at), sides * at ^ side) for side in range(sides) for at in range(columns))
        share_shape = (sides, columns, *widening.shape)
    else:
        tokens = [lax.all_gather(token_part, dp_axes, axis=1, tiled=True)[None]]
        token_codes = ((None,),)
        piece = jnp.concatenate([lax.all_gather(widen_part, dp_axes, axis=0, tiled=True), maps_own])
        layout = (piece.shape[0], features, features, 2 * rank)
        piece_x = swap(piece, "far")
        pieces = [piece, swap(piece, "core"), piece_x, swap(piece_x, "core")]
        spans = tuple(((None,), block * own_hidden) for block in range(4))
        codes = (((slice(None),), None),)
        share_shape = (features, own_hidden)

    def forward(chunk):
        out = token_forward(
            images, keep, tokens, token_codes, norm_gain, norm_bias, column, width_maps, *chunks[chunk]
        )
        return list(out)

    forwards = [forward(0)]
    if by_hand:
        narrow_part, widen_z[-1] = together(narrow_part, widen_z[-1])
        narrow_z = [narrow_part] + [swap(narrow_part, "line", code) for code in range(1, columns)]
        forwards[0][:] = together(*forwards[0], *widen_z, *narrow_z, grad_near, *tokens)
        widen_z, narrow_z = (forwards[0][7 : 7 + columns], forwards[0][7 + columns : 7 + 2 * columns])
        grad_near, *tokens = forwards[0][7 + 2 * columns :]
        forwards[0] = forwards[0][:7]
        widen_line = jnp.concatenate(widen_z)
        widen_y, widen_x = (swap(widen_line, "side"), swap(widen_line, "far"))
        narrow_line = jnp.concatenate(narrow_z)
        back_pair = back_sent(grad_near, narrow_line, columns, sides)
        back_y = swap(back_pair[4 * count :], "side")
        tokens[0], back_pair = together(tokens[0], back_pair)
        forwards.append(forward(1))
        forwards[1][:] = together(*forwards[1], widen_y, widen_x, back_y)
        widen_y, widen_x, back_y = forwards[1][7:]
        forwards[1] = forwards[1][:7]
        half = widen_line.shape[0] // 2
        corner_x, corner_y = (widen_y[:half], widen_x[half:])
        back_part = added(back_pair[: 4 * count], back_y)
        back_part, corner_x, corner_y = together(back_part, corner_x, corner_y)
        widen_xy, widen_yx = (swap(corner_x, "far"), swap(corner_y, "side"))
        pieces = [widen_line, widen_y, widen_x, widen_xy, widen_yx]
        pieces = pieces + [swap(piece, "core") for piece in pieces]
        near = [(line_codes, 0), (side_codes, 0), (line_codes, 2), (side_codes[:cut], 2), (side_codes[cut:], 2)]
        spans = tuple((codes, block * own_hidden) for codes, block in near) + tuple(
            (codes, (block + 1) * own_hidden) for codes, block in near
        )
    else:
        grad_pair = jnp.concatenate([grad_low, swap(grad_low, "core")])
        grad_group = jnp.concatenate([grad_pair, swap(grad_pair, "far")])
        narrow_t = lax.all_gather(narrow_part, dp_axes, axis=0, tiled=True)
        grad_all = lax.all_gather(grad_group, dp_axes, axis=0, tiled=True)
        grad_all = lax.dynamic_slice_in_dim(grad_all, group * own_width, own_width, 1)
        back_part = dot(grad_group, narrow_t).astype(bf16)
        forwards.append(forward(1))
    back_part = back_part.reshape(4, count, own_hidden)
    back_x = swap(back_part[2:], "far")
    back_core = swap(jnp.stack([back_part[1], back_x[1]]), "core")
    back_rows = jnp.concatenate([back_part[0], back_core[0], back_x[0], back_core[1]], axis=1)

    row_ends = [-(-share * (place + 1) // mixers) for place in range(groups)]
    row_starts = tuple(share * place // mixers for place in range(groups))
    part_rows = max(end - start for start, end in zip(row_starts, row_ends))
    queries_t = jnp.swapaxes(queries, 0, 1)
    if share % 16 != 0:
        offset = lax.rem(group * share, mixers)
        queries_t = lax.dynamic_update_slice(
            jnp.zeros((part_rows * mixers, asked), bf16), queries_t, (offset, jnp.int32(0))
        )

    def channel_chunk(chunk, second, left, before):
        first, last = chunks[chunk]
        number = last - first
        return channel(
            second.reshape(number * rows, features), keep, left.reshape(number * rows, rank),
            back_rows, bias_row, grad_low, width_maps, pieces, spans, layout, codes, share_shape, before, mixers,
            chunk, first, last, last == count,
        )

    def backward(chunk, grad, saved, adapters, hidden_sum, before):
        first, last = chunks[chunk]
        hidden, slope, _, normed, inverse = saved[:5]
        image_grad, *parts, sums, token_total, token_share = token_backward(
            images, keep, grad_rows[:, None, :], grad.reshape(last - first, rows, features), normed, inverse, hidden,
            slope, tokens, token_codes, norm_gain, norm_bias, adapters,
            hidden_sum, output_sum, before, row_starts, part_rows, columns,
            first, last,
        )
        return image_grad, parts, sums, token_total, token_share

    second_grad, chan_first, hidden_sum, adapters, shares_first = channel_chunk(
        0, forwards[0][2], forwards[0][6], None
    )
    if by_hand:
        narrow_y = swap(narrow_line, "side")
        second_grad, chan_first, hidden_sum, adapters, shares_first, narrow_y = together(
            second_grad, chan_first, hidden_sum, adapters, shares_first, narrow_y
        )
    image_grad_first, parts, sums, token_total, _ = backward(
        0, second_grad, forwards[0], adapters, hidden_sum, None
    )
    second, shares_first, *parts = together(forwards[1][2], shares_first, *parts)
    received_first = lax.all_to_all(parts[0], dp_axes, split_axis=0, concat_axis=0, tiled=True)

    second_grad, chan_second, hidden_sum, adapters, *shares = channel_chunk(
        1, second, forwards[1][6], (hidden_sum, shares_first)
    )
    second_grad, chan_second, hidden_sum, adapters, *shares, received_first = together(
        second_grad, chan_second, hidden_sum, adapters, *shares, received_first
    )
    share_core = swap(shares[1], "core")
    chan_pooled = jnp.concatenate([chan_first, chan_second]).astype(bf16).reshape(count, 4, own_hidden)
    chan_x = swap(chan_pooled[:, 2:], "far")
    image_grad, parts, sums, _, token_share = backward(
        1, second_grad, forwards[1], adapters, hidden_sum, (token_total, sums, image_grad_first)
    )
    image_grad, parts[0], sums, token_share, chan_x, share_core = together(
        image_grad, parts[0], sums, token_share, chan_x, share_core
    )
    received_second = lax.all_to_all(parts[0], dp_axes, split_axis=0, concat_axis=0, tiled=True)
    chan_core = swap(jnp.stack([chan_pooled[:, 1], chan_x[:, 1]]), "core")
    chan_group = jnp.concatenate([chan_pooled[:, 0], chan_core[0], chan_x[:, 0], chan_core[1]])

    own_mixers, wide = token_share.shape[2:]
    lines = features // mixers
    if by_hand:
        own_line, own_side, far_line, far_side = join(shares[0], share_core)
        message = jnp.concatenate([token_share[1].reshape(-1, wide), chan_group])
        own_line, own_side, far_line, far_side, message = together(own_line, own_side, far_line, far_side, message)
        far_x = swap(far_side, "far")
        message = swap(message, "side")
        image_grad = images_apart(image_grad, count)
        far_x, far_line, image_grad = together(far_x, far_line, image_grad)
        own_y = swap(added(own_side, far_x), "side")
        line_x = swap(far_line, "far")
        token_total, *messages = lines_out(token_share[0], message, chan_group)
        received_second, *messages = together(received_second, *messages)
        messages = [swap(part, "line", code) for code, part in enumerate(messages, 1)]
        arrived = jnp.concatenate([received_first, received_second], axis=1)
        arrived = jnp.moveaxis(arrived, 2, 0).reshape(part_rows, groups * count, mixers)
        partial_scores = scores(arrived, queries_t)
        partial_scores, own_y, line_x, chan_late, *messages = together(
            partial_scores, own_y, line_x, chan_group, *messages
        )
        widening_grad, *widen_sums = spread(own_line, line_x, own_y)
        widen_sums = [swap(part, "line", code) for code, part in enumerate(widen_sums, 1)]
        image_grad = jnp.swapaxes(image_grad, 0, 1)
        total = token_total
        for part in messages:
            total = total + part[:own_mixers].astype(f32)
        chan_pair = jnp.concatenate([chan_group, message[-chan_group.shape[0] :]])
        chan_all = jnp.concatenate([chan_pair] + [part[own_mixers:] for part in messages])
        total = total.astype(bf16)
        total = added(total, swap(total, "far"))
        token_grad, mixing_grad, gain_grad, shift_grad, patch_grad, hidden_grad, output_grad = unpack(
            total, swap(total, "core"), patches, mixers, features, hidden_size
        )
        mixing_grad, patch_grad, hidden_grad, output_grad = (
            row[0] for row in (mixing_grad, patch_grad, hidden_grad, output_grad)
        )
        narrowing_grad = narrow_sums(chan_all, pieces, own_width, count, layout).T
        for widen_sum in widen_sums:
            widening_grad = widening_grad + widen_sum.astype(f32)
        narrow_pair = jnp.stack([narrow_line, narrow_y]).reshape(sides, columns, own_width, own_hidden)
        narrow_t = jnp.swapaxes(narrow_pair, 0, 1).reshape(features, own_hidden)
    else:
        narrowing_grad, chan_late = (None, chan_group)
        image_grad = jnp.swapaxes(image_grad.reshape(patches, count, features), 0, 1)
        arrived = jnp.concatenate([received_first, received_second], axis=1)
        arrived = jnp.moveaxis(arrived, 2, 0).reshape(part_rows, groups * count, mixers)
        partial_scores = scores(arrived, queries_t)
        both = added(shares[0], share_core)
        own, far = (both[0], both[1])
        own = added(own, jnp.concatenate([swap(far[:1], "far"), swap(far[1:], "far")]))
        widening_grad = lax.psum_scatter(own, dp_axes, scatter_dimension=0, tiled=True).astype(f32)
        chan_all = lax.all_gather(chan_group, dp_axes, axis=0, tiled=True)
        summed = jnp.swapaxes(token_share, 0, 1).reshape(groups, own_mixers, wide)
        summed = by_code(summed, group).astype(f32)
        total = lax.psum(lax.psum_scatter(summed, dp_axes, scatter_dimension=0, tiled=True)[0], ("far", "core"))
        half = wide // 3
        sums, more = lax.psum((sums, jnp.concatenate([hidden_sum, output_sum], axis=1)[0]), dp_axes + ("far", "core"))
        token_grad = jnp.stack([total[:, :patches], total[:, half : half + patches]])
        mixing_grad = sums[0]
        gain_grad = sums[1 : 1 + 2 * lines].reshape(2, features)
        shift_grad = sums[1 + 2 * lines : 1 + 4 * lines].reshape(2, features)
        patch_grad = sums[1 + 4 * lines, :patches]
        hidden_grad, output_grad = (more[:hidden_size], more[hidden_size : hidden_size + features])
    token_grad = jnp.swapaxes(token_grad, 1, 2)
    if narrowing_grad is None:
        narrowing_grad = dot_tn(grad_all, chan_all).T

    out_part = dot_nt(chan_late, narrow_t).reshape(4, count, features)
    out_pair = out_part[:2] + swap(out_part[2:], "far")
    chan_out = out_pair[0] + swap(out_pair[1], "core")
    if by_hand:
        chan_out = by_code(jnp.moveaxis(chan_out.reshape(count, groups, own_width), 1, 0), group)
        chan_out = jnp.moveaxis(chan_out, 0, 1).reshape(count, features)
    pooled_in = jnp.concatenate([forwards[0][5][:, 0], forwards[1][5][:, 0]])
    pooled = (pooled_in + chan_out) / kept_count + output_bias

    partial_scores = partial_scores.reshape(groups, count, asked)
    influence = jnp.sum(
        lax.all_to_all(partial_scores, dp_axes, split_axis=0, concat_axis=0, tiled=True), axis=0
    )
    return (
        pooled,
        image_grad,
        token_grad,
        gain_grad,
        shift_grad,
        mixing_grad,
        patch_grad,
        widening_grad,
        narrowing_grad,
        hidden_grad,
        output_grad,
        influence,
    )


def solution(mesh):
    groups = mesh.shape["dp"]
    models = mesh.shape["mp"]
    mesh = Mesh(mesh.devices.reshape(groups // 2, 2, models // 2, 2), ("line", "side", "far", "core"))
    dp = ("line", "side")
    mp = ("far", "core")
    every = dp + mp
    placed = (
        P(every, None, None),
        P(every, None),
        P(every, None),
        P(None, None, dp),
        P(),
        P(),
        P(),
        P(),
        P(dp, mp),
        P(mp, dp),
        P(),
        P(),
        P(),
        P(None, mp, None),
        P(None, dp),
    )
    return jax.shard_map(
        body,
        mesh=mesh,
        in_specs=placed,
        out_specs=(
            P(every, None),
            P(every, None, None),
            P(None, None, dp),
            P(),
            P(),
            P(),
            P(),
            P(dp, mp),
            P(mp, dp),
            P(),
            P(),
            P(every, None),
        ),
        check_vma=False,
    )
```

```python
import functools

import jax
import jax.numpy as jnp
from jax import lax
from jax.experimental import pallas as pl
from jax.experimental.pallas import tpu as pltpu
from jax.sharding import Mesh
from jax.sharding import PartitionSpec as P

norm_eps = 1e-06
bf16 = jnp.bfloat16
f32 = jnp.float32
vmem_cap = 58 * 1024 * 1024
dp_axes = ("line", "side")


def dot(left, right):
    return jnp.dot(left, right, preferred_element_type=f32)


def dot_nt(left, right):
    return lax.dot_general(left, right, (((1,), (1,)), ((), ())), preferred_element_type=f32)


def dot_tn(left, right):
    return lax.dot_general(left, right, (((0,), (0,)), ((), ())), preferred_element_type=f32)


def exact_tn(left, right):
    return lax.dot_general(
        left, right, (((0,), (0,)), ((), ())), precision=lax.Precision.HIGHEST, preferred_element_type=f32
    )


def gelu_pair(values):
    cumulative = 0.5 + 0.5 * lax.erf(values * 0.7071067811865476)
    density = jnp.exp2(values * values * -0.7213475204444817) * 0.3989422804014327
    return (values * cumulative, cumulative + values * density)


def normalize(values):
    average = jnp.mean(values, axis=-1, keepdims=True)
    centered = values - average
    spread = jnp.mean(centered * centered, axis=-1, keepdims=True)
    inverse = lax.rsqrt(spread + norm_eps)
    return (centered * inverse, inverse)


def norm_back(grad_norm, normed, inverse):
    first_mean = jnp.mean(grad_norm, axis=-1, keepdims=True)
    second_mean = jnp.mean(grad_norm * normed, axis=-1, keepdims=True)
    return inverse * (grad_norm - first_mean - normed * second_mean)


def whole(shape):
    return pl.BlockSpec(shape, lambda i: (0,) * len(shape))


def each(shape, first=0):
    return pl.BlockSpec((1,) + shape, lambda i: (i + first,) + (0,) * len(shape))


def struct(shape, dtype=f32):
    return jax.ShapeDtypeStruct(shape, dtype)


def place_of():
    return lax.axis_index("line") * lax.axis_size("side") + lax.axis_index("side")


def assemble_tokens(piece_refs, codes, token_ref):
    place = place_of()
    for piece_ref, own_codes in zip(piece_refs, codes):
        own = piece_ref.shape[2]
        for at, code in enumerate(own_codes):
            start = 0 if code is None else pl.multiple_of((place ^ code) * own, own)
            for which in range(2):
                token_ref[which, pl.ds(start, own)] = piece_ref[at, which]


def token_forward_kernel(
    codes, image_ref, keep_ref, gain_ref, shift_ref, column_ref, width_ref, *refs,
):
    piece_refs, refs = (refs[: len(codes)], refs[len(codes) :])
    hidden_ref, slope_ref, second_ref, normed_ref, inverse_ref, pooled_ref, left_ref, token_ref, padded_ref = refs
    mixers = token_ref.shape[1]
    patches = image_ref.shape[1]

    @pl.when(pl.program_id(0) == 0)
    def _():
        assemble_tokens(piece_refs, codes, token_ref)
        padded_ref[patches:] = jnp.zeros((padded_ref.shape[0] - patches, padded_ref.shape[1]), f32)

    padded_ref[:patches] = image_ref[0].astype(f32)
    inputs = padded_ref[...]
    keep = keep_ref[0]
    normed_one, _ = normalize(inputs)
    masked = ((normed_one * gain_ref[0:1] + shift_ref[0:1]) * keep).astype(bf16)
    mixed = dot(token_ref[0], masked) + column_ref[:mixers]
    hidden, slope = gelu_pair(mixed)
    hidden = hidden.astype(bf16)
    hidden_ref[0] = hidden
    slope_ref[0] = slope.astype(bf16)
    residual = inputs + dot_tn(token_ref[1], hidden) + column_ref[mixers:]
    pooled_ref[0] = jnp.sum(residual * keep, axis=0, keepdims=True)
    normed_two, inverse_two = normalize(residual)
    second = (normed_two * gain_ref[1:2] + shift_ref[1:2]).astype(bf16)
    second_ref[0] = second
    normed_ref[0] = normed_two.astype(bf16)
    inverse_ref[0] = inverse_two
    left_ref[0] = dot_nt(second, width_ref[0])


def token_forward(images, keep, tokens, codes, norm_gain, norm_bias, column, width_maps, first, last):
    count = last - first
    _, patches, features = images.shape
    rows = keep.shape[1]
    mixers = column.shape[0] - rows
    rank = width_maps.shape[1]
    return pl.pallas_call(
        functools.partial(token_forward_kernel, codes),
        grid=(count,),
        in_specs=[
            each((patches, features), first), each((rows, 1), first),
            whole((2, features)), whole((2, features)), whole((mixers + rows, 1)), whole((2, rank, features)),
        ]
        + [whole(piece.shape) for piece in tokens],
        out_specs=[
            each((mixers, features)), each((mixers, features)), each((rows, features)), each((rows, features)),
            each((rows, 1)), each((1, features)), each((rows, rank)),
        ],
        out_shape=[
            struct((count, mixers, features), bf16), struct((count, mixers, features), bf16),
            struct((count, rows, features), bf16), struct((count, rows, features), bf16),
            struct((count, rows, 1)), struct((count, 1, features)), struct((count, rows, rank)),
        ],
        scratch_shapes=[pltpu.VMEM((2, mixers, rows), bf16), pltpu.VMEM((rows, features), f32)],
        compiler_params=pltpu.CompilerParams(vmem_limit_bytes=vmem_cap),
        name="token_forward",
    )(images, keep, norm_gain, norm_bias, column, width_maps, *tokens)


def piece_copies(piece_refs, widen_ref, maps_ref, sems, spans, layout):
    depth, wide_rows, map_at, map_rows = layout
    copies = []
    place = place_of()
    for at, (piece_ref, (codes, column)) in enumerate(zip(piece_refs, spans)):
        cols = pl.ds(column, piece_ref.shape[1])
        for part, code in enumerate(codes):
            for which, (target, first, rows) in enumerate(((widen_ref, 0, wide_rows), (maps_ref, map_at, map_rows))):
                start = 0 if code is None else pl.multiple_of((place ^ code) * rows, rows)
                copy = pltpu.make_async_copy(
                    piece_ref.at[pl.ds(part * depth + first, rows)],
                    target.at[pl.ds(start, rows), cols],
                    sems.at[at, part, which],
                )
                copies.append((column, copy))
    return copies


def channel_kernel(
    spans, layout, codes, first, resumed, final,
    second_ref, keep_ref, left_ref, back_ref, bias_ref, rows_ref, width_ref, *refs,
):
    if resumed:
        widen_ref, maps_ref, sum_before_ref, before_ref, *refs = refs
    else:
        piece_refs, refs = (refs[: len(spans)], refs[len(spans) :])
    grad_ref, pooled_ref, sum_ref, adapter_ref, *refs = refs
    share_refs, refs = (refs[: 2 if final else 1], refs[2 if final else 1 :])
    if resumed:
        total_ref, right_ref, out_ref, pair_ref = refs
    else:
        widen_out, maps_out, widen_ref, maps_ref, total_ref, right_ref, out_ref, pair_ref, sems, out_sems = refs
    step = pl.program_id(0)
    steps = pl.num_programs(0)
    count = pooled_ref.shape[0]
    total_rows, features = second_ref.shape
    rows = total_rows // count
    rank = left_ref.shape[1]
    own = bias_ref.shape[1] // 4
    model = lax.axis_index("far") * lax.axis_size("core") + lax.axis_index("core")
    second = second_ref[...]
    keep = keep_ref[...].reshape(total_rows, 1)
    if not resumed:
        copies = piece_copies(piece_refs, widen_ref, maps_ref, sems, spans, layout)
        kept = [
            pltpu.make_async_copy(widen_ref, widen_out, out_sems.at[0]),
            pltpu.make_async_copy(maps_ref, maps_out, out_sems.at[1]),
        ]

    @pl.when(step == 0)
    def _():
        if resumed:
            sum_ref[...] = sum_before_ref[...]
        else:
            for _, copy in copies:
                copy.start()
            for column, copy in copies:
                if column < 2 * own:
                    copy.wait()
            sum_ref[...] = jnp.zeros_like(sum_ref)
        right_ref[...] = jnp.zeros_like(right_ref)
        out_ref[...] = jnp.zeros_like(out_ref)
        grad_ref[...] = jnp.zeros_like(grad_ref)

    if not resumed:

        @pl.when(step > 0)
        def _():
            for column, copy in copies:
                if column >= 2 * own:
                    copy.wait()
            for copy in kept:
                copy.start()

    for half in range(2):
        cols = slice(half * own, (half + 1) * own)
        wide = cols if resumed else pl.ds(pl.multiple_of((2 * step + half) * own, own), own)
        widen = widen_ref[:, wide]
        bias_at = pl.multiple_of((model ^ (2 * step + half)) * own, own)
        pre = dot(second, widen) + bias_ref[:, pl.ds(bias_at, own)]
        hidden, slope = gelu_pair(pre)
        hidden = (hidden.astype(bf16).astype(f32) * keep).reshape(count, rows, own)
        pooled_hidden = jnp.sum(hidden, axis=1)
        pooled_ref[:, cols] = pooled_hidden
        back = back_ref[first : first + count, cols].astype(f32)[:, None, :]
        pre_grad = (slope * keep).reshape(count, rows, own) * back
        pre_grad = pre_grad.reshape(total_rows, own).astype(bf16)
        sum_ref[:, pl.ds(bias_at, own)] += jnp.sum(pre_grad.astype(f32), axis=0, keepdims=True)
        grad_ref[...] += dot_nt(pre_grad, widen)
        right_ref[...] += dot_nt(pre_grad, maps_ref[:rank, wide])
        out_ref[...] += dot_nt(pooled_hidden.astype(bf16), maps_ref[rank:, wide])
        share = dot_tn(second, pre_grad)
        if resumed:
            share = share + before_ref[:, cols].astype(f32)
        if not final:
            share_refs[0][:, cols] = share.astype(bf16)
            continue
        total_ref[...] = share
        place = place_of()
        part_rows = share_refs[half].shape[-2]
        for index, code in codes:
            start = 0 if code is None else pl.multiple_of((place ^ code) * part_rows, part_rows)
            share_refs[half][(0, *index)] = total_ref[pl.ds(start, part_rows)].astype(bf16)

    @pl.when(step == steps - 1)
    def _():
        if not resumed:
            for copy in kept:
                copy.wait()
        outer = dot_nt(rows_ref[first : first + count], width_ref[1])
        lines = adapter_ref.shape[2] // rank
        pair_ref[2 * rank :] = jnp.zeros((pair_ref.shape[0] - 2 * rank, rank), f32)
        for image in range(count):
            span = slice(image * rows, (image + 1) * rows)
            pair_ref[:rank] = exact_tn(left_ref[span], right_ref[span])
            pair_ref[rank : 2 * rank] = exact_tn(out_ref[image : image + 1], outer[image : image + 1])
            adapter_ref[image] = jnp.concatenate(
                [pair_ref[pl.ds(line, adapter_ref.shape[1], stride=lines)] for line in range(lines)], axis=1
            ).astype(bf16)


def channel(
    second, keep, left, back_rows, bias_row, grad_low, width_maps, pieces, spans, layout, codes, share_shape, before,
    mixers, chunk, first, last, final,
):
    count = last - first
    total_rows, features = second.shape
    hidden_size = bias_row.shape[1]
    rank = left.shape[1]
    held = back_rows.shape[0]
    lines = mixers // rank
    adapter_rows = -(-2 * rank // lines)
    once = pl.Buffered(1)
    resumed = before is not None
    anywhere = pl.BlockSpec(memory_space=pl.ANY)
    wide = hidden_size // 2

    def columns(rows):
        return pl.BlockSpec((rows, wide), lambda i: (0, i))

    if final:
        share_specs = [
            pl.BlockSpec((1, *share_shape), lambda i: (i,) + (0,) * len(share_shape)) for _ in range(2)
        ]
        share_out = [struct((2, *share_shape), bf16) for _ in range(2)]
    else:
        share_specs = [columns(features)]
        share_out = [struct((features, hidden_size), bf16)]
    scratch = [
        pltpu.VMEM((features, hidden_size // 4), f32),
        pltpu.VMEM((total_rows, rank), f32),
        pltpu.VMEM((count, rank), f32),
        pltpu.VMEM((adapter_rows * lines, rank), f32),
    ]
    if resumed:
        matrix_specs = [columns(features), columns(2 * rank), whole((1, hidden_size)), columns(features)]
        matrices = before
    else:
        matrix_specs = [anywhere] * len(pieces)
        matrices = pieces
        share_specs = share_specs + [anywhere, anywhere]
        share_out = share_out + [struct((features, hidden_size), bf16), struct((2 * rank, hidden_size), bf16)]
        scratch = [
            pltpu.VMEM((features, hidden_size), bf16), pltpu.VMEM((2 * rank, hidden_size), bf16), *scratch,
            pltpu.SemaphoreType.DMA((len(spans), max(len(span[0]) for span in spans), 2)),
            pltpu.SemaphoreType.DMA((2,)),
        ]
    return pl.pallas_call(
        functools.partial(channel_kernel, spans, layout, codes, first, resumed, final),
        grid=(2,),
        in_specs=[
            whole((total_rows, features)), pl.BlockSpec((count, total_rows // count, 1), lambda i: (chunk, 0, 0)),
            whole((total_rows, rank)), columns(held),
            whole((1, hidden_size)), whole((held, features)), whole((2, rank, features)),
        ]
        + matrix_specs,
        out_specs=[
            whole((total_rows, features)), columns(count), whole((1, hidden_size)), whole((count, adapter_rows, mixers)),
        ]
        + share_specs,
        out_shape=[
            struct((total_rows, features)), struct((count, hidden_size)), struct((1, hidden_size)),
            struct((count, adapter_rows, mixers), bf16),
        ]
        + share_out,
        scratch_shapes=scratch,
        compiler_params=pltpu.CompilerParams(vmem_limit_bytes=vmem_cap),
        name="channel",
    )(
        second, keep, left, back_rows, bias_row, grad_low, width_maps, *matrices
    )


def token_backward_kernel(
    codes, resumed, patches, row_starts,
    image_ref, keep_ref, row_ref, grad_ref, normed_ref, inverse_ref, hidden_ref, slope_ref,
    gain_ref, shift_ref, adapter_ref, hidden_sum_ref, output_sum_ref, *refs,
):
    piece_refs, refs = (refs[: len(codes)], refs[len(codes) :])
    if resumed:
        total_before_ref, sums_before_ref, _, *refs = refs
    image_grad_ref, parts_ref, sums_ref, total_ref, share_ref, vector_ref, token_ref, padded_ref = refs
    step = pl.program_id(0)
    steps = pl.num_programs(0)
    rows, features = padded_ref.shape
    mixers = hidden_ref.shape[1]
    keep = keep_ref[0]
    grad = grad_ref[0]

    @pl.when(step == 0)
    def _():
        if resumed:
            total_ref[...] = total_before_ref[...]
            sums_ref[...] = sums_before_ref[...]
        else:
            total_ref[...] = jnp.zeros_like(total_ref)
            sums_ref[...] = jnp.zeros_like(sums_ref)
        vector_ref[...] = jnp.zeros_like(vector_ref)
        padded_ref[patches:] = jnp.zeros((rows - patches, features), f32)
        assemble_tokens(piece_refs, codes, token_ref)

    normed_two = normed_ref[0].astype(f32)
    residual_grad = keep * row_ref[0] + norm_back(grad * gain_ref[1:2], normed_two, inverse_ref[0])
    gain_two = jnp.sum(grad * normed_two, axis=0, keepdims=True)
    shift_two = jnp.sum(grad, axis=0, keepdims=True)
    low = residual_grad.astype(bf16)
    outward_grad = dot_nt(low, hidden_ref[0])
    mixed_grad = (dot(token_ref[1], low) * slope_ref[0].astype(f32)).astype(bf16)
    ones = jnp.ones((8, features), bf16)
    mixing = dot_nt(ones, mixed_grad)[0:1]
    patch_sum = dot_nt(ones, low)[0:1]
    padded_ref[:patches] = image_ref[0].astype(f32)
    normed_one, inverse_one = normalize(padded_ref[...])
    masked = ((normed_one * gain_ref[0:1] + shift_ref[0:1]) * keep).astype(bf16)
    inward_grad = dot_nt(masked, mixed_grad)
    first_grad = dot_tn(token_ref[0], mixed_grad) * keep
    gain_one = jnp.sum(first_grad * normed_one, axis=0, keepdims=True)
    shift_one = jnp.sum(first_grad, axis=0, keepdims=True)
    image_grad = residual_grad + norm_back(first_grad * gain_ref[0:1], normed_one, inverse_one)
    image_grad_ref[...] = image_grad[:patches]
    lines = [mixing]
    for row in (gain_one, gain_two, shift_one, shift_two):
        for at in range(0, features, mixers):
            lines.append(row[:, at : at + mixers])
    small = jnp.concatenate(lines, axis=0)
    adapter_at = 2 * patches + len(lines)
    vector_ref[0:patches] = inward_grad[:patches]
    vector_ref[patches : 2 * patches] = outward_grad[:patches]
    vector_ref[2 * patches : adapter_at] = small
    vector_ref[adapter_at : adapter_at + adapter_ref.shape[1]] = adapter_ref[0].astype(f32)
    part_rows = parts_ref.shape[2]
    for place, start in enumerate(row_starts):
        parts_ref[place, 0] = vector_ref[start : start + part_rows].astype(bf16)
    total_ref[0] += inward_grad
    total_ref[1] += outward_grad
    sums_ref[0 : len(lines)] += small
    sums_ref[len(lines) : len(lines) + 1, 0:rows] += patch_sum

    @pl.when(step == steps - 1)
    def _():
        sides, columns, own, wide = share_ref.shape
        half = wide // 3
        line, side = (lax.axis_index("line"), lax.axis_index("side"))
        turned = [total_ref[which].T.astype(bf16) for which in range(2)]
        sums = [sums_ref[row : row + 1, at : at + 128] for row in range(sums_ref.shape[0]) for at in range(0, mixers, 128)]
        for ref in (hidden_sum_ref, output_sum_ref):
            sums += [ref[:, at : at + 128] for at in range(0, ref.shape[1], 128)]
        per_row = half // 128
        depth = len(sums) // per_row
        sums = [jnp.concatenate(sums[at::per_row], axis=0) for at in range(per_row)]
        sums = jnp.concatenate(sums, axis=1).astype(bf16)
        for place in range(sides * columns):
            at = ((place % sides) ^ side, (place // sides) ^ line)
            for which in range(2):
                part = turned[which][place * own : (place + 1) * own]
                share_ref[at[0], at[1], :, which * half : which * half + rows] = part
            if depth <= own:
                share_ref[at[0], at[1], 0:depth, 2 * half :] = sums


def token_backward(
    images, keep, grad_rows, grad, normed, inverse, hidden, slope, tokens, codes, norm_gain, norm_bias, adapters, hidden_sum,
    output_sum, before, row_starts, part_rows, columns, first, last,
):
    count = last - first
    _, patches, features = images.shape
    rows = keep.shape[1]
    mixers = hidden.shape[1]
    adapter_rows = adapters.shape[1]
    groups = len(row_starts)
    resumed = before is not None
    small = 2 + 4 * (features // mixers)
    held = -(-(row_starts[-1] + part_rows) // 8) * 8
    held = max(held, -(-(2 * patches + small + adapter_rows) // 8) * 8)
    wide = 3 * (-(-rows // 128) * 128)
    share_shape = (groups // columns, columns, mixers // groups, wide)
    return pl.pallas_call(
        functools.partial(token_backward_kernel, codes, resumed, patches, row_starts),
        grid=(count,),
        in_specs=[
            each((patches, features), first), each((rows, 1), first), each((1, features), first), each((rows, features)),
            each((rows, features)), each((rows, 1)), each((mixers, features)), each((mixers, features)),
            whole((2, features)), whole((2, features)), each((adapter_rows, mixers)), whole(hidden_sum.shape), whole(output_sum.shape),
        ]
        + [whole(piece.shape) for piece in tokens]
        + ([whole((2, rows, mixers)), whole((small, mixers)), pl.BlockSpec(memory_space=pl.ANY)] if resumed else []),
        out_specs=[
            pl.BlockSpec((patches, features), lambda i: (0, i + first)), pl.BlockSpec((groups, 1, part_rows, mixers), lambda i: (0, i, 0, 0)),
            whole((small, mixers)), whole((2, rows, mixers)), whole(share_shape),
        ],
        out_shape=[
            struct((patches, images.shape[0] * features)), struct((groups, count, part_rows, mixers), bf16),
            struct((small, mixers)), struct((2, rows, mixers)), struct(share_shape, bf16),
        ],
        scratch_shapes=[
            pltpu.VMEM((held, mixers), f32), pltpu.VMEM((2, mixers, rows), bf16), pltpu.VMEM((rows, features), f32),
        ],
        compiler_params=pltpu.CompilerParams(vmem_limit_bytes=vmem_cap),
        input_output_aliases={len(tokens) + 15: 0} if resumed else {},
        name="token_backward",
    )(
        images, keep, grad_rows, grad, normed, inverse, hidden, slope, norm_gain, norm_bias, adapters, hidden_sum, output_sum,
        *tokens, *(before if resumed else []),
    )


def back_kernel(own, columns, sides, grad_ref, narrow_ref, back_ref, sent_ref, turned_ref):
    turned_ref[...] = grad_ref[...].astype(f32).T
    depth = narrow_ref.shape[0] // columns
    line, side = (lax.axis_index("line"), lax.axis_index("side"))
    total = None
    for code in range(columns):
        start = pl.multiple_of(((line ^ code) * sides + side) * own, own)
        part = dot_tn(turned_ref[pl.ds(start, own)].astype(bf16), narrow_ref[code * depth : code * depth + own])
        total = part if total is None else total + part
    half = total.shape[0] // 2
    back_ref[...] = total[:half]
    sent_ref[...] = total[half:].astype(bf16)


def back_sent(grads, narrow_line, own, columns, sides):
    return pl.pallas_call(
        functools.partial(back_kernel, own, columns, sides),
        out_shape=[
            struct((grads.shape[0] // 2, narrow_line.shape[1])), struct((grads.shape[0] // 2, narrow_line.shape[1]), bf16),
        ],
        scratch_shapes=[pltpu.VMEM((grads.shape[1], grads.shape[0]), f32)],
        compiler_params=pltpu.CompilerParams(vmem_limit_bytes=vmem_cap),
        name="back_sent",
    )(grads, narrow_line)


def narrow_kernel(own, columns, line_ref, side_ref, *refs):
    *chan_refs, grad_ref, grads_ref, chan_ref, product_ref = refs
    depth = line_ref.shape[0] // columns
    held = depth - own
    for line in range(columns):
        for side, ref in enumerate((line_ref, side_ref)):
            at = (2 * line + side) * held
            grads_ref[at : at + held] = ref[line * depth + own : (line + 1) * depth]
    at = 0
    for ref in chan_refs:
        rows = min(ref.shape[0], 2 * held)
        chan_ref[at : at + rows] = ref[ref.shape[0] - rows :]
        at += rows
    product_ref[...] = dot_tn(grads_ref[...], chan_ref[...])
    grad_ref[...] = product_ref[pl.ds(pl.multiple_of(place_of() * own, own), own)]


def narrow_sums(narrow_line, narrow_side, chan_group, others, own, columns):
    features = narrow_line.shape[1]
    hidden = chan_group.shape[1]
    total = 2 * columns * chan_group.shape[0]
    return pl.pallas_call(
        functools.partial(narrow_kernel, own, columns),
        out_shape=struct((own, hidden)),
        scratch_shapes=[
            pltpu.VMEM((total, features), bf16), pltpu.VMEM((total, hidden), bf16), pltpu.VMEM((features, hidden), f32),
        ],
        compiler_params=pltpu.CompilerParams(vmem_limit_bytes=vmem_cap),
        name="narrow_sums",
    )(narrow_line, narrow_side, chan_group, *others)


def pooled_kernel(own, columns, chan_ref, line_ref, side_ref, own_ref, sent_ref, turned_ref):
    depth = line_ref.shape[0] // columns
    place = place_of()
    for line in range(columns):
        for side, ref in enumerate((line_ref, side_ref)):
            start = pl.multiple_of((place ^ (2 * line + side)) * own, own)
            turned_ref[pl.ds(start, own)] = dot_nt(ref[line * depth : line * depth + own], chan_ref[...])
    total = turned_ref[...].T
    half = total.shape[0] // 2
    own_ref[...] = total[:half]
    sent_ref[...] = total[half:]


def pooled_parts(chan_group, narrow_line, narrow_side, own, columns):
    images = chan_group.shape[0]
    features = 2 * columns * own
    return pl.pallas_call(
        functools.partial(pooled_kernel, own, columns),
        out_shape=[struct((images // 2, features)), struct((images // 2, features))],
        scratch_shapes=[pltpu.VMEM((features, images), f32)],
        compiler_params=pltpu.CompilerParams(vmem_limit_bytes=vmem_cap),
        name="pooled_parts",
    )(chan_group, narrow_line, narrow_side)


def join_kernel(even_ref, other_ref, *part_refs):
    step = pl.program_id(0)
    total = (even_ref[0, 0].astype(f32) + other_ref[0, 0].astype(f32)).astype(bf16)
    for at, part_ref in enumerate(part_refs):

        @pl.when(step == at)
        def _(part_ref=part_ref):
            part_ref[...] = total


def join(even, other):
    blocks, sides, *rest = even.shape
    spec = pl.BlockSpec((1, 1, *rest), lambda i: (i // sides, i % sides, 0, 0, 0))
    return pl.pallas_call(
        join_kernel,
        grid=(blocks * sides,),
        in_specs=[spec, spec],
        out_specs=[whole(tuple(rest)) for _ in range(blocks * sides)],
        out_shape=[struct(tuple(rest), bf16) for _ in range(blocks * sides)],
        compiler_params=pltpu.CompilerParams(vmem_limit_bytes=vmem_cap),
        name="join",
    )(even, other)


def lines_kernel(share_ref, message_ref, chan_ref, own_ref, *message_refs):
    own = share_ref.shape[1]
    held = chan_ref.shape[0]
    for line in range(share_ref.shape[0]):
        total = share_ref[line].astype(f32) + message_ref[line * own : (line + 1) * own].astype(f32)
        if line == 0:
            own_ref[...] = total
            continue
        message_refs[line - 1][:own] = total.astype(bf16)
        message_refs[line - 1][own : own + held] = chan_ref[...]
        message_refs[line - 1][own + held :] = message_ref[-held:]


def lines_out(share, message, chan_group):
    lines, own, wide = share.shape
    depth = own + 2 * chan_group.shape[0]
    return pl.pallas_call(
        lines_kernel,
        out_shape=[struct((own, wide))] + [struct((depth, wide), bf16) for _ in range(lines - 1)],
        compiler_params=pltpu.CompilerParams(vmem_limit_bytes=vmem_cap),
        name="lines_out",
    )(share, message, chan_group)


def spread_kernel(own_ref, line_ref, side_ref, mine_ref, *part_refs):
    for line in range(own_ref.shape[0]):
        total = own_ref[line].astype(f32) + line_ref[line].astype(f32) + side_ref[line].astype(f32)
        if line == 0:
            mine_ref[...] = total
        else:
            part_refs[line - 1][...] = total.astype(bf16)


def spread(own, line_x, own_y):
    lines, *rest = own.shape
    return pl.pallas_call(
        spread_kernel,
        out_shape=[struct(tuple(rest))] + [struct(tuple(rest), bf16) for _ in range(lines - 1)],
        compiler_params=pltpu.CompilerParams(vmem_limit_bytes=vmem_cap),
        name="spread",
    )(own, line_x, own_y)


def images_kernel(side_by_side_ref, image_ref):
    features = image_ref.shape[2]
    for image in range(image_ref.shape[1]):
        image_ref[:, image] = side_by_side_ref[:, image * features : (image + 1) * features]


def images_apart(side_by_side, count):
    patches, wide = side_by_side.shape
    step = 56
    return pl.pallas_call(
        images_kernel,
        grid=(-(-patches // step),),
        in_specs=[pl.BlockSpec((step, wide), lambda i: (i, 0))],
        out_specs=pl.BlockSpec((step, count, wide // count), lambda i: (i, 0, 0)),
        out_shape=struct((patches, count, wide // count)),
        compiler_params=pltpu.CompilerParams(vmem_limit_bytes=vmem_cap),
        name="images_apart",
    )(side_by_side)


def unpack_kernel(patches, own_ref, other_ref, token_ref, mixing_ref, gain_ref, shift_ref, patch_ref, hidden_ref, output_ref):
    half = own_ref.shape[1] // 3
    total = own_ref[...].astype(f32) + other_ref[...].astype(f32)
    for which in range(2):
        token_ref[which] = total[:, which * half : which * half + patches]
    pieces = []
    for row in range(own_ref.shape[0]):
        for at in range(2 * half, 3 * half, 128):
            pieces.append(total[row : row + 1, at : at + 128])
    mixers, features = (mixing_ref.shape[0], gain_ref.shape[1])
    at = 0

    def fill(ref, row, width, held):
        nonlocal at
        for first in range(0, held, 128):
            size = min(128, width - first)
            if size > 0 and len(ref.shape) == 1:
                ref[first : first + size] = pieces[at][0, :size]
            elif size > 0:
                ref[row : row + 1, first : first + size] = pieces[at][:, :size]
            at += 1

    fill(mixing_ref, 0, mixers, mixers)
    for ref in (gain_ref, shift_ref):
        for row in range(2):
            fill(ref, row, features, features)
    fill(patch_ref, 0, patches, mixers)
    fill(hidden_ref, 0, hidden_ref.shape[0], hidden_ref.shape[0])
    fill(output_ref, 0, features, features)


def unpack(own, other, patches, mixers, features, hidden_size):
    return pl.pallas_call(
        functools.partial(unpack_kernel, patches),
        out_shape=[
            struct((2, own.shape[0], patches)), struct((mixers,)), struct((2, features)), struct((2, features)),
            struct((patches,)), struct((hidden_size,)), struct((features,)),
        ],
        name="unpack",
    )(own, other)


def score_kernel(parts, shifted, received_ref, query_hbm, score_ref, query_ref, sems):
    rows, _, width = received_ref.shape
    length = query_hbm.shape[0] // parts
    offset = 0
    if shifted:
        place = place_of()
        offset = pl.multiple_of(lax.rem(place * query_hbm.shape[0], width), 16)
        query_ref[0:width] = jnp.zeros((width, query_ref.shape[1]), bf16)
        last = rows * width - 2 * width
        query_ref[last:] = jnp.zeros((2 * width, query_ref.shape[1]), bf16)
    copies = [
        pltpu.make_async_copy(
            query_hbm.at[pl.ds(part * length, length)],
            query_ref.at[pl.ds(offset + part * length, length)],
            sems.at[part],
        )
        for part in range(parts)
    ]
    for copy in copies:
        copy.start()
    waited = 0
    total = None
    for row in range(rows):
        while waited < parts and waited * length < (row + 1) * width:
            copies[waited].wait()
            waited += 1
        part = dot(received_ref[row], query_ref[row * width : (row + 1) * width])
        total = part if total is None else total + part
    score_ref[...] = total


def scores(received, queries_t):
    rows, count, width = received.shape
    share, asked = queries_t.shape
    shifted = share != rows * width
    parts = 7 if share % 112 == 0 else 1
    return pl.pallas_call(
        functools.partial(score_kernel, parts, shifted),
        in_specs=[pl.BlockSpec(memory_space=pltpu.VMEM), pl.BlockSpec(memory_space=pl.ANY)],
        out_specs=pl.BlockSpec(memory_space=pltpu.VMEM),
        out_shape=struct((count, asked)),
        scratch_shapes=[pltpu.VMEM((rows * width, asked), bf16), pltpu.SemaphoreType.DMA((parts,))],
        compiler_params=pltpu.CompilerParams(vmem_limit_bytes=vmem_cap),
        name="scores",
    )(received, queries_t)


def score_parts_of(partial_scores, groups, count):
    partial_scores = partial_scores.reshape(groups, count, -1)
    return lax.all_to_all(partial_scores, dp_axes, split_axis=0, concat_axis=0, tiled=True)


def swap(array, axis, code=1):
    devices = lax.axis_size(axis)
    return lax.ppermute(array, axis, [(place, place ^ code) for place in range(devices)])


def swap_both(array, line_code, side_code):
    columns, sides = (lax.axis_size("line"), lax.axis_size("side"))
    pairs = [
        (line * sides + side, (line ^ line_code) * sides + (side ^ side_code))
        for line in range(columns)
        for side in range(sides)
    ]
    return lax.ppermute(array, dp_axes, pairs)


def by_code(parts, place):
    step = 1
    while step < parts.shape[0]:
        pairs = parts.reshape(-1, 2, step, *parts.shape[1:])
        turned = jnp.concatenate([pairs[:, 1:], pairs[:, :1]], axis=1)
        parts = jnp.where((place & step) > 0, turned, pairs).reshape(parts.shape)
        step *= 2
    return parts


def together(*arrays):
    return lax.optimization_barrier(arrays)


def added(left, right):
    return (left.astype(f32) + right.astype(f32)).astype(bf16)


def body(
    images,
    kept_mask,
    pooled_grad,
    token_weights,
    norm_gain,
    norm_bias,
    mixing_bias,
    patch_bias,
    widening,
    narrowing,
    hidden_bias,
    output_bias,
    width_maps,
    hidden_maps,
    queries,
):
    count, patches, features = images.shape
    mixers = mixing_bias.shape[0]
    rank = width_maps.shape[2]
    hidden_size = hidden_bias.shape[0]
    columns = lax.axis_size("line")
    sides = lax.axis_size("side")
    groups = columns * sides
    group = lax.axis_index(dp_axes)
    share, asked = (queries.shape[1], queries.shape[0])
    own_hidden = widening.shape[1]
    own_width = narrowing.shape[1]
    by_hand = groups <= 8 and widening.shape[0] % 16 == 0
    chunks = [(0, count // 2), (count // 2, count)]
    rows = -(-patches // 8) * 8
    extra = rows - patches
    cut = columns // 2

    widen_part = widening.astype(bf16)
    token_part = jnp.pad(jnp.swapaxes(token_weights, 1, 2).astype(bf16), ((0, 0), (0, 0), (0, extra)))
    narrow_part = jnp.swapaxes(narrowing, 0, 1).astype(bf16)
    keep_f = kept_mask.astype(f32)
    kept_count = jnp.sum(keep_f, axis=1, keepdims=True)
    grad_rows = pooled_grad / kept_count
    grad_low = grad_rows.astype(bf16)
    maps_own = jnp.swapaxes(hidden_maps, 1, 2).reshape(2 * rank, own_hidden)
    width_maps = jnp.swapaxes(width_maps, 1, 2)
    keep = jnp.pad(keep_f, ((0, 0), (0, extra)))[:, :, None]
    column = jnp.concatenate([mixing_bias, jnp.pad(patch_bias, (0, extra))])[:, None]
    bias_row = hidden_bias[None, :]
    output_sum = jnp.sum(grad_low.astype(f32) * kept_count, axis=0, keepdims=True)
    if by_hand:
        map_rows = 2 * rank // groups
        maps_part = lax.dynamic_slice_in_dim(maps_own, group * map_rows, map_rows)
        piece = jnp.concatenate([widen_part, maps_part])
        depth = piece.shape[0]
        layout = (depth, widen_part.shape[0], widen_part.shape[0], map_rows)
        token_line = jnp.stack([token_part] + [swap(token_part, "line", code) for code in range(1, columns)])
        grad_pair = jnp.concatenate([grad_low, swap(grad_low, "core")])
        piece, token_line, grad_pair = together(piece, token_line, grad_pair)
        tokens = [token_line, swap(token_line, "side")]
        widen_z = [piece] + [swap(piece, "line", code) for code in range(1, columns)]
        grad_group = jnp.concatenate([grad_pair, swap(grad_pair, "far")])
        grad_near = jnp.concatenate([grad_group, swap(grad_group, "side")])
        line_codes = tuple(sides * code for code in range(columns))
        side_codes = tuple(code ^ 1 for code in line_codes)
        token_codes = (line_codes, side_codes)
        codes = tuple(((side, at), sides * at ^ side) for side in range(sides) for at in range(columns))
        share_shape = (sides, columns, *widening.shape)
    else:
        tokens = [lax.all_gather(token_part, dp_axes, axis=1, tiled=True)[None]]
        token_codes = ((None,),)
        piece = jnp.concatenate([lax.all_gather(widen_part, dp_axes, axis=0, tiled=True), maps_own])
        layout = (piece.shape[0], features, features, 2 * rank)
        piece_x = swap(piece, "far")
        pieces = [piece, swap(piece, "core"), piece_x, swap(piece_x, "core")]
        spans = tuple(((None,), block * own_hidden) for block in range(4))
        codes = (((slice(None),), None),)
        share_shape = (features, own_hidden)

    def forward(chunk):
        out = token_forward(
            images, keep, tokens, token_codes, norm_gain, norm_bias, column, width_maps, *chunks[chunk]
        )
        return list(out)

    forwards = [forward(0)]
    if by_hand:
        narrow_part = jnp.concatenate([narrow_part, grad_near[: 4 * count]])
        forwards[0][:] = together(*forwards[0], *widen_z, narrow_part, grad_near, *tokens)
        widen_z = forwards[0][7 : 7 + columns]
        narrow_part, grad_near, *tokens = forwards[0][7 + columns :]
        forwards[0] = forwards[0][:7]
        widen_line = jnp.concatenate(widen_z)
        widen_y, widen_x = (swap(widen_line, "side"), swap(widen_line, "far"))
        narrow_z = [narrow_part] + [swap(narrow_part, "line", code) for code in range(1, columns)]
        forwards.append(forward(1))
        forwards[1][:] = together(*forwards[1], widen_y, widen_x, *narrow_z)
        widen_y, widen_x, *narrow_z = forwards[1][7:]
        forwards[1] = forwards[1][:7]
        narrow_line = jnp.concatenate(narrow_z)
        half = widen_line.shape[0] // 2
        widen_xy, widen_yx = (swap(widen_y[:half], "far"), swap(widen_x[half:], "side"))
        back_part, back_y = back_sent(grad_near, narrow_line, own_width, columns, sides)
        back_part = added(back_part, swap(back_y, "side"))
        narrow_line, widen_xy, widen_yx = together(narrow_line, widen_xy, widen_yx)
        narrow_y = swap(narrow_line, "side")
        pieces = [widen_line, widen_y, widen_x, widen_xy, widen_yx]
        pieces = pieces + [swap(piece, "core") for piece in pieces]
        near = [(line_codes, 0), (side_codes, 0), (line_codes, 2), (side_codes[:cut], 2), (side_codes[cut:], 2)]
        spans = tuple((codes, block * own_hidden) for codes, block in near) + tuple(
            (codes, (block + 1) * own_hidden) for codes, block in near
        )
    else:
        grad_pair = jnp.concatenate([grad_low, swap(grad_low, "core")])
        grad_group = jnp.concatenate([grad_pair, swap(grad_pair, "far")])
        narrow_t = lax.all_gather(narrow_part, dp_axes, axis=0, tiled=True)
        grad_all = lax.all_gather(grad_group, dp_axes, axis=0, tiled=True)
        grad_all = lax.dynamic_slice_in_dim(grad_all, group * own_width, own_width, 1)
        back_part = dot(grad_group, narrow_t).astype(bf16)
        forwards.append(forward(1))
    back_part = back_part.reshape(4, count, own_hidden)
    back_x = swap(back_part[2:], "far")
    back_core = swap(jnp.stack([back_part[1], back_x[1]]), "core")
    back_rows = jnp.concatenate([back_part[0], back_core[0], back_x[0], back_core[1]], axis=1)

    row_ends = [-(-share * (place + 1) // mixers) for place in range(groups)]
    row_starts = tuple(share * place // mixers for place in range(groups))
    part_rows = max(end - start for start, end in zip(row_starts, row_ends))
    queries_t = jnp.swapaxes(queries, 0, 1)
    if share % 16 != 0:
        offset = lax.rem(group * share, mixers)
        queries_t = lax.dynamic_update_slice(
            jnp.zeros((part_rows * mixers, asked), bf16), queries_t, (offset, jnp.int32(0))
        )

    def channel_chunk(chunk, second, left, before):
        first, last = chunks[chunk]
        number = last - first
        return channel(
            second.reshape(number * rows, features), keep, left.reshape(number * rows, rank),
            back_rows, bias_row, grad_low, width_maps, pieces, spans, layout, codes, share_shape, before, mixers,
            chunk, first, last, last == count,
        )

    def backward(chunk, grad, saved, adapters, hidden_sum, before):
        first, last = chunks[chunk]
        hidden, slope, _, normed, inverse = saved[:5]
        image_grad, *parts, sums, token_total, token_share = token_backward(
            images, keep, grad_rows[:, None, :], grad.reshape(last - first, rows, features), normed, inverse, hidden,
            slope, tokens, token_codes, norm_gain, norm_bias, adapters,
            hidden_sum, output_sum, before, row_starts, part_rows, columns,
            first, last,
        )
        return image_grad, parts, sums, token_total, token_share

    second_grad, chan_first, hidden_sum, adapters, shares_first, widen_full, maps_full = channel_chunk(
        0, forwards[0][2], forwards[0][6], None
    )
    if by_hand:
        second_grad, chan_first, hidden_sum, adapters, shares_first, widen_full, maps_full, narrow_y = together(
            second_grad, chan_first, hidden_sum, adapters, shares_first, widen_full, maps_full, narrow_y
        )
    image_grad_first, parts, sums, token_total, _ = backward(
        0, second_grad, forwards[0], adapters, hidden_sum, None
    )
    second, shares_first, *parts = together(forwards[1][2], shares_first, *parts)
    received_first = lax.all_to_all(parts[0], dp_axes, split_axis=0, concat_axis=0, tiled=True)


    second_grad, chan_second, hidden_sum, adapters, *shares = channel_chunk(
        1, second, forwards[1][6], (widen_full, maps_full, hidden_sum, shares_first)
    )
    second_grad, chan_second, hidden_sum, adapters, *shares, received_first = together(
        second_grad, chan_second, hidden_sum, adapters, *shares, received_first
    )
    share_core = swap(shares[1], "core")
    chan_pooled = jnp.concatenate([chan_first, chan_second]).astype(bf16).reshape(count, 4, own_hidden)
    chan_x = swap(chan_pooled[:, 2:], "far")
    image_grad, parts, sums, _, token_share = backward(
        1, second_grad, forwards[1], adapters, hidden_sum, (token_total, sums, image_grad_first)
    )
    image_grad, parts[0], sums, token_share, chan_x, share_core = together(
        image_grad, parts[0], sums, token_share, chan_x, share_core
    )
    received_second = lax.all_to_all(parts[0], dp_axes, split_axis=0, concat_axis=0, tiled=True)
    chan_core = swap(jnp.stack([chan_pooled[:, 1], chan_x[:, 1]]), "core")
    chan_group = jnp.concatenate([chan_pooled[:, 0], chan_core[0], chan_x[:, 0], chan_core[1]])

    own_mixers, wide = token_share.shape[2:]
    lines = features // mixers
    if by_hand:
        own_line, own_side, far_line, far_side = join(shares[0], share_core)
        message = jnp.concatenate([token_share[1].reshape(-1, wide), chan_group])
        own_line, own_side, far_line, far_side, message = together(own_line, own_side, far_line, far_side, message)
        far_x = swap(far_side, "far")
        message = swap(message, "side")
        image_grad = images_apart(image_grad, count)
        out_own, out_sent = pooled_parts(chan_group, narrow_line, narrow_y, own_width, columns)
        far_x, far_line, image_grad, message, out_own, out_sent = together(
            far_x, far_line, image_grad, message, out_own, out_sent
        )
        own_y = swap(added(own_side, far_x), "side")
        line_x = swap(far_line, "far")
        token_total, *messages = lines_out(token_share[0], message, chan_group)
        received_second, *messages = together(received_second, *messages)
        messages = [swap(part, "line", code) for code, part in enumerate(messages, 1)]
        arrived = jnp.concatenate([received_first, received_second], axis=1)
        arrived = jnp.moveaxis(arrived, 2, 0).reshape(part_rows, groups * count, mixers)
        own_y, line_x, arrived = together(own_y, line_x, arrived)
        widening_grad, *widen_sums = spread(own_line, line_x, own_y)
        arrived, *widen_sums = together(arrived, *widen_sums)
        widen_sums = [swap(part, "line", code) for code, part in enumerate(widen_sums, 1)]
        partial_scores = scores(arrived, queries_t)
        _, out_sent, *messages = together(partial_scores, out_sent, *messages)
        image_grad = jnp.swapaxes(image_grad, 0, 1)
        total = token_total
        for part in messages:
            total = total + part[:own_mixers].astype(f32)
        total = total.astype(bf16)
        total_x = swap(total, "far")
        out_x = swap(out_sent, "far")
        narrowing_grad = narrow_sums(
            narrow_line, narrow_y, chan_group, [message[-chan_group.shape[0] :], *messages], own_width, columns
        ).T
        total_x, out_x, narrowing_grad, *widen_sums = together(total_x, out_x, narrowing_grad, *widen_sums)
        total = added(total, total_x)
        token_grad, mixing_grad, gain_grad, shift_grad, patch_grad, hidden_grad, output_grad = unpack(
            total, swap(total, "core"), patches, mixers, features, hidden_size
        )
        score_parts = score_parts_of(partial_scores, groups, count)
        for widen_sum in widen_sums:
            widening_grad = widening_grad + widen_sum.astype(f32)
    else:
        narrowing_grad = None
        image_grad = jnp.swapaxes(image_grad.reshape(patches, count, features), 0, 1)
        arrived = jnp.concatenate([received_first, received_second], axis=1)
        arrived = jnp.moveaxis(arrived, 2, 0).reshape(part_rows, groups * count, mixers)
        score_parts = score_parts_of(scores(arrived, queries_t), groups, count)
        both = added(shares[0], share_core)
        own, far = (both[0], both[1])
        own = added(own, jnp.concatenate([swap(far[:1], "far"), swap(far[1:], "far")]))
        widening_grad = lax.psum_scatter(own, dp_axes, scatter_dimension=0, tiled=True).astype(f32)
        chan_all = lax.all_gather(chan_group, dp_axes, axis=0, tiled=True)
        summed = jnp.swapaxes(token_share, 0, 1).reshape(groups, own_mixers, wide)
        summed = by_code(summed, group).astype(f32)
        total = lax.psum(lax.psum_scatter(summed, dp_axes, scatter_dimension=0, tiled=True)[0], ("far", "core"))
        half = wide // 3
        sums, more = lax.psum((sums, jnp.concatenate([hidden_sum, output_sum], axis=1)[0]), dp_axes + ("far", "core"))
        token_grad = jnp.stack([total[:, :patches], total[:, half : half + patches]])
        mixing_grad = sums[0]
        gain_grad = sums[1 : 1 + 2 * lines].reshape(2, features)
        shift_grad = sums[1 + 2 * lines : 1 + 4 * lines].reshape(2, features)
        patch_grad = sums[1 + 4 * lines, :patches]
        hidden_grad, output_grad = (more[:hidden_size], more[hidden_size : hidden_size + features])
    token_grad = jnp.swapaxes(token_grad, 1, 2)
    if narrowing_grad is None:
        narrowing_grad = dot_tn(grad_all, chan_all).T

    if not by_hand:
        out_part = dot_nt(chan_group, narrow_t)
        out_own, out_x = (out_part[: 2 * count], swap(out_part[2 * count :], "far"))
    out_pair = out_own + out_x
    chan_out = out_pair[:count] + swap(out_pair[count:], "core")
    score_parts, token_grad, narrowing_grad, chan_out = together(score_parts, token_grad, narrowing_grad, chan_out)
    influence = jnp.sum(score_parts, axis=0)
    pooled_in = jnp.concatenate([forwards[0][5][:, 0], forwards[1][5][:, 0]])
    pooled = (pooled_in + chan_out) / kept_count + output_bias

    return (
        pooled,
        image_grad,
        token_grad,
        gain_grad,
        shift_grad,
        mixing_grad,
        patch_grad,
        widening_grad,
        narrowing_grad,
        hidden_grad,
        output_grad,
        influence,
    )


def solution(mesh):
    groups = mesh.shape["dp"]
    models = mesh.shape["mp"]
    mesh = Mesh(mesh.devices.reshape(groups // 2, 2, models // 2, 2), ("line", "side", "far", "core"))
    dp = ("line", "side")
    mp = ("far", "core")
    every = dp + mp
    placed = (
        P(every, None, None),
        P(every, None),
        P(every, None),
        P(None, None, dp),
        P(),
        P(),
        P(),
        P(),
        P(dp, mp),
        P(mp, dp),
        P(),
        P(),
        P(),
        P(None, mp, None),
        P(None, dp),
    )
    return jax.shard_map(
        body,
        mesh=mesh,
        in_specs=placed,
        out_specs=(
            P(every, None),
            P(every, None, None),
            P(None, None, dp),
            P(),
            P(),
            P(),
            P(),
            P(dp, mp),
            P(mp, dp),
            P(),
            P(),
            P(every, None),
        ),
        check_vma=False,
    )
```

```python
import functools

import jax
import jax.numpy as jnp
from jax import lax
from jax.experimental import pallas as pl
from jax.experimental.pallas import tpu as pltpu
from jax.sharding import Mesh
from jax.sharding import PartitionSpec as P

norm_eps = 1e-06
bf16 = jnp.bfloat16
f32 = jnp.float32
vmem_cap = 58 * 1024 * 1024
dp_axes = ("line", "side")


def dot(left, right):
    return jnp.dot(left, right, preferred_element_type=f32)


def dot_nt(left, right):
    return lax.dot_general(left, right, (((1,), (1,)), ((), ())), preferred_element_type=f32)


def dot_tn(left, right):
    return lax.dot_general(left, right, (((0,), (0,)), ((), ())), preferred_element_type=f32)


def exact_tn(left, right):
    return lax.dot_general(
        left, right, (((0,), (0,)), ((), ())), precision=lax.Precision.HIGHEST, preferred_element_type=f32
    )


def gelu_pair(values):
    cumulative = 0.5 + 0.5 * lax.erf(values * 0.7071067811865476)
    density = jnp.exp2(values * values * -0.7213475204444817) * 0.3989422804014327
    return (values * cumulative, cumulative + values * density)


def normalize(values):
    average = jnp.mean(values, axis=-1, keepdims=True)
    centered = values - average
    spread = jnp.mean(centered * centered, axis=-1, keepdims=True)
    inverse = lax.rsqrt(spread + norm_eps)
    return (centered * inverse, inverse)


def norm_back(grad_norm, normed, inverse):
    first_mean = jnp.mean(grad_norm, axis=-1, keepdims=True)
    second_mean = jnp.mean(grad_norm * normed, axis=-1, keepdims=True)
    return inverse * (grad_norm - first_mean - normed * second_mean)


def whole(shape):
    return pl.BlockSpec(shape, lambda i: (0,) * len(shape))


def each(shape, first=0):
    return pl.BlockSpec((1,) + shape, lambda i: (i + first,) + (0,) * len(shape))


def struct(shape, dtype=f32):
    return jax.ShapeDtypeStruct(shape, dtype)


def place_of():
    return lax.axis_index("line") * lax.axis_size("side") + lax.axis_index("side")


def assemble_tokens(piece_refs, codes, token_ref):
    place = place_of()
    for piece_ref, own_codes in zip(piece_refs, codes):
        own = piece_ref.shape[2]
        for at, code in enumerate(own_codes):
            start = 0 if code is None else pl.multiple_of((place ^ code) * own, own)
            for which in range(2):
                token_ref[which, pl.ds(start, own)] = piece_ref[at, which]


def token_forward_kernel(
    codes, image_ref, keep_ref, gain_ref, shift_ref, column_ref, width_ref, *refs,
):
    piece_refs, refs = (refs[: len(codes)], refs[len(codes) :])
    hidden_ref, slope_ref, second_ref, normed_ref, inverse_ref, pooled_ref, left_ref, token_ref, padded_ref = refs
    mixers = token_ref.shape[1]
    patches = image_ref.shape[1]

    @pl.when(pl.program_id(0) == 0)
    def _():
        assemble_tokens(piece_refs, codes, token_ref)
        padded_ref[patches:] = jnp.zeros((padded_ref.shape[0] - patches, padded_ref.shape[1]), f32)

    padded_ref[:patches] = image_ref[0].astype(f32)
    inputs = padded_ref[...]
    keep = keep_ref[0]
    normed_one, _ = normalize(inputs)
    masked = ((normed_one * gain_ref[0:1] + shift_ref[0:1]) * keep).astype(bf16)
    mixed = dot(token_ref[0], masked) + column_ref[:mixers]
    hidden, slope = gelu_pair(mixed)
    hidden = hidden.astype(bf16)
    hidden_ref[0] = hidden
    slope_ref[0] = slope.astype(bf16)
    residual = inputs + dot_tn(token_ref[1], hidden) + column_ref[mixers:]
    pooled_ref[0] = jnp.sum(residual * keep, axis=0, keepdims=True)
    normed_two, inverse_two = normalize(residual)
    second = (normed_two * gain_ref[1:2] + shift_ref[1:2]).astype(bf16)
    second_ref[0] = second
    normed_ref[0] = normed_two.astype(bf16)
    inverse_ref[0] = inverse_two
    left_ref[0] = dot_nt(second, width_ref[0])


def token_forward(images, keep, tokens, codes, norm_gain, norm_bias, column, width_maps, first, last):
    count = last - first
    _, patches, features = images.shape
    rows = keep.shape[1]
    mixers = column.shape[0] - rows
    rank = width_maps.shape[1]
    return pl.pallas_call(
        functools.partial(token_forward_kernel, codes),
        grid=(count,),
        in_specs=[
            each((patches, features), first), each((rows, 1), first),
            whole((2, features)), whole((2, features)), whole((mixers + rows, 1)), whole((2, rank, features)),
        ]
        + [whole(piece.shape) for piece in tokens],
        out_specs=[
            each((mixers, features)), each((mixers, features)), each((rows, features)), each((rows, features)),
            each((rows, 1)), each((1, features)), each((rows, rank)),
        ],
        out_shape=[
            struct((count, mixers, features), bf16), struct((count, mixers, features), bf16),
            struct((count, rows, features), bf16), struct((count, rows, features), bf16),
            struct((count, rows, 1)), struct((count, 1, features)), struct((count, rows, rank)),
        ],
        scratch_shapes=[pltpu.VMEM((2, mixers, rows), bf16), pltpu.VMEM((rows, features), f32)],
        compiler_params=pltpu.CompilerParams(vmem_limit_bytes=vmem_cap),
        name="token_forward",
    )(images, keep, norm_gain, norm_bias, column, width_maps, *tokens)


def piece_copies(piece_refs, widen_ref, maps_ref, sems, spans, layout):
    depth, wide_rows, map_at, map_rows = layout
    copies = []
    place = place_of()
    for at, (piece_ref, (codes, column)) in enumerate(zip(piece_refs, spans)):
        cols = pl.ds(column, piece_ref.shape[1])
        for part, code in enumerate(codes):
            for which, (target, first, rows) in enumerate(((widen_ref, 0, wide_rows), (maps_ref, map_at, map_rows))):
                start = 0 if code is None else pl.multiple_of((place ^ code) * rows, rows)
                copy = pltpu.make_async_copy(
                    piece_ref.at[pl.ds(part * depth + first, rows)],
                    target.at[pl.ds(start, rows), cols],
                    sems.at[at, part, which],
                )
                copies.append((column, copy))
    return copies


def channel_kernel(
    spans, layout, codes, first, resumed, final,
    second_ref, keep_ref, left_ref, back_ref, bias_ref, rows_ref, width_ref, *refs,
):
    if resumed:
        widen_ref, maps_ref, sum_before_ref, before_ref, *refs = refs
    else:
        piece_refs, refs = (refs[: len(spans)], refs[len(spans) :])
    grad_ref, pooled_ref, sum_ref, adapter_ref, *refs = refs
    share_refs, refs = (refs[: 2 if final else 1], refs[2 if final else 1 :])
    if resumed:
        total_ref, right_ref, out_ref, pair_ref = refs
    else:
        widen_out, maps_out, widen_ref, maps_ref, total_ref, right_ref, out_ref, pair_ref, sems, out_sems = refs
    step = pl.program_id(0)
    steps = pl.num_programs(0)
    count = pooled_ref.shape[0]
    total_rows, features = second_ref.shape
    rows = total_rows // count
    rank = left_ref.shape[1]
    own = bias_ref.shape[1] // 4
    model = lax.axis_index("far") * lax.axis_size("core") + lax.axis_index("core")
    second = second_ref[...]
    keep = keep_ref[...].reshape(total_rows, 1)
    if not resumed:
        copies = piece_copies(piece_refs, widen_ref, maps_ref, sems, spans, layout)
        kept = [
            pltpu.make_async_copy(widen_ref, widen_out, out_sems.at[0]),
            pltpu.make_async_copy(maps_ref, maps_out, out_sems.at[1]),
        ]

    @pl.when(step == 0)
    def _():
        if resumed:
            sum_ref[...] = sum_before_ref[...]
        else:
            for _, copy in copies:
                copy.start()
            for column, copy in copies:
                if column < 2 * own:
                    copy.wait()
            sum_ref[...] = jnp.zeros_like(sum_ref)
        right_ref[...] = jnp.zeros_like(right_ref)
        out_ref[...] = jnp.zeros_like(out_ref)
        grad_ref[...] = jnp.zeros_like(grad_ref)

    if not resumed:

        @pl.when(step > 0)
        def _():
            for column, copy in copies:
                if column >= 2 * own:
                    copy.wait()
            for copy in kept:
                copy.start()

    for half in range(2):
        cols = slice(half * own, (half + 1) * own)
        wide = cols if resumed else pl.ds(pl.multiple_of((2 * step + half) * own, own), own)
        widen = widen_ref[:, wide]
        bias_at = pl.multiple_of((model ^ (2 * step + half)) * own, own)
        pre = dot(second, widen) + bias_ref[:, pl.ds(bias_at, own)]
        hidden, slope = gelu_pair(pre)
        hidden = (hidden.astype(bf16).astype(f32) * keep).reshape(count, rows, own)
        pooled_hidden = jnp.sum(hidden, axis=1)
        pooled_ref[:, cols] = pooled_hidden
        back = back_ref[first : first + count, cols].astype(f32)[:, None, :]
        pre_grad = (slope * keep).reshape(count, rows, own) * back
        pre_grad = pre_grad.reshape(total_rows, own).astype(bf16)
        sum_ref[:, pl.ds(bias_at, own)] += jnp.sum(pre_grad.astype(f32), axis=0, keepdims=True)
        grad_ref[...] += dot_nt(pre_grad, widen)
        right_ref[...] += dot_nt(pre_grad, maps_ref[:rank, wide])
        out_ref[...] += dot_nt(pooled_hidden.astype(bf16), maps_ref[rank:, wide])
        share = dot_tn(second, pre_grad)
        if resumed:
            share = share + before_ref[:, cols].astype(f32)
        if not final:
            share_refs[0][:, cols] = share.astype(bf16)
            continue
        total_ref[...] = share
        place = place_of()
        part_rows = share_refs[half].shape[-2]
        for index, code in codes:
            start = 0 if code is None else pl.multiple_of((place ^ code) * part_rows, part_rows)
            share_refs[half][(0, *index)] = total_ref[pl.ds(start, part_rows)].astype(bf16)

    @pl.when(step == steps - 1)
    def _():
        if not resumed:
            for copy in kept:
                copy.wait()
        outer = dot_nt(rows_ref[first : first + count], width_ref[1])
        lines = adapter_ref.shape[2] // rank
        pair_ref[2 * rank :] = jnp.zeros((pair_ref.shape[0] - 2 * rank, rank), f32)
        for image in range(count):
            span = slice(image * rows, (image + 1) * rows)
            pair_ref[:rank] = exact_tn(left_ref[span], right_ref[span])
            pair_ref[rank : 2 * rank] = exact_tn(out_ref[image : image + 1], outer[image : image + 1])
            adapter_ref[image] = jnp.concatenate(
                [pair_ref[pl.ds(line, adapter_ref.shape[1], stride=lines)] for line in range(lines)], axis=1
            ).astype(bf16)


def channel(
    second, keep, left, back_rows, bias_row, grad_low, width_maps, pieces, spans, layout, codes, share_shape, before,
    mixers, chunk, first, last, final,
):
    count = last - first
    total_rows, features = second.shape
    hidden_size = bias_row.shape[1]
    rank = left.shape[1]
    held = back_rows.shape[0]
    lines = mixers // rank
    adapter_rows = -(-2 * rank // lines)
    once = pl.Buffered(1)
    resumed = before is not None
    anywhere = pl.BlockSpec(memory_space=pl.ANY)
    wide = hidden_size // 2

    def columns(rows):
        return pl.BlockSpec((rows, wide), lambda i: (0, i))

    if final:
        share_specs = [
            pl.BlockSpec((1, *share_shape), lambda i: (i,) + (0,) * len(share_shape)) for _ in range(2)
        ]
        share_out = [struct((2, *share_shape), bf16) for _ in range(2)]
    else:
        share_specs = [columns(features)]
        share_out = [struct((features, hidden_size), bf16)]
    scratch = [
        pltpu.VMEM((features, hidden_size // 4), f32),
        pltpu.VMEM((total_rows, rank), f32),
        pltpu.VMEM((count, rank), f32),
        pltpu.VMEM((adapter_rows * lines, rank), f32),
    ]
    if resumed:
        matrix_specs = [columns(features), columns(2 * rank), whole((1, hidden_size)), columns(features)]
        matrices = before
    else:
        matrix_specs = [anywhere] * len(pieces)
        matrices = pieces
        share_specs = share_specs + [anywhere, anywhere]
        share_out = share_out + [struct((features, hidden_size), bf16), struct((2 * rank, hidden_size), bf16)]
        scratch = [
            pltpu.VMEM((features, hidden_size), bf16), pltpu.VMEM((2 * rank, hidden_size), bf16), *scratch,
            pltpu.SemaphoreType.DMA((len(spans), max(len(span[0]) for span in spans), 2)),
            pltpu.SemaphoreType.DMA((2,)),
        ]
    return pl.pallas_call(
        functools.partial(channel_kernel, spans, layout, codes, first, resumed, final),
        grid=(2,),
        in_specs=[
            whole((total_rows, features)), pl.BlockSpec((count, total_rows // count, 1), lambda i: (chunk, 0, 0)),
            whole((total_rows, rank)), columns(held),
            whole((1, hidden_size)), whole((held, features)), whole((2, rank, features)),
        ]
        + matrix_specs,
        out_specs=[
            whole((total_rows, features)), columns(count), whole((1, hidden_size)), whole((count, adapter_rows, mixers)),
        ]
        + share_specs,
        out_shape=[
            struct((total_rows, features)), struct((count, hidden_size)), struct((1, hidden_size)),
            struct((count, adapter_rows, mixers), bf16),
        ]
        + share_out,
        scratch_shapes=scratch,
        compiler_params=pltpu.CompilerParams(vmem_limit_bytes=vmem_cap),
        name="channel",
    )(
        second, keep, left, back_rows, bias_row, grad_low, width_maps, *matrices
    )


def token_backward_kernel(
    codes, resumed, patches, row_starts,
    image_ref, keep_ref, row_ref, grad_ref, normed_ref, inverse_ref, hidden_ref, slope_ref,
    gain_ref, shift_ref, adapter_ref, hidden_sum_ref, output_sum_ref, *refs,
):
    piece_refs, refs = (refs[: len(codes)], refs[len(codes) :])
    if resumed:
        total_before_ref, sums_before_ref, _, *refs = refs
    image_grad_ref, parts_ref, sums_ref, total_ref, share_ref, vector_ref, token_ref, padded_ref = refs
    step = pl.program_id(0)
    steps = pl.num_programs(0)
    rows, features = padded_ref.shape
    mixers = hidden_ref.shape[1]
    keep = keep_ref[0]
    grad = grad_ref[0]

    @pl.when(step == 0)
    def _():
        if resumed:
            total_ref[...] = total_before_ref[...]
            sums_ref[...] = sums_before_ref[...]
        else:
            total_ref[...] = jnp.zeros_like(total_ref)
            sums_ref[...] = jnp.zeros_like(sums_ref)
        vector_ref[...] = jnp.zeros_like(vector_ref)
        padded_ref[patches:] = jnp.zeros((rows - patches, features), f32)
        assemble_tokens(piece_refs, codes, token_ref)

    normed_two = normed_ref[0].astype(f32)
    residual_grad = keep * row_ref[0] + norm_back(grad * gain_ref[1:2], normed_two, inverse_ref[0])
    gain_two = jnp.sum(grad * normed_two, axis=0, keepdims=True)
    shift_two = jnp.sum(grad, axis=0, keepdims=True)
    low = residual_grad.astype(bf16)
    outward_grad = dot_nt(low, hidden_ref[0])
    mixed_grad = (dot(token_ref[1], low) * slope_ref[0].astype(f32)).astype(bf16)
    ones = jnp.ones((8, features), bf16)
    mixing = dot_nt(ones, mixed_grad)[0:1]
    patch_sum = dot_nt(ones, low)[0:1]
    padded_ref[:patches] = image_ref[0].astype(f32)
    normed_one, inverse_one = normalize(padded_ref[...])
    masked = ((normed_one * gain_ref[0:1] + shift_ref[0:1]) * keep).astype(bf16)
    inward_grad = dot_nt(masked, mixed_grad)
    first_grad = dot_tn(token_ref[0], mixed_grad) * keep
    gain_one = jnp.sum(first_grad * normed_one, axis=0, keepdims=True)
    shift_one = jnp.sum(first_grad, axis=0, keepdims=True)
    image_grad = residual_grad + norm_back(first_grad * gain_ref[0:1], normed_one, inverse_one)
    image_grad_ref[...] = image_grad[:patches]
    lines = [mixing]
    for row in (gain_one, gain_two, shift_one, shift_two):
        for at in range(0, features, mixers):
            lines.append(row[:, at : at + mixers])
    small = jnp.concatenate(lines, axis=0)
    adapter_at = 2 * patches + len(lines)
    vector_ref[0:patches] = inward_grad[:patches]
    vector_ref[patches : 2 * patches] = outward_grad[:patches]
    vector_ref[2 * patches : adapter_at] = small
    vector_ref[adapter_at : adapter_at + adapter_ref.shape[1]] = adapter_ref[0].astype(f32)
    part_rows = parts_ref.shape[2]
    for place, start in enumerate(row_starts):
        parts_ref[place, 0] = vector_ref[start : start + part_rows].astype(bf16)
    total_ref[0] += inward_grad
    total_ref[1] += outward_grad
    sums_ref[0 : len(lines)] += small
    sums_ref[len(lines) : len(lines) + 1, 0:rows] += patch_sum

    @pl.when(step == steps - 1)
    def _():
        sides, columns, own, wide = share_ref.shape
        half = wide // 3
        line, side = (lax.axis_index("line"), lax.axis_index("side"))
        turned = [total_ref[which].T.astype(bf16) for which in range(2)]
        sums = [sums_ref[row : row + 1, at : at + 128] for row in range(sums_ref.shape[0]) for at in range(0, mixers, 128)]
        for ref in (hidden_sum_ref, output_sum_ref):
            sums += [ref[:, at : at + 128] for at in range(0, ref.shape[1], 128)]
        per_row = half // 128
        depth = len(sums) // per_row
        sums = [jnp.concatenate(sums[at::per_row], axis=0) for at in range(per_row)]
        sums = jnp.concatenate(sums, axis=1).astype(bf16)
        for place in range(sides * columns):
            at = ((place % sides) ^ side, (place // sides) ^ line)
            for which in range(2):
                part = turned[which][place * own : (place + 1) * own]
                share_ref[at[0], at[1], :, which * half : which * half + rows] = part
            if depth <= own:
                share_ref[at[0], at[1], 0:depth, 2 * half :] = sums


def token_backward(
    images, keep, grad_rows, grad, normed, inverse, hidden, slope, tokens, codes, norm_gain, norm_bias, adapters, hidden_sum,
    output_sum, before, row_starts, part_rows, columns, first, last,
):
    count = last - first
    _, patches, features = images.shape
    rows = keep.shape[1]
    mixers = hidden.shape[1]
    adapter_rows = adapters.shape[1]
    groups = len(row_starts)
    resumed = before is not None
    small = 2 + 4 * (features // mixers)
    held = -(-(row_starts[-1] + part_rows) // 8) * 8
    held = max(held, -(-(2 * patches + small + adapter_rows) // 8) * 8)
    wide = 3 * (-(-rows // 128) * 128)
    share_shape = (groups // columns, columns, mixers // groups, wide)
    return pl.pallas_call(
        functools.partial(token_backward_kernel, codes, resumed, patches, row_starts),
        grid=(count,),
        in_specs=[
            each((patches, features), first), each((rows, 1), first), each((1, features), first), each((rows, features)),
            each((rows, features)), each((rows, 1)), each((mixers, features)), each((mixers, features)),
            whole((2, features)), whole((2, features)), each((adapter_rows, mixers)), whole(hidden_sum.shape), whole(output_sum.shape),
        ]
        + [whole(piece.shape) for piece in tokens]
        + ([whole((2, rows, mixers)), whole((small, mixers)), pl.BlockSpec(memory_space=pl.ANY)] if resumed else []),
        out_specs=[
            pl.BlockSpec((patches, features), lambda i: (0, i + first)), pl.BlockSpec((groups, 1, part_rows, mixers), lambda i: (0, i, 0, 0)),
            whole((small, mixers)), whole((2, rows, mixers)), whole(share_shape),
        ],
        out_shape=[
            struct((patches, images.shape[0] * features)), struct((groups, count, part_rows, mixers), bf16),
            struct((small, mixers)), struct((2, rows, mixers)), struct(share_shape, bf16),
        ],
        scratch_shapes=[
            pltpu.VMEM((held, mixers), f32), pltpu.VMEM((2, mixers, rows), bf16), pltpu.VMEM((rows, features), f32),
        ],
        compiler_params=pltpu.CompilerParams(vmem_limit_bytes=vmem_cap),
        input_output_aliases={len(tokens) + 15: 0} if resumed else {},
        name="token_backward",
    )(
        images, keep, grad_rows, grad, normed, inverse, hidden, slope, norm_gain, norm_bias, adapters, hidden_sum, output_sum,
        *tokens, *(before if resumed else []),
    )


def back_kernel(own, columns, sides, grad_ref, narrow_ref, back_ref, sent_ref, turned_ref):
    turned_ref[...] = grad_ref[...].astype(f32).T
    depth = narrow_ref.shape[0] // columns
    line, side = (lax.axis_index("line"), lax.axis_index("side"))
    total = None
    for code in range(columns):
        start = pl.multiple_of(((line ^ code) * sides + side) * own, own)
        part = dot_tn(turned_ref[pl.ds(start, own)].astype(bf16), narrow_ref[code * depth : code * depth + own])
        total = part if total is None else total + part
    half = total.shape[0] // 2
    back_ref[...] = total[:half]
    sent_ref[...] = total[half:].astype(bf16)


def back_sent(grads, narrow_line, own, columns, sides):
    return pl.pallas_call(
        functools.partial(back_kernel, own, columns, sides),
        out_shape=[
            struct((grads.shape[0] // 2, narrow_line.shape[1])), struct((grads.shape[0] // 2, narrow_line.shape[1]), bf16),
        ],
        scratch_shapes=[pltpu.VMEM((grads.shape[1], grads.shape[0]), f32)],
        compiler_params=pltpu.CompilerParams(vmem_limit_bytes=vmem_cap),
        name="back_sent",
    )(grads, narrow_line)


def narrow_kernel(own, columns, line_ref, side_ref, *refs):
    *chan_refs, grad_ref, grads_ref, chan_ref, product_ref = refs
    depth = line_ref.shape[0] // columns
    held = depth - own
    for line in range(columns):
        for side, ref in enumerate((line_ref, side_ref)):
            at = (2 * line + side) * held
            grads_ref[at : at + held] = ref[line * depth + own : (line + 1) * depth]
    at = 0
    for index, ref in enumerate(chan_refs):
        rows = held if index < 2 else 2 * held
        chan_ref[at : at + rows] = ref[ref.shape[0] - rows :]
        at += rows
    product_ref[...] = dot_tn(grads_ref[...], chan_ref[...])
    grad_ref[...] = product_ref[pl.ds(pl.multiple_of(place_of() * own, own), own)]


def narrow_sums(narrow_line, narrow_side, chan_group, others, own, columns):
    features = narrow_line.shape[1]
    hidden = chan_group.shape[1]
    total = 2 * columns * chan_group.shape[0]
    return pl.pallas_call(
        functools.partial(narrow_kernel, own, columns),
        out_shape=struct((own, hidden)),
        scratch_shapes=[
            pltpu.VMEM((total, features), bf16), pltpu.VMEM((total, hidden), bf16), pltpu.VMEM((features, hidden), f32),
        ],
        compiler_params=pltpu.CompilerParams(vmem_limit_bytes=vmem_cap),
        name="narrow_sums",
    )(narrow_line, narrow_side, chan_group, *others)


def pooled_kernel(own, columns, chan_ref, line_ref, side_ref, own_ref, sent_ref, turned_ref):
    depth = line_ref.shape[0] // columns
    place = place_of()
    for line in range(columns):
        for side, ref in enumerate((line_ref, side_ref)):
            start = pl.multiple_of((place ^ (2 * line + side)) * own, own)
            turned_ref[pl.ds(start, own)] = dot_nt(ref[line * depth : line * depth + own], chan_ref[...])
    total = turned_ref[...].T
    half = total.shape[0] // 2
    own_ref[...] = total[:half]
    sent_ref[...] = total[half:]


def pooled_parts(chan_group, narrow_line, narrow_side, own, columns):
    images = chan_group.shape[0]
    features = 2 * columns * own
    return pl.pallas_call(
        functools.partial(pooled_kernel, own, columns),
        out_shape=[struct((images // 2, features)), struct((images // 2, features))],
        scratch_shapes=[pltpu.VMEM((features, images), f32)],
        compiler_params=pltpu.CompilerParams(vmem_limit_bytes=vmem_cap),
        name="pooled_parts",
    )(chan_group, narrow_line, narrow_side)


def join_kernel(even_ref, other_ref, *part_refs):
    step = pl.program_id(0)
    total = (even_ref[0, 0].astype(f32) + other_ref[0, 0].astype(f32)).astype(bf16)
    for at, part_ref in enumerate(part_refs):

        @pl.when(step == at)
        def _(part_ref=part_ref):
            part_ref[...] = total


def join(even, other):
    blocks, sides, *rest = even.shape
    spec = pl.BlockSpec((1, 1, *rest), lambda i: (i // sides, i % sides, 0, 0, 0))
    return pl.pallas_call(
        join_kernel,
        grid=(blocks * sides,),
        in_specs=[spec, spec],
        out_specs=[whole(tuple(rest)) for _ in range(blocks * sides)],
        out_shape=[struct(tuple(rest), bf16) for _ in range(blocks * sides)],
        compiler_params=pltpu.CompilerParams(vmem_limit_bytes=vmem_cap),
        name="join",
    )(even, other)


def lines_kernel(share_ref, message_ref, chan_ref, own_ref, *message_refs):
    own = share_ref.shape[1]
    held = chan_ref.shape[0]
    for line in range(share_ref.shape[0]):
        total = share_ref[line].astype(f32) + message_ref[line * own : (line + 1) * own].astype(f32)
        if line == 0:
            own_ref[...] = total
            continue
        message_refs[line - 1][:own] = total.astype(bf16)
        message_refs[line - 1][own : own + held] = chan_ref[...]
        message_refs[line - 1][own + held :] = message_ref[-held:]


def lines_out(share, message, chan_group):
    lines, own, wide = share.shape
    depth = own + 2 * chan_group.shape[0]
    return pl.pallas_call(
        lines_kernel,
        out_shape=[struct((own, wide))] + [struct((depth, wide), bf16) for _ in range(lines - 1)],
        compiler_params=pltpu.CompilerParams(vmem_limit_bytes=vmem_cap),
        name="lines_out",
    )(share, message, chan_group)


def spread_kernel(own_ref, line_ref, side_ref, mine_ref, *part_refs):
    for line in range(own_ref.shape[0]):
        total = own_ref[line].astype(f32) + line_ref[line].astype(f32) + side_ref[line].astype(f32)
        if line == 0:
            mine_ref[...] = total
        else:
            part_refs[line - 1][...] = total.astype(bf16)


def spread(own, line_x, own_y):
    lines, *rest = own.shape
    return pl.pallas_call(
        spread_kernel,
        out_shape=[struct(tuple(rest))] + [struct(tuple(rest), bf16) for _ in range(lines - 1)],
        compiler_params=pltpu.CompilerParams(vmem_limit_bytes=vmem_cap),
        name="spread",
    )(own, line_x, own_y)


def images_kernel(side_by_side_ref, image_ref):
    features = image_ref.shape[2]
    for image in range(image_ref.shape[1]):
        image_ref[:, image] = side_by_side_ref[:, image * features : (image + 1) * features]


def images_apart(side_by_side, count):
    patches, wide = side_by_side.shape
    step = 56
    return pl.pallas_call(
        images_kernel,
        grid=(-(-patches // step),),
        in_specs=[pl.BlockSpec((step, wide), lambda i: (i, 0))],
        out_specs=pl.BlockSpec((step, count, wide // count), lambda i: (i, 0, 0)),
        out_shape=struct((patches, count, wide // count)),
        compiler_params=pltpu.CompilerParams(vmem_limit_bytes=vmem_cap),
        name="images_apart",
    )(side_by_side)


def unpack_kernel(patches, own_ref, other_ref, token_ref, mixing_ref, gain_ref, shift_ref, patch_ref, hidden_ref, output_ref):
    half = own_ref.shape[1] // 3
    total = own_ref[...].astype(f32) + other_ref[...].astype(f32)
    for which in range(2):
        token_ref[which] = total[:, which * half : which * half + patches]
    pieces = []
    for row in range(own_ref.shape[0]):
        for at in range(2 * half, 3 * half, 128):
            pieces.append(total[row : row + 1, at : at + 128])
    mixers, features = (mixing_ref.shape[0], gain_ref.shape[1])
    at = 0

    def fill(ref, row, width, held):
        nonlocal at
        for first in range(0, held, 128):
            size = min(128, width - first)
            if size > 0 and len(ref.shape) == 1:
                ref[first : first + size] = pieces[at][0, :size]
            elif size > 0:
                ref[row : row + 1, first : first + size] = pieces[at][:, :size]
            at += 1

    fill(mixing_ref, 0, mixers, mixers)
    for ref in (gain_ref, shift_ref):
        for row in range(2):
            fill(ref, row, features, features)
    fill(patch_ref, 0, patches, mixers)
    fill(hidden_ref, 0, hidden_ref.shape[0], hidden_ref.shape[0])
    fill(output_ref, 0, features, features)


def unpack(own, other, patches, mixers, features, hidden_size):
    return pl.pallas_call(
        functools.partial(unpack_kernel, patches),
        out_shape=[
            struct((2, own.shape[0], patches)), struct((mixers,)), struct((2, features)), struct((2, features)),
            struct((patches,)), struct((hidden_size,)), struct((features,)),
        ],
        name="unpack",
    )(own, other)


def score_kernel(parts, shifted, received_ref, query_hbm, score_ref, query_ref, sems):
    rows, _, width = received_ref.shape
    length = query_hbm.shape[0] // parts
    offset = 0
    if shifted:
        place = place_of()
        offset = pl.multiple_of(lax.rem(place * query_hbm.shape[0], width), 16)
        query_ref[0:width] = jnp.zeros((width, query_ref.shape[1]), bf16)
        last = query_hbm.shape[0] // width * width
        query_ref[last:] = jnp.zeros((rows * width - last, query_ref.shape[1]), bf16)
    copies = [
        pltpu.make_async_copy(
            query_hbm.at[pl.ds(part * length, length)],
            query_ref.at[pl.ds(offset + part * length, length)],
            sems.at[part],
        )
        for part in range(parts)
    ]
    for copy in copies:
        copy.start()
    waited = 0
    total = None
    for row in range(rows):
        while waited < parts and waited * length < (row + 1) * width:
            copies[waited].wait()
            waited += 1
        part = dot(received_ref[row], query_ref[row * width : (row + 1) * width])
        total = part if total is None else total + part
    score_ref[...] = total


def scores(received, queries_t):
    rows, count, width = received.shape
    share, asked = queries_t.shape
    shifted = share != rows * width
    parts = 7 if share % 112 == 0 else 1
    return pl.pallas_call(
        functools.partial(score_kernel, parts, shifted),
        in_specs=[pl.BlockSpec(memory_space=pltpu.VMEM), pl.BlockSpec(memory_space=pl.ANY)],
        out_specs=pl.BlockSpec(memory_space=pltpu.VMEM),
        out_shape=struct((count, asked)),
        scratch_shapes=[pltpu.VMEM((rows * width, asked), bf16), pltpu.SemaphoreType.DMA((parts,))],
        compiler_params=pltpu.CompilerParams(vmem_limit_bytes=vmem_cap),
        name="scores",
    )(received, queries_t)


def score_parts_of(partial_scores, groups, count):
    partial_scores = partial_scores.reshape(groups, count, -1)
    return lax.all_to_all(partial_scores, dp_axes, split_axis=0, concat_axis=0, tiled=True)


def swap(array, axis, code=1):
    devices = lax.axis_size(axis)
    return lax.ppermute(array, axis, [(place, place ^ code) for place in range(devices)])


def swap_both(array, line_code, side_code):
    columns, sides = (lax.axis_size("line"), lax.axis_size("side"))
    pairs = [
        (line * sides + side, (line ^ line_code) * sides + (side ^ side_code))
        for line in range(columns)
        for side in range(sides)
    ]
    return lax.ppermute(array, dp_axes, pairs)


def by_code(parts, place):
    step = 1
    while step < parts.shape[0]:
        pairs = parts.reshape(-1, 2, step, *parts.shape[1:])
        turned = jnp.concatenate([pairs[:, 1:], pairs[:, :1]], axis=1)
        parts = jnp.where((place & step) > 0, turned, pairs).reshape(parts.shape)
        step *= 2
    return parts


def together(*arrays):
    return lax.optimization_barrier(arrays)


def added(left, right):
    return (left.astype(f32) + right.astype(f32)).astype(bf16)


def body(
    images,
    kept_mask,
    pooled_grad,
    token_weights,
    norm_gain,
    norm_bias,
    mixing_bias,
    patch_bias,
    widening,
    narrowing,
    hidden_bias,
    output_bias,
    width_maps,
    hidden_maps,
    queries,
):
    count, patches, features = images.shape
    mixers = mixing_bias.shape[0]
    rank = width_maps.shape[2]
    hidden_size = hidden_bias.shape[0]
    columns = lax.axis_size("line")
    sides = lax.axis_size("side")
    groups = columns * sides
    group = lax.axis_index(dp_axes)
    share, asked = (queries.shape[1], queries.shape[0])
    own_hidden = widening.shape[1]
    own_width = narrowing.shape[1]
    by_hand = groups <= 8 and widening.shape[0] % 16 == 0
    chunks = [(0, count // 2), (count // 2, count)]
    rows = -(-patches // 8) * 8
    extra = rows - patches
    cut = columns // 2

    widen_part = widening.astype(bf16)
    token_part = jnp.pad(jnp.swapaxes(token_weights, 1, 2).astype(bf16), ((0, 0), (0, 0), (0, extra)))
    narrow_part = jnp.swapaxes(narrowing, 0, 1).astype(bf16)
    keep_f = kept_mask.astype(f32)
    kept_count = jnp.sum(keep_f, axis=1, keepdims=True)
    grad_rows = pooled_grad / kept_count
    grad_low = grad_rows.astype(bf16)
    maps_own = jnp.swapaxes(hidden_maps, 1, 2).reshape(2 * rank, own_hidden)
    width_maps = jnp.swapaxes(width_maps, 1, 2)
    keep = jnp.pad(keep_f, ((0, 0), (0, extra)))[:, :, None]
    column = jnp.concatenate([mixing_bias, jnp.pad(patch_bias, (0, extra))])[:, None]
    bias_row = hidden_bias[None, :]
    output_sum = jnp.sum(grad_low.astype(f32) * kept_count, axis=0, keepdims=True)
    if by_hand:
        map_rows = 2 * rank // groups
        maps_part = lax.dynamic_slice_in_dim(maps_own, group * map_rows, map_rows)
        piece = jnp.concatenate([widen_part, maps_part])
        depth = piece.shape[0]
        layout = (depth, widen_part.shape[0], widen_part.shape[0], map_rows)
        token_line = jnp.stack([token_part] + [swap(token_part, "line", code) for code in range(1, columns)])
        grad_pair = jnp.concatenate([grad_low, swap(grad_low, "core")])
        piece, token_line, grad_pair = together(piece, token_line, grad_pair)
        tokens = [token_line, swap(token_line, "side")]
        widen_z = [piece] + [swap(piece, "line", code) for code in range(1, columns)]
        grad_group = jnp.concatenate([grad_pair, swap(grad_pair, "far")])
        grad_near = jnp.concatenate([grad_group, swap(grad_group, "side")])
        line_codes = tuple(sides * code for code in range(columns))
        side_codes = tuple(code ^ 1 for code in line_codes)
        token_codes = (line_codes, side_codes)
        codes = tuple(((side, at), sides * at ^ side) for side in range(sides) for at in range(columns))
        share_shape = (sides, columns, *widening.shape)
    else:
        tokens = [lax.all_gather(token_part, dp_axes, axis=1, tiled=True)[None]]
        token_codes = ((None,),)
        piece = jnp.concatenate([lax.all_gather(widen_part, dp_axes, axis=0, tiled=True), maps_own])
        layout = (piece.shape[0], features, features, 2 * rank)
        piece_x = swap(piece, "far")
        pieces = [piece, swap(piece, "core"), piece_x, swap(piece_x, "core")]
        spans = tuple(((None,), block * own_hidden) for block in range(4))
        codes = (((slice(None),), None),)
        share_shape = (features, own_hidden)

    def forward(chunk):
        out = token_forward(
            images, keep, tokens, token_codes, norm_gain, norm_bias, column, width_maps, *chunks[chunk]
        )
        return list(out)

    forwards = [forward(0)]
    if by_hand:
        narrow_part = jnp.concatenate([narrow_part, grad_near[: 4 * count]])
        forwards[0][:] = together(*forwards[0], *widen_z, narrow_part, grad_near, *tokens)
        widen_z = forwards[0][7 : 7 + columns]
        narrow_part, grad_near, *tokens = forwards[0][7 + columns :]
        forwards[0] = forwards[0][:7]
        widen_line = jnp.concatenate(widen_z)
        widen_y, widen_x = (swap(widen_line, "side"), swap(widen_line, "far"))
        narrow_z = [narrow_part] + [swap(narrow_part, "line", code) for code in range(1, columns)]
        forwards.append(forward(1))
        forwards[1][:] = together(*forwards[1], widen_y, widen_x, *narrow_z)
        widen_y, widen_x, *narrow_z = forwards[1][7:]
        forwards[1] = forwards[1][:7]
        narrow_line = jnp.concatenate(narrow_z)
        half = widen_line.shape[0] // 2
        widen_xy, widen_yx = (swap(widen_y[:half], "far"), swap(widen_x[half:], "side"))
        back_part, back_y = back_sent(grad_near, narrow_line, own_width, columns, sides)
        back_part = added(back_part, swap(back_y, "side"))
        narrow_line, widen_xy, widen_yx = together(narrow_line, widen_xy, widen_yx)
        narrow_y = swap(narrow_line, "side")
        pieces = [widen_line, widen_y, widen_x, widen_xy, widen_yx]
        pieces = pieces + [swap(piece, "core") for piece in pieces]
        near = [(line_codes, 0), (side_codes, 0), (line_codes, 2), (side_codes[:cut], 2), (side_codes[cut:], 2)]
        spans = tuple((codes, block * own_hidden) for codes, block in near) + tuple(
            (codes, (block + 1) * own_hidden) for codes, block in near
        )
    else:
        grad_pair = jnp.concatenate([grad_low, swap(grad_low, "core")])
        grad_group = jnp.concatenate([grad_pair, swap(grad_pair, "far")])
        narrow_t = lax.all_gather(narrow_part, dp_axes, axis=0, tiled=True)
        grad_all = lax.all_gather(grad_group, dp_axes, axis=0, tiled=True)
        grad_all = lax.dynamic_slice_in_dim(grad_all, group * own_width, own_width, 1)
        back_part = dot(grad_group, narrow_t).astype(bf16)
        forwards.append(forward(1))
    back_part = back_part.reshape(4, count, own_hidden)
    back_x = swap(back_part[2:], "far")
    back_core = swap(jnp.stack([back_part[1], back_x[1]]), "core")
    back_rows = jnp.concatenate([back_part[0], back_core[0], back_x[0], back_core[1]], axis=1)

    row_ends = [-(-share * (place + 1) // mixers) for place in range(groups)]
    row_starts = tuple(share * place // mixers for place in range(groups))
    part_rows = -(-max(end - start for start, end in zip(row_starts, row_ends)) // 8) * 8
    queries_t = jnp.swapaxes(queries, 0, 1)
    if share % 16 != 0:
        offset = lax.rem(group * share, mixers)
        queries_t = lax.dynamic_update_slice(
            jnp.zeros((part_rows * mixers, asked), bf16), queries_t, (offset, jnp.int32(0))
        )

    def channel_chunk(chunk, second, left, before):
        first, last = chunks[chunk]
        number = last - first
        return channel(
            second.reshape(number * rows, features), keep, left.reshape(number * rows, rank),
            back_rows, bias_row, grad_low, width_maps, pieces, spans, layout, codes, share_shape, before, mixers,
            chunk, first, last, last == count,
        )

    def backward(chunk, grad, saved, adapters, hidden_sum, before):
        first, last = chunks[chunk]
        hidden, slope, _, normed, inverse = saved[:5]
        image_grad, *parts, sums, token_total, token_share = token_backward(
            images, keep, grad_rows[:, None, :], grad.reshape(last - first, rows, features), normed, inverse, hidden,
            slope, tokens, token_codes, norm_gain, norm_bias, adapters,
            hidden_sum, output_sum, before, row_starts, part_rows, columns,
            first, last,
        )
        return image_grad, parts, sums, token_total, token_share

    second_grad, chan_first, hidden_sum, adapters, shares_first, widen_full, maps_full = channel_chunk(
        0, forwards[0][2], forwards[0][6], None
    )
    if by_hand:
        second_grad, chan_first, hidden_sum, adapters, shares_first, widen_full, maps_full, narrow_y = together(
            second_grad, chan_first, hidden_sum, adapters, shares_first, widen_full, maps_full, narrow_y
        )
    image_grad_first, parts, sums, token_total, _ = backward(
        0, second_grad, forwards[0], adapters, hidden_sum, None
    )
    second, shares_first, *parts = together(forwards[1][2], shares_first, *parts)
    received_first = lax.all_to_all(parts[0], dp_axes, split_axis=0, concat_axis=0, tiled=True)


    second_grad, chan_second, hidden_sum, adapters, *shares = channel_chunk(
        1, second, forwards[1][6], (widen_full, maps_full, hidden_sum, shares_first)
    )
    second_grad, chan_second, hidden_sum, adapters, *shares, received_first = together(
        second_grad, chan_second, hidden_sum, adapters, *shares, received_first
    )
    share_core = swap(shares[1], "core")
    chan_pooled = jnp.concatenate([chan_first, chan_second]).astype(bf16).reshape(count, 4, own_hidden)
    chan_x = swap(chan_pooled[:, 2:], "far")
    image_grad, parts, sums, _, token_share = backward(
        1, second_grad, forwards[1], adapters, hidden_sum, (token_total, sums, image_grad_first)
    )
    image_grad, parts[0], sums, token_share, chan_x, share_core = together(
        image_grad, parts[0], sums, token_share, chan_x, share_core
    )
    received_second = lax.all_to_all(parts[0], dp_axes, split_axis=0, concat_axis=0, tiled=True)
    chan_core = swap(jnp.stack([chan_pooled[:, 1], chan_x[:, 1]]), "core")
    chan_group = jnp.concatenate([chan_pooled[:, 0], chan_core[0], chan_x[:, 0], chan_core[1]])

    own_mixers, wide = token_share.shape[2:]
    lines = features // mixers
    if by_hand:
        own_line, own_side, far_line, far_side = join(shares[0], share_core)
        message = jnp.concatenate([token_share[1].reshape(-1, wide), chan_group])
        own_line, own_side, far_line, far_side, message = together(own_line, own_side, far_line, far_side, message)
        far_x = swap(far_side, "far")
        message = swap(message, "side")
        image_grad = images_apart(image_grad, count)
        out_own, out_sent = pooled_parts(chan_group, narrow_line, narrow_y, own_width, columns)
        far_x, far_line, image_grad, message, out_own, out_sent = together(
            far_x, far_line, image_grad, message, out_own, out_sent
        )
        own_y = swap(added(own_side, far_x), "side")
        line_x = swap(far_line, "far")
        token_total, *messages = lines_out(token_share[0], message, chan_group)
        received_second, *messages = together(received_second, *messages)
        messages = [swap(part, "line", code) for code, part in enumerate(messages, 1)]
        arrived = jnp.concatenate([received_first, received_second], axis=1)
        arrived = jnp.moveaxis(arrived, 2, 0).reshape(part_rows, groups * count, mixers)
        own_y, line_x, arrived = together(own_y, line_x, arrived)
        widening_grad, *widen_sums = spread(own_line, line_x, own_y)
        arrived, *widen_sums = together(arrived, *widen_sums)
        widen_sums = [swap(part, "line", code) for code, part in enumerate(widen_sums, 1)]
        partial_scores = scores(arrived, queries_t)
        _, out_sent, *messages = together(partial_scores, out_sent, *messages)
        image_grad = jnp.swapaxes(image_grad, 0, 1)
        total = token_total
        for part in messages:
            total = total + part[:own_mixers].astype(f32)
        total = total.astype(bf16)
        total_x = swap(total, "far")
        out_x = swap(out_sent, "far")
        narrowing_grad = narrow_sums(
            narrow_line, narrow_y, chan_group, [message, *messages], own_width, columns
        ).T
        total_x, out_x, narrowing_grad, *widen_sums = together(total_x, out_x, narrowing_grad, *widen_sums)
        total = added(total, total_x)
        token_grad, mixing_grad, gain_grad, shift_grad, patch_grad, hidden_grad, output_grad = unpack(
            total, swap(total, "core"), patches, mixers, features, hidden_size
        )
        score_parts = score_parts_of(partial_scores, groups, count)
        for widen_sum in widen_sums:
            widening_grad = widening_grad + widen_sum.astype(f32)
    else:
        narrowing_grad = None
        image_grad = jnp.swapaxes(image_grad.reshape(patches, count, features), 0, 1)
        arrived = jnp.concatenate([received_first, received_second], axis=1)
        arrived = jnp.moveaxis(arrived, 2, 0).reshape(part_rows, groups * count, mixers)
        score_parts = score_parts_of(scores(arrived, queries_t), groups, count)
        both = added(shares[0], share_core)
        own, far = (both[0], both[1])
        own = added(own, jnp.concatenate([swap(far[:1], "far"), swap(far[1:], "far")]))
        widening_grad = lax.psum_scatter(own, dp_axes, scatter_dimension=0, tiled=True).astype(f32)
        chan_all = lax.all_gather(chan_group, dp_axes, axis=0, tiled=True)
        summed = jnp.swapaxes(token_share, 0, 1).reshape(groups, own_mixers, wide)
        summed = by_code(summed, group).astype(f32)
        total = lax.psum(lax.psum_scatter(summed, dp_axes, scatter_dimension=0, tiled=True)[0], ("far", "core"))
        half = wide // 3
        sums, more = lax.psum((sums, jnp.concatenate([hidden_sum, output_sum], axis=1)[0]), dp_axes + ("far", "core"))
        token_grad = jnp.stack([total[:, :patches], total[:, half : half + patches]])
        mixing_grad = sums[0]
        gain_grad = sums[1 : 1 + 2 * lines].reshape(2, features)
        shift_grad = sums[1 + 2 * lines : 1 + 4 * lines].reshape(2, features)
        patch_grad = sums[1 + 4 * lines, :patches]
        hidden_grad, output_grad = (more[:hidden_size], more[hidden_size : hidden_size + features])
    token_grad = jnp.swapaxes(token_grad, 1, 2)
    if narrowing_grad is None:
        narrowing_grad = dot_tn(grad_all, chan_all).T

    if not by_hand:
        out_part = dot_nt(chan_group, narrow_t)
        out_own, out_x = (out_part[: 2 * count], swap(out_part[2 * count :], "far"))
    out_pair = out_own + out_x
    chan_out = out_pair[:count] + swap(out_pair[count:], "core")
    score_parts, token_grad, narrowing_grad, chan_out = together(score_parts, token_grad, narrowing_grad, chan_out)
    influence = jnp.sum(score_parts, axis=0)
    pooled_in = jnp.concatenate([forwards[0][5][:, 0], forwards[1][5][:, 0]])
    pooled = (pooled_in + chan_out) / kept_count + output_bias

    return (
        pooled,
        image_grad,
        token_grad,
        gain_grad,
        shift_grad,
        mixing_grad,
        patch_grad,
        widening_grad,
        narrowing_grad,
        hidden_grad,
        output_grad,
        influence,
    )


def solution(mesh):
    groups = mesh.shape["dp"]
    models = mesh.shape["mp"]
    mesh = Mesh(mesh.devices.reshape(groups // 2, 2, models // 2, 2), ("line", "side", "far", "core"))
    dp = ("line", "side")
    mp = ("far", "core")
    every = dp + mp
    placed = (
        P(every, None, None),
        P(every, None),
        P(every, None),
        P(None, None, dp),
        P(),
        P(),
        P(),
        P(),
        P(dp, mp),
        P(mp, dp),
        P(),
        P(),
        P(),
        P(None, mp, None),
        P(None, dp),
    )
    return jax.shard_map(
        body,
        mesh=mesh,
        in_specs=placed,
        out_specs=(
            P(every, None),
            P(every, None, None),
            P(None, None, dp),
            P(),
            P(),
            P(),
            P(),
            P(dp, mp),
            P(mp, dp),
            P(),
            P(),
            P(every, None),
        ),
        check_vma=False,
    )
```

```python
import functools

import jax
import jax.numpy as jnp
from jax import lax
from jax.experimental import pallas as pl
from jax.experimental.pallas import tpu as pltpu
from jax.sharding import Mesh
from jax.sharding import PartitionSpec as P

norm_eps = 1e-06
bf16 = jnp.bfloat16
f32 = jnp.float32
vmem_cap = 58 * 1024 * 1024
dp_axes = ("line", "side")


def dot(left, right):
    return jnp.dot(left, right, preferred_element_type=f32)


def dot_nt(left, right):
    return lax.dot_general(left, right, (((1,), (1,)), ((), ())), preferred_element_type=f32)


def dot_tn(left, right):
    return lax.dot_general(left, right, (((0,), (0,)), ((), ())), preferred_element_type=f32)


def exact_tn(left, right):
    return lax.dot_general(
        left, right, (((0,), (0,)), ((), ())), precision=lax.Precision.HIGHEST, preferred_element_type=f32
    )


def gelu_pair(values):
    cumulative = 0.5 + 0.5 * lax.erf(values * 0.7071067811865476)
    density = jnp.exp2(values * values * -0.7213475204444817) * 0.3989422804014327
    return (values * cumulative, cumulative + values * density)


def normalize(values):
    average = jnp.mean(values, axis=-1, keepdims=True)
    centered = values - average
    spread = jnp.mean(centered * centered, axis=-1, keepdims=True)
    inverse = lax.rsqrt(spread + norm_eps)
    return (centered * inverse, inverse)


def norm_back(grad_norm, normed, inverse):
    first_mean = jnp.mean(grad_norm, axis=-1, keepdims=True)
    second_mean = jnp.mean(grad_norm * normed, axis=-1, keepdims=True)
    return inverse * (grad_norm - first_mean - normed * second_mean)


def whole(shape):
    return pl.BlockSpec(shape, lambda i: (0,) * len(shape))


def each(shape, first=0):
    return pl.BlockSpec((1,) + shape, lambda i: (i + first,) + (0,) * len(shape))


def struct(shape, dtype=f32):
    return jax.ShapeDtypeStruct(shape, dtype)


def place_of():
    return lax.axis_index("line") * lax.axis_size("side") + lax.axis_index("side")


def assemble_tokens(piece_refs, codes, token_ref):
    place = place_of()
    for piece_ref, own_codes in zip(piece_refs, codes):
        own = piece_ref.shape[2]
        for at, code in enumerate(own_codes):
            start = 0 if code is None else pl.multiple_of((place ^ code) * own, own)
            for which in range(2):
                token_ref[which, pl.ds(start, own)] = piece_ref[at, which]


def token_forward_kernel(
    codes, image_ref, keep_ref, gain_ref, shift_ref, column_ref, width_ref, *refs,
):
    piece_refs, refs = (refs[: len(codes)], refs[len(codes) :])
    hidden_ref, slope_ref, second_ref, normed_ref, inverse_ref, pooled_ref, left_ref, token_ref, padded_ref = refs
    mixers = token_ref.shape[1]
    patches = image_ref.shape[1]

    @pl.when(pl.program_id(0) == 0)
    def _():
        assemble_tokens(piece_refs, codes, token_ref)
        padded_ref[patches:] = jnp.zeros((padded_ref.shape[0] - patches, padded_ref.shape[1]), f32)

    padded_ref[:patches] = image_ref[0].astype(f32)
    inputs = padded_ref[...]
    keep = keep_ref[0]
    normed_one, _ = normalize(inputs)
    masked = ((normed_one * gain_ref[0:1] + shift_ref[0:1]) * keep).astype(bf16)
    mixed = dot(token_ref[0], masked) + column_ref[:mixers]
    hidden, slope = gelu_pair(mixed)
    hidden = hidden.astype(bf16)
    hidden_ref[0] = hidden
    slope_ref[0] = slope.astype(bf16)
    residual = inputs + dot_tn(token_ref[1], hidden) + column_ref[mixers:]
    pooled_ref[0] = jnp.sum(residual * keep, axis=0, keepdims=True)
    normed_two, inverse_two = normalize(residual)
    second = (normed_two * gain_ref[1:2] + shift_ref[1:2]).astype(bf16)
    second_ref[0] = second
    normed_ref[0] = normed_two.astype(bf16)
    inverse_ref[0] = inverse_two
    left_ref[0] = dot_nt(second, width_ref[0])


def token_forward(images, keep, tokens, codes, norm_gain, norm_bias, column, width_maps, first, last):
    count = last - first
    _, patches, features = images.shape
    rows = keep.shape[1]
    mixers = column.shape[0] - rows
    rank = width_maps.shape[1]
    return pl.pallas_call(
        functools.partial(token_forward_kernel, codes),
        grid=(count,),
        in_specs=[
            each((patches, features), first), each((rows, 1), first),
            whole((2, features)), whole((2, features)), whole((mixers + rows, 1)), whole((2, rank, features)),
        ]
        + [whole(piece.shape) for piece in tokens],
        out_specs=[
            each((mixers, features)), each((mixers, features)), each((rows, features)), each((rows, features)),
            each((rows, 1)), each((1, features)), each((rows, rank)),
        ],
        out_shape=[
            struct((count, mixers, features), bf16), struct((count, mixers, features), bf16),
            struct((count, rows, features), bf16), struct((count, rows, features), bf16),
            struct((count, rows, 1)), struct((count, 1, features)), struct((count, rows, rank)),
        ],
        scratch_shapes=[pltpu.VMEM((2, mixers, rows), bf16), pltpu.VMEM((rows, features), f32)],
        compiler_params=pltpu.CompilerParams(vmem_limit_bytes=vmem_cap),
        name="token_forward",
    )(images, keep, norm_gain, norm_bias, column, width_maps, *tokens)


def piece_copies(piece_refs, widen_ref, maps_ref, sems, spans, layout):
    depth, wide_rows, map_at, map_rows = layout
    copies = []
    place = place_of()
    for at, (piece_ref, (codes, column)) in enumerate(zip(piece_refs, spans)):
        cols = pl.ds(column, piece_ref.shape[1])
        for part, code in enumerate(codes):
            for which, (target, first, rows) in enumerate(((widen_ref, 0, wide_rows), (maps_ref, map_at, map_rows))):
                start = 0 if code is None else pl.multiple_of((place ^ code) * rows, rows)
                copy = pltpu.make_async_copy(
                    piece_ref.at[pl.ds(part * depth + first, rows)],
                    target.at[pl.ds(start, rows), cols],
                    sems.at[at, part, which],
                )
                copies.append((column, copy))
    return copies


def channel_kernel(
    spans, layout, codes, first, resumed, final,
    second_ref, keep_ref, left_ref, back_ref, bias_ref, rows_ref, width_ref, *refs,
):
    if resumed:
        widen_ref, maps_ref, sum_before_ref, before_ref, *refs = refs
    else:
        piece_refs, refs = (refs[: len(spans)], refs[len(spans) :])
    grad_ref, pooled_ref, sum_ref, adapter_ref, *refs = refs
    share_refs, refs = (refs[: 2 if final else 1], refs[2 if final else 1 :])
    if resumed:
        total_ref, right_ref, out_ref, pair_ref, low_ref = refs
    else:
        widen_out, maps_out, widen_ref, maps_ref, total_ref, right_ref, out_ref, pair_ref, low_ref, sems, out_sems = refs
    step = pl.program_id(0)
    steps = pl.num_programs(0)
    count = pooled_ref.shape[0]
    total_rows, features = second_ref.shape
    rows = total_rows // count
    rank = left_ref.shape[1]
    own = bias_ref.shape[1] // 4
    model = lax.axis_index("far") * lax.axis_size("core") + lax.axis_index("core")
    second = second_ref[...]
    keep = keep_ref[...].reshape(total_rows, 1)
    if not resumed:
        copies = piece_copies(piece_refs, widen_ref, maps_ref, sems, spans, layout)
        kept = [
            pltpu.make_async_copy(widen_ref, widen_out, out_sems.at[0]),
            pltpu.make_async_copy(maps_ref, maps_out, out_sems.at[1]),
        ]

    @pl.when(step == 0)
    def _():
        if resumed:
            sum_ref[...] = sum_before_ref[...]
        else:
            for _, copy in copies:
                copy.start()
            for column, copy in copies:
                if column < 2 * own:
                    copy.wait()
            sum_ref[...] = jnp.zeros_like(sum_ref)
        right_ref[...] = jnp.zeros_like(right_ref)
        out_ref[...] = jnp.zeros_like(out_ref)
        grad_ref[...] = jnp.zeros_like(grad_ref)

    if not resumed:

        @pl.when(step > 0)
        def _():
            for column, copy in copies:
                if column >= 2 * own:
                    copy.wait()
            for copy in kept:
                copy.start()

    for half in range(2):
        cols = slice(half * own, (half + 1) * own)
        wide = cols if resumed else pl.ds(pl.multiple_of((2 * step + half) * own, own), own)
        widen = widen_ref[:, wide]
        bias_at = pl.multiple_of((model ^ (2 * step + half)) * own, own)
        hidden_sums = jnp.zeros((1, own), f32)
        number = 2 if count % 2 == 0 else count
        for at in range(0, count, number):
            span = slice(at * rows, (at + number) * rows)
            pre = dot(second[span], widen) + bias_ref[:, pl.ds(bias_at, own)]
            hidden, slope = gelu_pair(pre)
            hidden = (hidden.astype(bf16).astype(f32) * keep[span]).reshape(number, rows, own)
            pooled_ref[at : at + number, cols] = jnp.sum(hidden, axis=1)
            back = back_ref[first + at : first + at + number, cols].astype(f32)[:, None, :]
            pre_grad = (slope * keep[span]).reshape(number, rows, own) * back
            pre_grad = pre_grad.reshape(number * rows, own).astype(bf16)
            low_ref[span] = pre_grad
            hidden_sums = hidden_sums + jnp.sum(pre_grad.astype(f32), axis=0, keepdims=True)
        sum_ref[:, pl.ds(bias_at, own)] += hidden_sums
        pooled_hidden = pooled_ref[:, cols]
        pre_grad = low_ref[...]
        grad_ref[...] += dot_nt(pre_grad, widen)
        right_ref[...] += dot_nt(pre_grad, maps_ref[:rank, wide])
        out_ref[...] += dot_nt(pooled_hidden.astype(bf16), maps_ref[rank:, wide])
        share = dot_tn(second, pre_grad)
        if resumed:
            share = share + before_ref[:, cols].astype(f32)
        if not final:
            share_refs[0][:, cols] = share.astype(bf16)
            continue
        total_ref[...] = share
        place = place_of()
        part_rows = share_refs[half].shape[-2]
        for index, code in codes:
            start = 0 if code is None else pl.multiple_of((place ^ code) * part_rows, part_rows)
            share_refs[half][(0, *index)] = total_ref[pl.ds(start, part_rows)].astype(bf16)

    @pl.when(step == steps - 1)
    def _():
        if not resumed:
            for copy in kept:
                copy.wait()
        outer = dot_nt(rows_ref[first : first + count], width_ref[1])
        lines = adapter_ref.shape[2] // rank
        pair_ref[2 * rank :] = jnp.zeros((pair_ref.shape[0] - 2 * rank, rank), f32)
        for image in range(count):
            span = slice(image * rows, (image + 1) * rows)
            pair_ref[:rank] = exact_tn(left_ref[span], right_ref[span])
            pair_ref[rank : 2 * rank] = exact_tn(out_ref[image : image + 1], outer[image : image + 1])
            adapter_ref[image] = jnp.concatenate(
                [pair_ref[pl.ds(line, adapter_ref.shape[1], stride=lines)] for line in range(lines)], axis=1
            ).astype(bf16)


def channel(
    second, keep, left, back_rows, bias_row, grad_low, width_maps, pieces, spans, layout, codes, share_shape, before,
    mixers, chunk, first, last, final,
):
    count = last - first
    total_rows, features = second.shape
    hidden_size = bias_row.shape[1]
    rank = left.shape[1]
    held = back_rows.shape[0]
    lines = mixers // rank
    adapter_rows = -(-2 * rank // lines)
    once = pl.Buffered(1)
    resumed = before is not None
    anywhere = pl.BlockSpec(memory_space=pl.ANY)
    wide = hidden_size // 2

    def columns(rows):
        return pl.BlockSpec((rows, wide), lambda i: (0, i))

    if final:
        share_specs = [
            pl.BlockSpec((1, *share_shape), lambda i: (i,) + (0,) * len(share_shape)) for _ in range(2)
        ]
        share_out = [struct((2, *share_shape), bf16) for _ in range(2)]
    else:
        share_specs = [columns(features)]
        share_out = [struct((features, hidden_size), bf16)]
    scratch = [
        pltpu.VMEM((features, hidden_size // 4), f32),
        pltpu.VMEM((total_rows, rank), f32),
        pltpu.VMEM((count, rank), f32),
        pltpu.VMEM((adapter_rows * lines, rank), f32),
        pltpu.VMEM((total_rows, hidden_size // 4), bf16),
    ]
    if resumed:
        matrix_specs = [columns(features), columns(2 * rank), whole((1, hidden_size)), columns(features)]
        matrices = before
    else:
        matrix_specs = [anywhere] * len(pieces)
        matrices = pieces
        share_specs = share_specs + [anywhere, anywhere]
        share_out = share_out + [struct((features, hidden_size), bf16), struct((2 * rank, hidden_size), bf16)]
        scratch = [
            pltpu.VMEM((features, hidden_size), bf16), pltpu.VMEM((2 * rank, hidden_size), bf16), *scratch,
            pltpu.SemaphoreType.DMA((len(spans), max(len(span[0]) for span in spans), 2)),
            pltpu.SemaphoreType.DMA((2,)),
        ]
    return pl.pallas_call(
        functools.partial(channel_kernel, spans, layout, codes, first, resumed, final),
        grid=(2,),
        in_specs=[
            whole((total_rows, features)), pl.BlockSpec((count, total_rows // count, 1), lambda i: (chunk, 0, 0)),
            whole((total_rows, rank)), columns(held),
            whole((1, hidden_size)), whole((held, features)), whole((2, rank, features)),
        ]
        + matrix_specs,
        out_specs=[
            whole((total_rows, features)), columns(count), whole((1, hidden_size)), whole((count, adapter_rows, mixers)),
        ]
        + share_specs,
        out_shape=[
            struct((total_rows, features)), struct((count, hidden_size)), struct((1, hidden_size)),
            struct((count, adapter_rows, mixers), bf16),
        ]
        + share_out,
        scratch_shapes=scratch,
        compiler_params=pltpu.CompilerParams(vmem_limit_bytes=vmem_cap),
        name="channel",
    )(
        second, keep, left, back_rows, bias_row, grad_low, width_maps, *matrices
    )


def token_backward_kernel(
    codes, resumed, patches, row_starts,
    image_ref, keep_ref, row_ref, grad_ref, normed_ref, inverse_ref, hidden_ref, slope_ref,
    gain_ref, shift_ref, adapter_ref, hidden_sum_ref, output_sum_ref, *refs,
):
    piece_refs, refs = (refs[: len(codes)], refs[len(codes) :])
    if resumed:
        total_before_ref, sums_before_ref, _, *refs = refs
    image_grad_ref, parts_ref, sums_ref, total_ref, share_ref, vector_ref, token_ref, padded_ref = refs
    step = pl.program_id(0)
    steps = pl.num_programs(0)
    rows, features = padded_ref.shape
    mixers = hidden_ref.shape[1]
    keep = keep_ref[0]
    grad = grad_ref[0]

    @pl.when(step == 0)
    def _():
        if resumed:
            total_ref[...] = total_before_ref[...]
            sums_ref[...] = sums_before_ref[...]
        else:
            total_ref[...] = jnp.zeros_like(total_ref)
            sums_ref[...] = jnp.zeros_like(sums_ref)
        vector_ref[...] = jnp.zeros_like(vector_ref)
        padded_ref[patches:] = jnp.zeros((rows - patches, features), f32)
        assemble_tokens(piece_refs, codes, token_ref)

    normed_two = normed_ref[0].astype(f32)
    residual_grad = keep * row_ref[0] + norm_back(grad * gain_ref[1:2], normed_two, inverse_ref[0])
    gain_two = jnp.sum(grad * normed_two, axis=0, keepdims=True)
    shift_two = jnp.sum(grad, axis=0, keepdims=True)
    low = residual_grad.astype(bf16)
    outward_grad = dot_nt(low, hidden_ref[0])
    mixed_grad = (dot(token_ref[1], low) * slope_ref[0].astype(f32)).astype(bf16)
    ones = jnp.ones((8, features), bf16)
    mixing = dot_nt(ones, mixed_grad)[0:1]
    patch_sum = dot_nt(ones, low)[0:1]
    padded_ref[:patches] = image_ref[0].astype(f32)
    normed_one, inverse_one = normalize(padded_ref[...])
    masked = ((normed_one * gain_ref[0:1] + shift_ref[0:1]) * keep).astype(bf16)
    inward_grad = dot_nt(masked, mixed_grad)
    first_grad = dot_tn(token_ref[0], mixed_grad) * keep
    gain_one = jnp.sum(first_grad * normed_one, axis=0, keepdims=True)
    shift_one = jnp.sum(first_grad, axis=0, keepdims=True)
    image_grad = residual_grad + norm_back(first_grad * gain_ref[0:1], normed_one, inverse_one)
    image_grad_ref[...] = image_grad[:patches]
    lines = [mixing]
    for row in (gain_one, gain_two, shift_one, shift_two):
        for at in range(0, features, mixers):
            lines.append(row[:, at : at + mixers])
    small = jnp.concatenate(lines, axis=0)
    adapter_at = 2 * patches + len(lines)
    vector_ref[0:patches] = inward_grad[:patches]
    vector_ref[patches : 2 * patches] = outward_grad[:patches]
    vector_ref[2 * patches : adapter_at] = small
    vector_ref[adapter_at : adapter_at + adapter_ref.shape[1]] = adapter_ref[0].astype(f32)
    part_rows = parts_ref.shape[2]
    for place, start in enumerate(row_starts):
        parts_ref[place, 0] = vector_ref[start : start + part_rows].astype(bf16)
    total_ref[0] += inward_grad
    total_ref[1] += outward_grad
    sums_ref[0 : len(lines)] += small
    sums_ref[len(lines) : len(lines) + 1, 0:rows] += patch_sum

    @pl.when(step == steps - 1)
    def _():
        sides, columns, own, wide = share_ref.shape
        half = wide // 3
        line, side = (lax.axis_index("line"), lax.axis_index("side"))
        turned = [total_ref[which].T.astype(bf16) for which in range(2)]
        sums = [sums_ref[row : row + 1, at : at + 128] for row in range(sums_ref.shape[0]) for at in range(0, mixers, 128)]
        for ref in (hidden_sum_ref, output_sum_ref):
            sums += [ref[:, at : at + 128] for at in range(0, ref.shape[1], 128)]
        per_row = half // 128
        depth = len(sums) // per_row
        sums = [jnp.concatenate(sums[at::per_row], axis=0) for at in range(per_row)]
        sums = jnp.concatenate(sums, axis=1).astype(bf16)
        for place in range(sides * columns):
            at = ((place % sides) ^ side, (place // sides) ^ line)
            for which in range(2):
                part = turned[which][place * own : (place + 1) * own]
                share_ref[at[0], at[1], :, which * half : which * half + rows] = part
            if depth <= own:
                share_ref[at[0], at[1], 0:depth, 2 * half :] = sums


def token_backward(
    images, keep, grad_rows, grad, normed, inverse, hidden, slope, tokens, codes, norm_gain, norm_bias, adapters, hidden_sum,
    output_sum, before, row_starts, part_rows, columns, first, last,
):
    count = last - first
    _, patches, features = images.shape
    rows = keep.shape[1]
    mixers = hidden.shape[1]
    adapter_rows = adapters.shape[1]
    groups = len(row_starts)
    resumed = before is not None
    small = 2 + 4 * (features // mixers)
    held = -(-(row_starts[-1] + part_rows) // 8) * 8
    held = max(held, -(-(2 * patches + small + adapter_rows) // 8) * 8)
    wide = 3 * (-(-rows // 128) * 128)
    share_shape = (groups // columns, columns, mixers // groups, wide)
    return pl.pallas_call(
        functools.partial(token_backward_kernel, codes, resumed, patches, row_starts),
        grid=(count,),
        in_specs=[
            each((patches, features), first), each((rows, 1), first), each((1, features), first), each((rows, features)),
            each((rows, features)), each((rows, 1)), each((mixers, features)), each((mixers, features)),
            whole((2, features)), whole((2, features)), each((adapter_rows, mixers)), whole(hidden_sum.shape), whole(output_sum.shape),
        ]
        + [whole(piece.shape) for piece in tokens]
        + ([whole((2, rows, mixers)), whole((small, mixers)), pl.BlockSpec(memory_space=pl.ANY)] if resumed else []),
        out_specs=[
            pl.BlockSpec((patches, features), lambda i: (0, i + first)), pl.BlockSpec((groups, 1, part_rows, mixers), lambda i: (0, i, 0, 0)),
            whole((small, mixers)), whole((2, rows, mixers)), whole(share_shape),
        ],
        out_shape=[
            struct((patches, images.shape[0] * features)), struct((groups, count, part_rows, mixers), bf16),
            struct((small, mixers)), struct((2, rows, mixers)), struct(share_shape, bf16),
        ],
        scratch_shapes=[
            pltpu.VMEM((held, mixers), f32), pltpu.VMEM((2, mixers, rows), bf16), pltpu.VMEM((rows, features), f32),
        ],
        compiler_params=pltpu.CompilerParams(vmem_limit_bytes=vmem_cap),
        input_output_aliases={len(tokens) + 15: 0} if resumed else {},
        name="token_backward",
    )(
        images, keep, grad_rows, grad, normed, inverse, hidden, slope, norm_gain, norm_bias, adapters, hidden_sum, output_sum,
        *tokens, *(before if resumed else []),
    )


def back_kernel(own, columns, sides, grad_ref, narrow_ref, back_ref, sent_ref, turned_ref):
    turned_ref[...] = grad_ref[...].astype(f32).T
    depth = narrow_ref.shape[0] // columns
    line, side = (lax.axis_index("line"), lax.axis_index("side"))
    total = None
    for code in range(columns):
        start = pl.multiple_of(((line ^ code) * sides + side) * own, own)
        part = dot_tn(turned_ref[pl.ds(start, own)].astype(bf16), narrow_ref[code * depth : code * depth + own])
        total = part if total is None else total + part
    half = total.shape[0] // 2
    back_ref[...] = total[:half]
    sent_ref[...] = total[half:].astype(bf16)


def back_sent(grads, narrow_line, own, columns, sides):
    return pl.pallas_call(
        functools.partial(back_kernel, own, columns, sides),
        out_shape=[
            struct((grads.shape[0] // 2, narrow_line.shape[1])), struct((grads.shape[0] // 2, narrow_line.shape[1]), bf16),
        ],
        scratch_shapes=[pltpu.VMEM((grads.shape[1], grads.shape[0]), f32)],
        compiler_params=pltpu.CompilerParams(vmem_limit_bytes=vmem_cap),
        name="back_sent",
    )(grads, narrow_line)


def narrow_kernel(own, columns, line_ref, side_ref, *refs):
    *chan_refs, grad_ref, grads_ref, chan_ref, product_ref = refs
    depth = line_ref.shape[0] // columns
    held = depth - own
    for line in range(columns):
        for side, ref in enumerate((line_ref, side_ref)):
            at = (2 * line + side) * held
            grads_ref[at : at + held] = ref[line * depth + own : (line + 1) * depth]
    at = 0
    for index, ref in enumerate(chan_refs):
        rows = held if index < 2 else 2 * held
        chan_ref[at : at + rows] = ref[ref.shape[0] - rows :]
        at += rows
    product_ref[...] = dot_tn(grads_ref[...], chan_ref[...])
    grad_ref[...] = product_ref[pl.ds(pl.multiple_of(place_of() * own, own), own)]


def narrow_sums(narrow_line, narrow_side, chan_group, others, own, columns):
    features = narrow_line.shape[1]
    hidden = chan_group.shape[1]
    total = 2 * columns * chan_group.shape[0]
    return pl.pallas_call(
        functools.partial(narrow_kernel, own, columns),
        out_shape=struct((own, hidden)),
        scratch_shapes=[
            pltpu.VMEM((total, features), bf16), pltpu.VMEM((total, hidden), bf16), pltpu.VMEM((features, hidden), f32),
        ],
        compiler_params=pltpu.CompilerParams(vmem_limit_bytes=vmem_cap),
        name="narrow_sums",
    )(narrow_line, narrow_side, chan_group, *others)


def pooled_kernel(own, columns, chan_ref, line_ref, side_ref, own_ref, sent_ref, turned_ref):
    depth = line_ref.shape[0] // columns
    place = place_of()
    for line in range(columns):
        for side, ref in enumerate((line_ref, side_ref)):
            start = pl.multiple_of((place ^ (2 * line + side)) * own, own)
            turned_ref[pl.ds(start, own)] = dot_nt(ref[line * depth : line * depth + own], chan_ref[...])
    total = turned_ref[...].T
    half = total.shape[0] // 2
    own_ref[...] = total[:half]
    sent_ref[...] = total[half:]


def pooled_parts(chan_group, narrow_line, narrow_side, own, columns):
    images = chan_group.shape[0]
    features = 2 * columns * own
    return pl.pallas_call(
        functools.partial(pooled_kernel, own, columns),
        out_shape=[struct((images // 2, features)), struct((images // 2, features))],
        scratch_shapes=[pltpu.VMEM((features, images), f32)],
        compiler_params=pltpu.CompilerParams(vmem_limit_bytes=vmem_cap),
        name="pooled_parts",
    )(chan_group, narrow_line, narrow_side)


def join_kernel(even_ref, other_ref, *part_refs):
    step = pl.program_id(0)
    total = (even_ref[0, 0].astype(f32) + other_ref[0, 0].astype(f32)).astype(bf16)
    for at, part_ref in enumerate(part_refs):

        @pl.when(step == at)
        def _(part_ref=part_ref):
            part_ref[...] = total


def join(even, other):
    blocks, sides, *rest = even.shape
    spec = pl.BlockSpec((1, 1, *rest), lambda i: (i // sides, i % sides, 0, 0, 0))
    return pl.pallas_call(
        join_kernel,
        grid=(blocks * sides,),
        in_specs=[spec, spec],
        out_specs=[whole(tuple(rest)) for _ in range(blocks * sides)],
        out_shape=[struct(tuple(rest), bf16) for _ in range(blocks * sides)],
        compiler_params=pltpu.CompilerParams(vmem_limit_bytes=vmem_cap),
        name="join",
    )(even, other)


def lines_kernel(share_ref, message_ref, chan_ref, own_ref, *message_refs):
    own = share_ref.shape[1]
    held = chan_ref.shape[0]
    for line in range(share_ref.shape[0]):
        total = share_ref[line].astype(f32) + message_ref[line * own : (line + 1) * own].astype(f32)
        if line == 0:
            own_ref[...] = total
            continue
        message_refs[line - 1][:own] = total.astype(bf16)
        message_refs[line - 1][own : own + held] = chan_ref[...]
        message_refs[line - 1][own + held :] = message_ref[-held:]


def lines_out(share, message, chan_group):
    lines, own, wide = share.shape
    depth = own + 2 * chan_group.shape[0]
    return pl.pallas_call(
        lines_kernel,
        out_shape=[struct((own, wide))] + [struct((depth, wide), bf16) for _ in range(lines - 1)],
        compiler_params=pltpu.CompilerParams(vmem_limit_bytes=vmem_cap),
        name="lines_out",
    )(share, message, chan_group)


def spread_kernel(own_ref, line_ref, side_ref, mine_ref, *part_refs):
    for line in range(own_ref.shape[0]):
        total = own_ref[line].astype(f32) + line_ref[line].astype(f32) + side_ref[line].astype(f32)
        if line == 0:
            mine_ref[...] = total
        else:
            part_refs[line - 1][...] = total.astype(bf16)


def spread(own, line_x, own_y):
    lines, *rest = own.shape
    return pl.pallas_call(
        spread_kernel,
        out_shape=[struct(tuple(rest))] + [struct(tuple(rest), bf16) for _ in range(lines - 1)],
        compiler_params=pltpu.CompilerParams(vmem_limit_bytes=vmem_cap),
        name="spread",
    )(own, line_x, own_y)


def images_kernel(side_by_side_ref, image_ref):
    features = image_ref.shape[2]
    for image in range(image_ref.shape[1]):
        image_ref[:, image] = side_by_side_ref[:, image * features : (image + 1) * features]


def images_apart(side_by_side, count):
    patches, wide = side_by_side.shape
    step = 56
    return pl.pallas_call(
        images_kernel,
        grid=(-(-patches // step),),
        in_specs=[pl.BlockSpec((step, wide), lambda i: (i, 0))],
        out_specs=pl.BlockSpec((step, count, wide // count), lambda i: (i, 0, 0)),
        out_shape=struct((patches, count, wide // count)),
        compiler_params=pltpu.CompilerParams(vmem_limit_bytes=vmem_cap),
        name="images_apart",
    )(side_by_side)


def unpack_kernel(patches, own_ref, other_ref, token_ref, mixing_ref, gain_ref, shift_ref, patch_ref, hidden_ref, output_ref):
    half = own_ref.shape[1] // 3
    total = own_ref[...].astype(f32) + other_ref[...].astype(f32)
    for which in range(2):
        token_ref[which] = total[:, which * half : which * half + patches]
    pieces = []
    for row in range(own_ref.shape[0]):
        for at in range(2 * half, 3 * half, 128):
            pieces.append(total[row : row + 1, at : at + 128])
    mixers, features = (mixing_ref.shape[0], gain_ref.shape[1])
    at = 0

    def fill(ref, row, width, held):
        nonlocal at
        for first in range(0, held, 128):
            size = min(128, width - first)
            if size > 0 and len(ref.shape) == 1:
                ref[first : first + size] = pieces[at][0, :size]
            elif size > 0:
                ref[row : row + 1, first : first + size] = pieces[at][:, :size]
            at += 1

    fill(mixing_ref, 0, mixers, mixers)
    for ref in (gain_ref, shift_ref):
        for row in range(2):
            fill(ref, row, features, features)
    fill(patch_ref, 0, patches, mixers)
    fill(hidden_ref, 0, hidden_ref.shape[0], hidden_ref.shape[0])
    fill(output_ref, 0, features, features)


def unpack(own, other, patches, mixers, features, hidden_size):
    return pl.pallas_call(
        functools.partial(unpack_kernel, patches),
        out_shape=[
            struct((2, own.shape[0], patches)), struct((mixers,)), struct((2, features)), struct((2, features)),
            struct((patches,)), struct((hidden_size,)), struct((features,)),
        ],
        name="unpack",
    )(own, other)


def score_kernel(parts, shifted, received_ref, query_hbm, score_ref, query_ref, sems):
    rows, _, width = received_ref.shape
    length = query_hbm.shape[0] // parts
    offset = 0
    if shifted:
        place = place_of()
        offset = pl.multiple_of(lax.rem(place * query_hbm.shape[0], width), 16)
        query_ref[0:width] = jnp.zeros((width, query_ref.shape[1]), bf16)
        last = query_hbm.shape[0] // width * width
        query_ref[last:] = jnp.zeros((rows * width - last, query_ref.shape[1]), bf16)
    copies = [
        pltpu.make_async_copy(
            query_hbm.at[pl.ds(part * length, length)],
            query_ref.at[pl.ds(offset + part * length, length)],
            sems.at[part],
        )
        for part in range(parts)
    ]
    for copy in copies:
        copy.start()
    waited = 0
    total = None
    for row in range(rows):
        while waited < parts and waited * length < (row + 1) * width:
            copies[waited].wait()
            waited += 1
        part = dot(received_ref[row], query_ref[row * width : (row + 1) * width])
        total = part if total is None else total + part
    score_ref[...] = total


def scores(received, queries_t):
    rows, count, width = received.shape
    share, asked = queries_t.shape
    shifted = share != rows * width
    parts = 7 if share % 112 == 0 else 1
    return pl.pallas_call(
        functools.partial(score_kernel, parts, shifted),
        in_specs=[pl.BlockSpec(memory_space=pltpu.VMEM), pl.BlockSpec(memory_space=pl.ANY)],
        out_specs=pl.BlockSpec(memory_space=pltpu.VMEM),
        out_shape=struct((count, asked)),
        scratch_shapes=[pltpu.VMEM((rows * width, asked), bf16), pltpu.SemaphoreType.DMA((parts,))],
        compiler_params=pltpu.CompilerParams(vmem_limit_bytes=vmem_cap),
        name="scores",
    )(received, queries_t)


def score_parts_of(partial_scores, groups, count):
    partial_scores = partial_scores.reshape(groups, count, -1)
    return lax.all_to_all(partial_scores, dp_axes, split_axis=0, concat_axis=0, tiled=True)


def swap(array, axis, code=1):
    devices = lax.axis_size(axis)
    return lax.ppermute(array, axis, [(place, place ^ code) for place in range(devices)])


def swap_both(array, line_code, side_code):
    columns, sides = (lax.axis_size("line"), lax.axis_size("side"))
    pairs = [
        (line * sides + side, (line ^ line_code) * sides + (side ^ side_code))
        for line in range(columns)
        for side in range(sides)
    ]
    return lax.ppermute(array, dp_axes, pairs)


def by_code(parts, place):
    step = 1
    while step < parts.shape[0]:
        pairs = parts.reshape(-1, 2, step, *parts.shape[1:])
        turned = jnp.concatenate([pairs[:, 1:], pairs[:, :1]], axis=1)
        parts = jnp.where((place & step) > 0, turned, pairs).reshape(parts.shape)
        step *= 2
    return parts


def together(*arrays):
    return lax.optimization_barrier(arrays)


def added(left, right):
    return (left.astype(f32) + right.astype(f32)).astype(bf16)


def body(
    images,
    kept_mask,
    pooled_grad,
    token_weights,
    norm_gain,
    norm_bias,
    mixing_bias,
    patch_bias,
    widening,
    narrowing,
    hidden_bias,
    output_bias,
    width_maps,
    hidden_maps,
    queries,
):
    count, patches, features = images.shape
    mixers = mixing_bias.shape[0]
    rank = width_maps.shape[2]
    hidden_size = hidden_bias.shape[0]
    columns = lax.axis_size("line")
    sides = lax.axis_size("side")
    groups = columns * sides
    group = lax.axis_index(dp_axes)
    share, asked = (queries.shape[1], queries.shape[0])
    own_hidden = widening.shape[1]
    own_width = narrowing.shape[1]
    by_hand = groups <= 8 and widening.shape[0] % 16 == 0
    chunks = [(0, count // 2), (count // 2, count)]
    rows = -(-patches // 8) * 8
    extra = rows - patches
    cut = columns // 2

    widen_part = widening.astype(bf16)
    token_part = jnp.pad(jnp.swapaxes(token_weights, 1, 2).astype(bf16), ((0, 0), (0, 0), (0, extra)))
    narrow_part = jnp.swapaxes(narrowing, 0, 1).astype(bf16)
    keep_f = kept_mask.astype(f32)
    kept_count = jnp.sum(keep_f, axis=1, keepdims=True)
    grad_rows = pooled_grad / kept_count
    grad_low = grad_rows.astype(bf16)
    maps_own = jnp.swapaxes(hidden_maps, 1, 2).reshape(2 * rank, own_hidden)
    width_maps = jnp.swapaxes(width_maps, 1, 2)
    keep = jnp.pad(keep_f, ((0, 0), (0, extra)))[:, :, None]
    column = jnp.concatenate([mixing_bias, jnp.pad(patch_bias, (0, extra))])[:, None]
    bias_row = hidden_bias[None, :]
    output_sum = jnp.sum(grad_low.astype(f32) * kept_count, axis=0, keepdims=True)
    if by_hand:
        map_rows = 2 * rank // groups
        maps_part = lax.dynamic_slice_in_dim(maps_own, group * map_rows, map_rows)
        piece = jnp.concatenate([widen_part, maps_part])
        depth = piece.shape[0]
        layout = (depth, widen_part.shape[0], widen_part.shape[0], map_rows)
        token_line = jnp.stack([token_part] + [swap(token_part, "line", code) for code in range(1, columns)])
        grad_pair = jnp.concatenate([grad_low, swap(grad_low, "core")])
        piece, token_line, grad_pair = together(piece, token_line, grad_pair)
        tokens = [token_line, swap(token_line, "side")]
        widen_z = [piece] + [swap(piece, "line", code) for code in range(1, columns)]
        grad_group = jnp.concatenate([grad_pair, swap(grad_pair, "far")])
        grad_near = jnp.concatenate([grad_group, swap(grad_group, "side")])
        line_codes = tuple(sides * code for code in range(columns))
        side_codes = tuple(code ^ 1 for code in line_codes)
        token_codes = (line_codes, side_codes)
        codes = tuple(((side, at), sides * at ^ side) for side in range(sides) for at in range(columns))
        share_shape = (sides, columns, *widening.shape)
    else:
        tokens = [lax.all_gather(token_part, dp_axes, axis=1, tiled=True)[None]]
        token_codes = ((None,),)
        piece = jnp.concatenate([lax.all_gather(widen_part, dp_axes, axis=0, tiled=True), maps_own])
        layout = (piece.shape[0], features, features, 2 * rank)
        piece_x = swap(piece, "far")
        pieces = [piece, swap(piece, "core"), piece_x, swap(piece_x, "core")]
        spans = tuple(((None,), block * own_hidden) for block in range(4))
        codes = (((slice(None),), None),)
        share_shape = (features, own_hidden)

    def forward(chunk):
        out = token_forward(
            images, keep, tokens, token_codes, norm_gain, norm_bias, column, width_maps, *chunks[chunk]
        )
        return list(out)

    forwards = [forward(0)]
    if by_hand:
        narrow_part = jnp.concatenate([narrow_part, grad_near[: 4 * count]])
        forwards[0][:] = together(*forwards[0], *widen_z, narrow_part, grad_near, *tokens)
        widen_z = forwards[0][7 : 7 + columns]
        narrow_part, grad_near, *tokens = forwards[0][7 + columns :]
        forwards[0] = forwards[0][:7]
        widen_line = jnp.concatenate(widen_z)
        widen_y, widen_x = (swap(widen_line, "side"), swap(widen_line, "far"))
        narrow_z = [narrow_part] + [swap(narrow_part, "line", code) for code in range(1, columns)]
        forwards.append(forward(1))
        forwards[1][:] = together(*forwards[1], widen_y, widen_x, *narrow_z)
        widen_y, widen_x, *narrow_z = forwards[1][7:]
        forwards[1] = forwards[1][:7]
        narrow_line = jnp.concatenate(narrow_z)
        half = widen_line.shape[0] // 2
        widen_xy, widen_yx = (swap(widen_y[:half], "far"), swap(widen_x[half:], "side"))
        back_part, back_y = back_sent(grad_near, narrow_line, own_width, columns, sides)
        back_part = added(back_part, swap(back_y, "side"))
        narrow_line, widen_xy, widen_yx = together(narrow_line, widen_xy, widen_yx)
        narrow_y = swap(narrow_line, "side")
        pieces = [widen_line, widen_y, widen_x, widen_xy, widen_yx]
        pieces = pieces + [swap(piece, "core") for piece in pieces]
        near = [(line_codes, 0), (side_codes, 0), (line_codes, 2), (side_codes[:cut], 2), (side_codes[cut:], 2)]
        spans = tuple((codes, block * own_hidden) for codes, block in near) + tuple(
            (codes, (block + 1) * own_hidden) for codes, block in near
        )
    else:
        grad_pair = jnp.concatenate([grad_low, swap(grad_low, "core")])
        grad_group = jnp.concatenate([grad_pair, swap(grad_pair, "far")])
        narrow_t = lax.all_gather(narrow_part, dp_axes, axis=0, tiled=True)
        grad_all = lax.all_gather(grad_group, dp_axes, axis=0, tiled=True)
        grad_all = lax.dynamic_slice_in_dim(grad_all, group * own_width, own_width, 1)
        back_part = dot(grad_group, narrow_t).astype(bf16)
        forwards.append(forward(1))
    back_part = back_part.reshape(4, count, own_hidden)
    back_x = swap(back_part[2:], "far")
    back_core = swap(jnp.stack([back_part[1], back_x[1]]), "core")
    back_rows = jnp.concatenate([back_part[0], back_core[0], back_x[0], back_core[1]], axis=1)

    row_ends = [-(-share * (place + 1) // mixers) for place in range(groups)]
    row_starts = tuple(share * place // mixers for place in range(groups))
    part_rows = -(-max(end - start for start, end in zip(row_starts, row_ends)) // 8) * 8
    queries_t = jnp.swapaxes(queries, 0, 1)
    if share % 16 != 0:
        offset = lax.rem(group * share, mixers)
        queries_t = lax.dynamic_update_slice(
            jnp.zeros((part_rows * mixers, asked), bf16), queries_t, (offset, jnp.int32(0))
        )

    def channel_chunk(chunk, second, left, before):
        first, last = chunks[chunk]
        number = last - first
        return channel(
            second.reshape(number * rows, features), keep, left.reshape(number * rows, rank),
            back_rows, bias_row, grad_low, width_maps, pieces, spans, layout, codes, share_shape, before, mixers,
            chunk, first, last, last == count,
        )

    def backward(chunk, grad, saved, adapters, hidden_sum, before):
        first, last = chunks[chunk]
        hidden, slope, _, normed, inverse = saved[:5]
        image_grad, *parts, sums, token_total, token_share = token_backward(
            images, keep, grad_rows[:, None, :], grad.reshape(last - first, rows, features), normed, inverse, hidden,
            slope, tokens, token_codes, norm_gain, norm_bias, adapters,
            hidden_sum, output_sum, before, row_starts, part_rows, columns,
            first, last,
        )
        return image_grad, parts, sums, token_total, token_share

    second_grad, chan_first, hidden_sum, adapters, shares_first, widen_full, maps_full = channel_chunk(
        0, forwards[0][2], forwards[0][6], None
    )
    if by_hand:
        second_grad, chan_first, hidden_sum, adapters, shares_first, widen_full, maps_full, narrow_y = together(
            second_grad, chan_first, hidden_sum, adapters, shares_first, widen_full, maps_full, narrow_y
        )
    image_grad_first, parts, sums, token_total, _ = backward(
        0, second_grad, forwards[0], adapters, hidden_sum, None
    )
    second, shares_first, *parts = together(forwards[1][2], shares_first, *parts)
    received_first = lax.all_to_all(parts[0], dp_axes, split_axis=0, concat_axis=0, tiled=True)


    second_grad, chan_second, hidden_sum, adapters, *shares = channel_chunk(
        1, second, forwards[1][6], (widen_full, maps_full, hidden_sum, shares_first)
    )
    second_grad, chan_second, hidden_sum, adapters, *shares, received_first = together(
        second_grad, chan_second, hidden_sum, adapters, *shares, received_first
    )
    share_core = swap(shares[1], "core")
    chan_pooled = jnp.concatenate([chan_first, chan_second]).astype(bf16).reshape(count, 4, own_hidden)
    chan_x = swap(chan_pooled[:, 2:], "far")
    image_grad, parts, sums, _, token_share = backward(
        1, second_grad, forwards[1], adapters, hidden_sum, (token_total, sums, image_grad_first)
    )
    image_grad, parts[0], sums, token_share, chan_x, share_core = together(
        image_grad, parts[0], sums, token_share, chan_x, share_core
    )
    received_second = lax.all_to_all(parts[0], dp_axes, split_axis=0, concat_axis=0, tiled=True)
    chan_core = swap(jnp.stack([chan_pooled[:, 1], chan_x[:, 1]]), "core")
    chan_group = jnp.concatenate([chan_pooled[:, 0], chan_core[0], chan_x[:, 0], chan_core[1]])

    own_mixers, wide = token_share.shape[2:]
    lines = features // mixers
    if by_hand:
        own_line, own_side, far_line, far_side = join(shares[0], share_core)
        message = jnp.concatenate([token_share[1].reshape(-1, wide), chan_group])
        own_line, own_side, far_line, far_side, message = together(own_line, own_side, far_line, far_side, message)
        far_x = swap(far_side, "far")
        message = swap(message, "side")
        image_grad = images_apart(image_grad, count)
        out_own, out_sent = pooled_parts(chan_group, narrow_line, narrow_y, own_width, columns)
        far_x, far_line, image_grad, message, out_own, out_sent = together(
            far_x, far_line, image_grad, message, out_own, out_sent
        )
        own_y = swap(added(own_side, far_x), "side")
        line_x = swap(far_line, "far")
        token_total, *messages = lines_out(token_share[0], message, chan_group)
        received_second, *messages = together(received_second, *messages)
        messages = [swap(part, "line", code) for code, part in enumerate(messages, 1)]
        arrived = jnp.concatenate([received_first, received_second], axis=1)
        arrived = jnp.moveaxis(arrived, 2, 0).reshape(part_rows, groups * count, mixers)
        own_y, line_x, arrived = together(own_y, line_x, arrived)
        widening_grad, *widen_sums = spread(own_line, line_x, own_y)
        arrived, *widen_sums = together(arrived, *widen_sums)
        widen_sums = [swap(part, "line", code) for code, part in enumerate(widen_sums, 1)]
        partial_scores = scores(arrived, queries_t)
        _, out_sent, *messages = together(partial_scores, out_sent, *messages)
        image_grad = jnp.swapaxes(image_grad, 0, 1)
        total = token_total
        for part in messages:
            total = total + part[:own_mixers].astype(f32)
        total = total.astype(bf16)
        total_x = swap(total, "far")
        out_x = swap(out_sent, "far")
        narrowing_grad = narrow_sums(
            narrow_line, narrow_y, chan_group, [message, *messages], own_width, columns
        ).T
        total_x, out_x, narrowing_grad, *widen_sums = together(total_x, out_x, narrowing_grad, *widen_sums)
        total = added(total, total_x)
        token_grad, mixing_grad, gain_grad, shift_grad, patch_grad, hidden_grad, output_grad = unpack(
            total, swap(total, "core"), patches, mixers, features, hidden_size
        )
        score_parts = score_parts_of(partial_scores, groups, count)
        for widen_sum in widen_sums:
            widening_grad = widening_grad + widen_sum.astype(f32)
    else:
        narrowing_grad = None
        image_grad = jnp.swapaxes(image_grad.reshape(patches, count, features), 0, 1)
        arrived = jnp.concatenate([received_first, received_second], axis=1)
        arrived = jnp.moveaxis(arrived, 2, 0).reshape(part_rows, groups * count, mixers)
        score_parts = score_parts_of(scores(arrived, queries_t), groups, count)
        both = added(shares[0], share_core)
        own, far = (both[0], both[1])
        own = added(own, jnp.concatenate([swap(far[:1], "far"), swap(far[1:], "far")]))
        widening_grad = lax.psum_scatter(own, dp_axes, scatter_dimension=0, tiled=True).astype(f32)
        chan_all = lax.all_gather(chan_group, dp_axes, axis=0, tiled=True)
        summed = jnp.swapaxes(token_share, 0, 1).reshape(groups, own_mixers, wide)
        summed = by_code(summed, group).astype(f32)
        total = lax.psum(lax.psum_scatter(summed, dp_axes, scatter_dimension=0, tiled=True)[0], ("far", "core"))
        half = wide // 3
        sums, more = lax.psum((sums, jnp.concatenate([hidden_sum, output_sum], axis=1)[0]), dp_axes + ("far", "core"))
        token_grad = jnp.stack([total[:, :patches], total[:, half : half + patches]])
        mixing_grad = sums[0]
        gain_grad = sums[1 : 1 + 2 * lines].reshape(2, features)
        shift_grad = sums[1 + 2 * lines : 1 + 4 * lines].reshape(2, features)
        patch_grad = sums[1 + 4 * lines, :patches]
        hidden_grad, output_grad = (more[:hidden_size], more[hidden_size : hidden_size + features])
    token_grad = jnp.swapaxes(token_grad, 1, 2)
    if narrowing_grad is None:
        narrowing_grad = dot_tn(grad_all, chan_all).T

    if not by_hand:
        out_part = dot_nt(chan_group, narrow_t)
        out_own, out_x = (out_part[: 2 * count], swap(out_part[2 * count :], "far"))
    out_pair = out_own + out_x
    chan_out = out_pair[:count] + swap(out_pair[count:], "core")
    score_parts, token_grad, narrowing_grad, chan_out = together(score_parts, token_grad, narrowing_grad, chan_out)
    influence = jnp.sum(score_parts, axis=0)
    pooled_in = jnp.concatenate([forwards[0][5][:, 0], forwards[1][5][:, 0]])
    pooled = (pooled_in + chan_out) / kept_count + output_bias

    return (
        pooled,
        image_grad,
        token_grad,
        gain_grad,
        shift_grad,
        mixing_grad,
        patch_grad,
        widening_grad,
        narrowing_grad,
        hidden_grad,
        output_grad,
        influence,
    )


def solution(mesh):
    groups = mesh.shape["dp"]
    models = mesh.shape["mp"]
    mesh = Mesh(mesh.devices.reshape(groups // 2, 2, models // 2, 2), ("line", "side", "far", "core"))
    dp = ("line", "side")
    mp = ("far", "core")
    every = dp + mp
    placed = (
        P(every, None, None),
        P(every, None),
        P(every, None),
        P(None, None, dp),
        P(),
        P(),
        P(),
        P(),
        P(dp, mp),
        P(mp, dp),
        P(),
        P(),
        P(),
        P(None, mp, None),
        P(None, dp),
    )
    return jax.shard_map(
        body,
        mesh=mesh,
        in_specs=placed,
        out_specs=(
            P(every, None),
            P(every, None, None),
            P(None, None, dp),
            P(),
            P(),
            P(),
            P(),
            P(dp, mp),
            P(mp, dp),
            P(),
            P(),
            P(every, None),
        ),
        check_vma=False,
    )
```
